128 devices in a mesh: ctx: 16 (over y, x), rep: 8 (over z, core).
Axes of the slice: x: 4, y: 4, z: 4, core: 2. Of those that a mesh axis runs over, the one named last changes fastest.
Arguments:
- queries: bfloat16 [8, 2048, 4096], P('rep', 'ctx'), may hold values from -45 to 45
- cache_keys: bfloat16 [8, 2048, 1024], P('rep', 'ctx'), may hold values from -16 to 16
- cache_values: bfloat16 [8, 2048, 1024], P('rep', 'ctx'), may hold values from -6 to 6
- ssm_input: bfloat16 [8, 2048, 8192], P('rep', 'ctx'), may hold values from -6 to 6
- input_map: bfloat16 [8, 2048, 1024], P('rep', 'ctx'), may hold values from -0.03125 to 0.03125
- output_map: bfloat16 [8, 2048, 1024], P('rep', 'ctx'), may hold values from -6 to 6
- log_decay: float32 [8, 2048, 128], P('rep', 'ctx'), may hold values from -1.5 to 0
- skip_gain: float32 [128], replicated, may hold values from 0.25 to 1.75
- lengths: int32 [8], P('rep'), may hold values from 512 to 2048, as said below
- page_owner: int32 [8, 128, 1], P('rep', 'ctx'), may hold values from 0 to 7; in each aligned block of 8 rows (0 to 7, 8 to 15, ..., all dimensions but the last counted through in order) at most 4 rows name the same one
Outputs:
- attn_out: bfloat16 [8, 2048, 4096], P('rep', 'ctx')
- ssm_out: bfloat16 [8, 2048, 8192], P('rep', 'ctx')
- state_pool: bfloat16 [16, 8, 128, 64, 256], P('ctx', None, 'rep')
- page_pool: bfloat16 [16, 8, 8, 4, 2, 16, 1024], P('ctx', 'rep')
- page_ids: int32 [16, 8, 8, 4], P('ctx', 'rep')
The draws below stay inside these ranges and needn't reach their ends.
Inputs may be any that keep to these rules, and one draw needn't show every extreme that they name: `lengths`: every length is a multiple of 128; some prompt has length 2048. `page_owner`: among the 8 pages of one device, at most 4 name the same owner; on some devices exactly 4 do.
All inputs are finite; a program needn't handle non-finite values.
Results may differ from the reference program's by a relative error of at most 0.013.
Values may be sent and summed in bfloat16 or wider, within the bound.
A program may use at most 384 MiB of HBM per device.

```python
import math
import jax
import jax.numpy as jnp
import numpy as np
from jax import lax

QH = 32
KVH = 8
HD = 128
MH = 128
MP = 64
NS = 256
GR = 4
TOK_DEV = 128
PAGE = 16
CAP = 4
LEN_UNIT = 128
SEQ = 2048
PROMPTS = 8
N_CTX = 16
N_REP = 8


def shared_rows(key):
    return jnp.clip(jax.random.normal(key, (PROMPTS, SEQ, KVH * HD), jnp.float32), -4.0, 4.0)


def draw_cache_keys(key, part):
    base_rows = shared_rows(key)
    return base_rows.astype(jnp.bfloat16)


def draw_queries(key, part):
    key = jax.random.fold_in(key, 22)
    first_key = jax.random.fold_in(key, 0)
    drawn = jnp.clip(jax.random.normal(first_key, (PROMPTS, SEQ, QH * HD), jnp.float32), -4.0, 4.0)
    return drawn.astype(jnp.bfloat16)


def draw_log_decay(key, part):
    key = jax.random.fold_in(key, 23)
    subkeys = jax.random.split(key, 7)
    fast_share = 0.5
    blocks = SEQ // TOK_DEV
    fast_class = jax.random.uniform(subkeys[0], (PROMPTS, 1, MH), jnp.float32) < fast_share
    fast_block = jax.random.uniform(subkeys[6], (PROMPTS, blocks, MH), jnp.float32) < 0.5
    fast_head = jnp.repeat(fast_class & fast_block, TOK_DEV, axis=1)
    fast_rate = jnp.exp(jax.random.uniform(subkeys[1], (PROMPTS, blocks, MH), jnp.float32, math.log(1.0 / 50.0), math.log(1.0 / 30.0)))
    fast_rate = jnp.repeat(fast_rate, TOK_DEV, axis=1)
    slow_rate = jnp.exp(jax.random.uniform(subkeys[2], (PROMPTS, 1, MH), jnp.float32, math.log(0.1), math.log(0.6))) / SEQ
    scale_multiplier = jax.random.uniform(subkeys[3], (PROMPTS, blocks, MH), jnp.float32, 1.0, 2.5)
    scale_multiplier = jnp.repeat(scale_multiplier, TOK_DEV, axis=1)
    decay_speeds = jnp.where(fast_head, fast_rate, slow_rate * scale_multiplier)
    spots = jax.random.randint(subkeys[4], (PROMPTS, 3), 0, SEQ)
    dropped_entries = jax.random.uniform(subkeys[5], (PROMPTS, 3, MH), jnp.float32, math.log(0.5), math.log(0.8))
    positions = jnp.arange(SEQ)
    cache_matches = (positions[None, :, None] == spots[:, None, :]).astype(jnp.float32)
    arrival_groups = jnp.sum(cache_matches[..., None] * dropped_entries[:, None, :, :], axis=2)
    return -decay_speeds + arrival_groups


def draw_lengths(key, part):
    key = jax.random.fold_in(key, 24)
    first_key, second_key = jax.random.split(key)
    top_units = SEQ // LEN_UNIT
    low_units = max(1, top_units // 4)
    units = jax.random.randint(first_key, (PROMPTS,), low_units, top_units + 1)
    chosen = jax.random.randint(second_key, (), 0, PROMPTS)
    units = jnp.where(jnp.arange(PROMPTS) == chosen, top_units, units)
    return (units * LEN_UNIT).astype(jnp.int32)


def steps_of(stream_key, dims, pieces, low, high):
    level = 1.0
    for dim, shards_of in pieces:
        steps = jax.random.uniform(jax.random.fold_in(jax.random.fold_in(stream_key, 6), dim), (shards_of,), jnp.float32, low / len(pieces), high / len(pieces))
        level = level * jnp.repeat(jnp.exp(steps), dims[dim] // shards_of).reshape((-1,) + (1,) * (len(dims) - 1 - dim))
    return level


def deal_out(rng, own, number, rows, count, top, limit, slope):
    order = jax.random.permutation(rng, count)
    heavy_load, ordinary = shares(count, rows * top, limit, slope, True), shares(count, rows * top, limit, slope, False)
    places = jnp.arange(count)

    def named(tallies, turn):
        used = int((tallies > 0).sum())
        fixed = max(1, used // 4)
        moved = fixed + (places - fixed + turn * (used - fixed)) % max(1, count - fixed)
        return jnp.zeros((count,), jnp.int32).at[order[jnp.where(places < fixed, places, moved)]].set(jnp.asarray(tallies, jnp.int32))

    tallies = jnp.where(number % 4 == 0, named(heavy_load, number // 4), named(ordinary, number - number // 4 - 1))
    mixed = jax.random.permutation(jax.random.fold_in(own, 3), count)
    source_of, sink = mixed[0:count // 2 * 2:2], mixed[1:count // 2 * 2:2]
    slack = jnp.minimum(tallies[source_of] - 1, limit - tallies[sink]) // 2
    slack = jnp.where((source_of == order[0]) | (sink == order[0]) | (tallies[sink] == 0), 0, jnp.maximum(slack, 0))
    moved = jax.random.randint(jax.random.fold_in(own, 4), (count // 2,), 0, 1 << 20) % (slack + 1)
    tallies = tallies.at[source_of].add(-moved).at[sink].add(moved)
    items = jnp.searchsorted(jnp.cumsum(tallies), jnp.arange(rows * top), side="right").astype(jnp.int32)
    grid = items.reshape(top, rows).T
    grid = grid[jax.random.permutation(jax.random.fold_in(own, 1), rows)]
    turn = jax.random.randint(jax.random.fold_in(own, 2), (rows, 1), 0, top)
    return jnp.take_along_axis(grid, (jnp.arange(top)[None, :] + turn) % top, axis=1)


def shares(count, total, bound, lean, full):
    portions = [(1 << 20) // math.isqrt(rank ** lean) + 1 for rank in range(1, count + 1)]
    largest = bound if full else min(bound, max(-(-total // count), total * portions[0] // sum(portions)))
    least = 1 if total - largest >= count - 1 else 0
    counts, surplus = [largest] + [least] * (count - 1), total - largest - least * (count - 1)
    while surplus > 0:
        movable = [i for i in range(1, count) if counts[i] < largest] or [i for i in range(1, count) if counts[i] < bound]
        pool, budget = sum([portions[i] for i in movable]), surplus
        for i in movable:
            more = min(bound - counts[i], max(1, budget * portions[i] // pool), surplus)
            counts[i] = counts[i] + more
            surplus = surplus - more
    return np.array(counts)


def normal_values(own_key, shape, scale, bound, cuts=(), kind=jnp.bfloat16):
    values = jax.random.normal(own_key, shape, jnp.float32) * scale
    if len(cuts) > 0:
        values = steps_of(own_key, shape, cuts, -0.22, 0.18) * values
    return jnp.clip(values, min=-bound, max=bound).astype(kind)


def setup_inputs(seed: int = 0) -> dict:
    splits = jax.random.split(jax.random.key(seed), 11)
    queries = draw_queries(jax.random.fold_in(splits[10], 71), 0)
    cache_keys = draw_cache_keys(jax.random.fold_in(splits[10], 71), 0)
    cache_values = normal_values(splits[2], (PROMPTS, SEQ, KVH * HD), 1.0, 6.0, ((0, 8), (1, 16)))
    ssm_input = normal_values(splits[3], (PROMPTS, SEQ, MH * MP), 1.0, 6.0, ((0, 8), (1, 16)))
    input_map = normal_values(splits[4], (PROMPTS, SEQ, GR * NS), (NS * TOK_DEV) ** -0.5, 0.03125, ((0, 8), (1, 16)))
    output_map = normal_values(splits[5], (PROMPTS, SEQ, GR * NS), 1.0, 6.0, ((0, 8), (1, 16)))
    log_decay = draw_log_decay(jax.random.fold_in(splits[10], 71), 0)
    skip_gain = jnp.clip(1.0 + 0.15 * jax.random.normal(splits[7], (MH,), jnp.float32), 0.25, 1.75)
    lengths = draw_lengths(jax.random.fold_in(splits[10], 71), 0)
    page_owner_keys = jax.random.split(jax.random.fold_in(splits[9], 1), PROMPTS * (SEQ // PAGE) // (TOK_DEV // PAGE))
    page_owner_turns = jax.random.permutation(jax.random.fold_in(splits[9], 3), PROMPTS * (SEQ // PAGE) // (TOK_DEV // PAGE))
    page_owner = jax.vmap(lambda own, number: deal_out(jax.random.fold_in(splits[9], 2), own, number, TOK_DEV // PAGE, N_REP, 1, CAP, 1))(page_owner_keys, page_owner_turns).reshape((PROMPTS, SEQ // PAGE, 1))
    return {"queries": queries, "cache_keys": cache_keys, "cache_values": cache_values, "ssm_input": ssm_input, "input_map": input_map, "output_map": output_map, "log_decay": log_decay, "skip_gain": skip_gain, "lengths": lengths, "page_owner": page_owner}


def attention_prompt(queries, cache_keys, cache_values, length):
    groups = QH // KVH
    scaling = 1.0 / (HD ** 0.5)
    query_full = queries.astype(jnp.float32).reshape(SEQ, KVH, groups, HD)
    key_full = cache_keys.astype(jnp.float32).reshape(SEQ, KVH, HD)
    value_full = cache_values.astype(jnp.float32).reshape(SEQ, KVH, HD)
    block_rows = 512 if SEQ % 512 == 0 else SEQ
    outputs = []
    for block_index in range(SEQ // block_rows):
        row_start = block_index * block_rows
        row_end = row_start + block_rows
        scores = jnp.einsum("qkgd,tkd->kgqt", query_full[row_start:row_end], key_full[:row_end]) * scaling
        query_pos = jnp.arange(row_start, row_end, dtype=jnp.int32)
        key_pos = jnp.arange(row_end, dtype=jnp.int32)
        allowed = (key_pos[None, :] <= query_pos[:, None]) & (key_pos[None, :] < length)
        row_max = jnp.max(jnp.where(allowed, scores, -jnp.inf), axis=-1, keepdims=True)
        weights = jnp.where(allowed, jnp.exp(scores - row_max), 0.0)
        totals = jnp.sum(weights, axis=-1)
        rounded = lax.optimization_barrier(weights.astype(jnp.bfloat16)).astype(jnp.float32)
        blended = jnp.einsum("kgqt,tkd->qkgd", rounded, value_full[:row_end])
        blended = blended / jnp.transpose(totals, (2, 0, 1))[..., None]
        outputs.append(blended.reshape(block_rows, QH * HD))
    return jnp.concatenate(outputs, axis=0).astype(jnp.bfloat16)


def ssm_block(entering, inputs_block, in_map, out_map, decay_block, skip_gain):
    block_rows = inputs_block.shape[0]
    head_group = MH // GR
    cumulative = jnp.cumsum(decay_block, axis=0)
    inputs_f = inputs_block.astype(jnp.float32)
    in_f = in_map.astype(jnp.float32)
    out_f = out_map.astype(jnp.float32)
    products = jnp.einsum("tgn,sgn->gts", out_f, in_f)
    spans_log = cumulative[:, None, :] - cumulative[None, :, :]
    order_index = jnp.arange(block_rows, dtype=jnp.int32)
    causal = (order_index[None, :] <= order_index[:, None])[:, :, None]
    fading = jnp.where(causal, jnp.exp(jnp.where(causal, spans_log, 0.0)), 0.0)
    fading = fading.reshape(block_rows, block_rows, GR, head_group)
    mixing = jnp.transpose(products, (1, 2, 0))[:, :, :, None] * fading
    mixing = lax.optimization_barrier(mixing.astype(jnp.bfloat16)).astype(jnp.float32)
    inner_part = jnp.einsum("tsgh,sghp->tghp", mixing, inputs_f)
    to_end = jnp.exp(cumulative[-1][None, :] - cumulative).reshape(block_rows, GR, head_group)
    faded_input = lax.optimization_barrier((inputs_f * to_end[..., None]).astype(jnp.bfloat16)).astype(jnp.float32)
    block_state = jnp.einsum("sghp,sgn->ghpn", faded_input, in_f).reshape(MH, MP, NS)
    entering_bf = lax.optimization_barrier(entering.astype(jnp.bfloat16)).astype(jnp.float32)
    carried = jnp.einsum("tgn,ghpn->tghp", out_f, entering_bf.reshape(GR, head_group, MP, NS), precision=lax.Precision.HIGHEST)
    outer_part = jnp.exp(cumulative).reshape(block_rows, GR, head_group)[..., None] * carried
    skipped = skip_gain.reshape(GR, head_group)[None, :, :, None] * inputs_f
    outputs = (inner_part + outer_part + skipped).reshape(block_rows, MH * MP).astype(jnp.bfloat16)
    leaving = jnp.exp(cumulative[-1])[:, None, None] * entering + block_state
    return leaving, (outputs, leaving.astype(jnp.bfloat16))


def ssm_prompt(ssm_input, input_map, output_map, log_decay, skip_gain, length):
    blocks = SEQ // TOK_DEV
    head_group = MH // GR
    positions = jnp.arange(SEQ, dtype=jnp.int32)
    active = (positions < length)[:, None]
    decays = jnp.where(active, log_decay, jnp.zeros_like(log_decay))
    inputs = jnp.where(active, ssm_input, jnp.zeros_like(ssm_input))
    inputs_blocks = inputs.reshape(blocks, TOK_DEV, GR, head_group, MP)
    in_blocks = input_map.reshape(blocks, TOK_DEV, GR, NS)
    out_blocks = output_map.reshape(blocks, TOK_DEV, GR, NS)
    decay_blocks = decays.reshape(blocks, TOK_DEV, MH)

    def advance(entering, block_data):
        return ssm_block(entering, block_data[0], block_data[1], block_data[2], block_data[3], skip_gain)

    start_state = jnp.zeros((MH, MP, NS), jnp.float32)
    _, (outputs, snapshots) = lax.scan(advance, start_state, (inputs_blocks, in_blocks, out_blocks, decay_blocks))
    return outputs.reshape(SEQ, MH * MP), snapshots


def page_table(cache_keys, cache_values, page_owner, lengths):
    dev_pages = TOK_DEV // PAGE
    kv_width = KVH * HD
    stacked = jnp.stack([cache_keys.reshape(PROMPTS, N_CTX, dev_pages, PAGE, kv_width),
                         cache_values.reshape(PROMPTS, N_CTX, dev_pages, PAGE, kv_width)], axis=3)
    page_number = jnp.arange(N_CTX * dev_pages, dtype=jnp.int32).reshape(N_CTX, dev_pages)
    alive_page = page_number[None] * PAGE < lengths[:, None, None]
    stacked = jnp.where(alive_page[..., None, None, None], stacked, jnp.zeros_like(stacked))
    owners = page_owner[..., 0].reshape(PROMPTS, N_CTX, dev_pages)
    owner_onehot_mask = (owners[..., None] == jnp.arange(N_REP, dtype=jnp.int32)).astype(jnp.int32)
    ranking = jnp.cumsum(owner_onehot_mask, axis=2) - owner_onehot_mask
    slot_index = jnp.sum(ranking * owner_onehot_mask, axis=-1)
    selector = owner_onehot_mask[..., None] * (slot_index[..., None, None] == jnp.arange(CAP, dtype=jnp.int32)).astype(jnp.int32)
    flat = stacked.reshape(PROMPTS, N_CTX, dev_pages, 2 * PAGE * kv_width).astype(jnp.float32)
    pooled = jnp.einsum("gcpoq,gcpx->cogqx", selector.astype(jnp.float32), flat)
    page_pool = pooled.reshape(N_CTX, N_REP, PROMPTS, CAP, 2, PAGE, kv_width).astype(jnp.bfloat16)
    labels = jnp.where(alive_page, page_number[None], -1) + 1
    page_ids = jnp.sum(selector * labels[..., None, None], axis=2) - 1
    page_ids = jnp.transpose(page_ids, (1, 2, 0, 3)).astype(jnp.int32)
    return page_pool, page_ids


def reference(queries, cache_keys, cache_values, ssm_input, input_map, output_map, log_decay, skip_gain, lengths, page_owner):
    def single_attention_prompt(items):
        return attention_prompt(items[0], items[1], items[2], items[3])

    def ssm_one(items):
        return ssm_prompt(items[0], items[1], items[2], items[3], skip_gain, items[4])

    attn_out = lax.map(single_attention_prompt, (queries, cache_keys, cache_values, lengths))
    ssm_out, snapshots = lax.map(ssm_one, (ssm_input, input_map, output_map, log_decay, lengths))
    state_pool = jnp.transpose(snapshots, (1, 0, 2, 3, 4))
    page_pool, page_ids = page_table(cache_keys, cache_values, page_owner, lengths)
    return attn_out, ssm_out, state_pool, page_pool, page_ids
```

```python
import functools
import math

import jax
import jax.numpy as jnp
from jax import lax
from jax.experimental import pallas as pl
from jax.experimental.pallas import tpu as pltpu
from jax.sharding import PartitionSpec as P

HD = 128
GR = 4
PAGE = 16
CAP = 4
MP = 64
NS = 256
ROWS = 128
HG = 32
GW = HG * MP
PIECE = 8 * MP
MESH = pl.DeviceIdType.MESH
F32 = jnp.float32
BF16 = jnp.bfloat16


def mod4(v):
    return lax.rem(v + 8, 4)


def ssm_kernel(
    x_ref, b_ref, c_ref, ef_ref, cumt_ref, cumg_ref, ecum_ref, wg_ref, live_ref, skip_ref,
    out_ref, pool_ref,
    ft, ft_in, b_in, w_in, part, wprod, t_out, t_in, w4_in, e0_out, e0_in, e_out, e_in,
    inner, snap,
    s_ft, r_ft, s_b, r_b, s_w, r_w, s_t, r_t, s_w4, r_w4, s_e0, r_e0, s_e, r_e, s_p, r_p, l_p,
):
    ctx = lax.axis_index("ctx")
    rep = lax.axis_index("rep")
    mx = lax.rem(ctx, 4)
    my = ctx // 4
    mz = rep // 2

    def row_peer(j):
        return (my * 4 + j, rep)

    def col_peer(j):
        return (j * 4 + mx, rep)

    barrier = pltpu.get_barrier_semaphore()
    for i in range(1, 4):
        pl.semaphore_signal(barrier, inc=1, device_id=row_peer(mod4(mx + i)), device_id_type=MESH)
        pl.semaphore_signal(barrier, inc=1, device_id=col_peer(mod4(my + i)), device_id_type=MESH)
    for i in range(1, 8):
        pl.semaphore_signal(
            barrier, inc=1, device_id=(ctx, lax.rem(rep + i, 8)), device_id_type=MESH
        )
    pl.semaphore_wait(barrier, 13)

    def remote(src, dst, send, recv, device):
        return pltpu.make_async_remote_copy(
            src_ref=src, dst_ref=dst, send_sem=send, recv_sem=recv, device_id=device,
            device_id_type=MESH,
        )

    def rows_of(piece):
        return pl.ds(pl.multiple_of(piece * PIECE, PIECE), PIECE)

    def fade(j):
        def pair(p, carry):
            lanes = pl.ds(pl.multiple_of(j * GW + p * 128, 128), 128)
            turned = jnp.transpose(x_ref[:, lanes].astype(F32))
            factor = jnp.broadcast_to(
                ef_ref[j, pl.ds(2 * p, 2), :][:, None, :], (2, MP, ROWS)
            ).reshape(128, ROWS)
            ft[j, pl.ds(pl.multiple_of(p * 128, 128), 128), :] = (turned * factor).astype(BF16)
            return carry

        lax.fori_loop(0, HG // 2, pair, 0, unroll=4)

    sent = []
    for i in (1, 3, 2):
        j = mod4(mx + i)
        fade(j)
        lanes = pl.ds(pl.multiple_of(j * NS, NS), NS)
        for c in (
            remote(ft.at[j], ft_in.at[mx], s_ft.at[i], r_ft.at[mx], row_peer(j)),
            remote(b_ref.at[:, lanes], b_in.at[mx], s_b.at[i], r_b.at[mx], row_peer(j)),
            remote(wg_ref.at[j], w_in.at[mx], s_w.at[i], r_w.at[mx], row_peer(j)),
        ):
            c.start()
            sent.append(c)
    fade(mx)
    ft_in[mx] = ft[mx]
    b_in[mx] = b_ref[:, pl.ds(pl.multiple_of(mx * NS, NS), NS)]
    w_in[mx] = wg_ref[mx]

    live = live_ref[0:1, :]
    lane = lax.broadcasted_iota(jnp.int32, (ROWS, 128), 1)
    line = lax.broadcasted_iota(jnp.int32, (ROWS, 128), 0)
    causal = lane <= line
    low = lane < MP

    def inner_group(g, carry):
        lanes = pl.ds(pl.multiple_of(g * NS, NS), NS)
        products = lax.dot_general(
            c_ref[:, lanes], b_ref[:, lanes], (((1,), (1,)), ((), ())),
            preferred_element_type=F32,
        )
        products = jnp.where(causal, products * live, 0.0)
        for p in range(HG // 2):
            at = pl.ds(pl.multiple_of(g * GW + p * 128, 128), 128)
            values = x_ref[:, at]
            halves = []
            for k in range(2):
                h = 2 * p + k
                column = cumg_ref[g, :, h : h + 1]
                row = cumt_ref[g, h : h + 1, :]
                mix = (products * jnp.exp(jnp.minimum(column - row, 0.0))).astype(BF16)
                halves.append(jnp.dot(mix, values, preferred_element_type=F32))
            inner[:, at] = jnp.where(low, halves[0], halves[1]) + skip_ref[0:1, at] * (
                values.astype(F32) * live
            )
        return carry

    lax.fori_loop(0, GR, inner_group, 0)

    for i in (1, 3, 2):
        j = mod4(mx + i)
        remote(ft.at[j], ft_in.at[j], s_ft.at[i], r_ft.at[j], row_peer(j)).wait_recv()
        remote(b_in.at[j], b_in.at[j], s_b.at[i], r_b.at[j], row_peer(j)).wait_recv()
        remote(wg_ref.at[j], w_in.at[j], s_w.at[i], r_w.at[j], row_peer(j)).wait_recv()

    running = w_in[0]
    for k in range(1, 4):
        wprod[k - 1] = running
        running = running * w_in[k]
    wprod[3] = running

    def widen(rows, heads):
        both = jnp.concatenate([rows, rows], axis=1)
        return jnp.broadcast_to(both[:, None, :], (heads, MP, NS)).reshape(heads * MP, NS)

    def scan_piece(piece):
        def chunk(c, carry):
            first = piece * 8 + c * 4
            at = pl.ds(pl.multiple_of(first * MP, 256), 256)
            state = jnp.dot(ft_in[0, at, :], b_in[0], preferred_element_type=F32)
            for k in range(1, 4):
                part[k - 1, at, :] = state
                state = state * widen(w_in[k, pl.ds(first, 4), :], 4) + jnp.dot(
                    ft_in[k, at, :], b_in[k], preferred_element_type=F32
                )
            t_out[at, :] = state.astype(BF16)
            return carry

        lax.fori_loop(0, 2, chunk, 0)

    for i in (1, 3, 2):
        j = mod4(my + i)
        scan_piece(j)
        heads = pl.ds(pl.multiple_of(j * 8, 8), 8)
        for c in (
            remote(t_out.at[rows_of(j), :], t_in.at[my], s_t.at[i], r_t.at[my], col_peer(j)),
            remote(wprod.at[3, heads, :], w4_in.at[my], s_w4.at[i], r_w4.at[my], col_peer(j)),
        ):
            c.start()
            sent.append(c)
    scan_piece(my)
    t_in[my] = t_out[rows_of(my), :]
    w4_in[my] = wprod[3, pl.ds(pl.multiple_of(my * 8, 8), 8), :]
    for i in (1, 3, 2):
        j = mod4(my + i)
        remote(t_in.at[j], t_in.at[j], s_t.at[i], r_t.at[j], col_peer(j)).wait_recv()
        remote(w4_in.at[j], w4_in.at[j], s_w4.at[i], r_w4.at[j], col_peer(j)).wait_recv()

    def starts(c, carry):
        first = c * 4
        at = pl.ds(pl.multiple_of(first * MP, 256), 256)
        state = jnp.zeros((256, NS), F32)
        for k in range(4):
            e0_out[k, at, :] = state.astype(BF16)
            if k < 3:
                state = state * widen(w4_in[k, pl.ds(first, 4), :], 4) + t_in[k, at, :].astype(F32)
        return carry

    lax.fori_loop(0, 2, starts, 0)
    for i in (1, 3, 2):
        j = mod4(my + i)
        c = remote(e0_out.at[j], e0_in.at[my], s_e0.at[i], r_e0.at[my], col_peer(j))
        c.start()
        sent.append(c)
    e0_in[my] = e0_out[my]

    for t, d in enumerate((0, 1, 3, 2)):
        piece = mod4(my + d)
        if d != 0:
            remote(
                e0_in.at[piece], e0_in.at[piece], s_e0.at[d], r_e0.at[piece], col_peer(piece)
            ).wait_recv()

        def enter(c, carry):
            first = piece * 8 + c * 4
            at = pl.ds(pl.multiple_of(first * MP, 256), 256)
            low_start = e0_in[piece, pl.ds(pl.multiple_of(c * 256, 256), 256), :]
            start = low_start.astype(F32)
            e_out[0, at, :] = low_start
            for k in range(1, 4):
                e_out[k, at, :] = (
                    start * widen(wprod[k - 1, pl.ds(first, 4), :], 4) + part[k - 1, at, :]
                ).astype(BF16)
            return carry

        lax.fori_loop(0, 2, enter, 0)
        at = rows_of(piece)
        for i in (1, 3, 2):
            j = mod4(mx + i)
            c = remote(
                e_out.at[j, at, :], e_in.at[mx, at, :], s_e.at[i, d], r_e.at[mx, d], row_peer(j)
            )
            c.start()
            sent.append(c)
        e_in[mx, at, :] = e_out[mx, at, :]

    for d in (0, 1, 3, 2):
        piece = mod4(my + d)
        at = rows_of(piece)
        for s in range(4):
            j = mod4(mx + mz + s)

            @pl.when(j != mx)
            def _():
                remote(
                    e_in.at[j, at, :], e_in.at[j, at, :], s_e.at[1, d], r_e.at[j, d], row_peer(j)
                ).wait_recv()

            lanes = pl.ds(pl.multiple_of(j * NS, NS), NS)

            def finish(c, carry):
                sub = pl.ds(pl.multiple_of(piece * PIECE + c * 256, 256), 256)
                entering = e_in[j, sub, :]
                carried = lax.dot_general(
                    c_ref[:, lanes], entering, (((1,), (1,)), ((), ())),
                    preferred_element_type=F32,
                )
                for q in range(2):
                    scale = [
                        jnp.broadcast_to(
                            ecum_ref[j, piece * 2 + c, :, 2 * q + k : 2 * q + k + 1], (ROWS, 128)
                        )
                        for k in range(2)
                    ]
                    wide = pl.ds(
                        pl.multiple_of(j * GW + piece * PIECE + c * 256 + q * 128, 128), 128
                    )
                    out_ref[:, wide] = (
                        inner[:, wide]
                        + jnp.where(low, scale[0], scale[1]) * carried[:, q * 128 : q * 128 + 128]
                    ).astype(BF16)
                own = jnp.dot(ft[j, sub, :], b_ref[:, lanes], preferred_element_type=F32)
                factor = widen(wg_ref[j, pl.ds(piece * 8 + c * 4, 4), :], 4)
                leaving = (own + factor * entering.astype(F32)).astype(BF16)
                snap[j, pl.ds(piece * 8 + c * 4, 4)] = leaving.reshape(4, MP, NS)
                return carry

            lax.fori_loop(0, 2, finish, 0)
            owner = 2 * j + piece // 2
            half = lax.rem(piece, 2)
            source = snap.at[j, pl.ds(pl.multiple_of(piece * 8, 8), 8)]
            target = pool_ref.at[rep, pl.ds(pl.multiple_of(half * 8, 8), 8)]

            @pl.when(owner != rep)
            def _():
                remote(
                    source, target, s_p.at[s, d], r_p.at[rep, half], (ctx, owner)
                ).start()

            @pl.when(owner == rep)
            def _():
                pltpu.make_async_copy(source, target, l_p.at[half]).start()

    for c in sent:
        c.wait_send()
    for d in range(4):
        piece = mod4(my + d)
        for s in range(4):
            j = mod4(mx + mz + s)
            owner = 2 * j + piece // 2
            half = lax.rem(piece, 2)
            source = snap.at[j, pl.ds(pl.multiple_of(piece * 8, 8), 8)]
            target = pool_ref.at[rep, pl.ds(pl.multiple_of(half * 8, 8), 8)]

            @pl.when(owner != rep)
            def _():
                remote(
                    source, target, s_p.at[s, d], r_p.at[rep, half], (ctx, owner)
                ).wait_send()

            @pl.when(owner == rep)
            def _():
                pltpu.make_async_copy(source, target, l_p.at[half]).wait()
    for i in range(1, 8):
        other = lax.rem(rep + i, 8)
        for half in range(2):
            target = pool_ref.at[other, pl.ds(half * 8, 8)]
            remote(target, target, s_p.at[0, 0], r_p.at[other, half], (ctx, other)).wait_recv()


def ssm_call(x, b, c, ef, cumt, cumg, ecum, wg, live, skip):
    dma = pltpu.SemaphoreType.DMA
    vmem = pl.BlockSpec(memory_space=pltpu.VMEM)
    return pl.pallas_call(
        ssm_kernel,
        out_shape=(
            jax.ShapeDtypeStruct((ROWS, GR * GW), BF16),
            jax.ShapeDtypeStruct((8, 16, MP, NS), BF16),
        ),
        in_specs=[vmem] * 10,
        out_specs=(vmem, pl.BlockSpec(memory_space=pl.ANY)),
        scratch_shapes=[
            pltpu.VMEM((4, GW, ROWS), BF16),
            pltpu.VMEM((4, GW, ROWS), BF16),
            pltpu.VMEM((4, ROWS, NS), BF16),
            pltpu.VMEM((4, HG, 128), F32),
            pltpu.VMEM((3, GW, NS), F32),
            pltpu.VMEM((4, HG, 128), F32),
            pltpu.VMEM((GW, NS), BF16),
            pltpu.VMEM((4, PIECE, NS), BF16),
            pltpu.VMEM((4, 8, 128), F32),
            pltpu.VMEM((4, PIECE, NS), BF16),
            pltpu.VMEM((4, PIECE, NS), BF16),
            pltpu.VMEM((4, GW, NS), BF16),
            pltpu.VMEM((4, GW, NS), BF16),
            pltpu.VMEM((ROWS, GR * GW), F32),
            pltpu.VMEM((4, HG, MP, NS), BF16),
            dma((4,)), dma((4,)), dma((4,)), dma((4,)), dma((4,)), dma((4,)),
            dma((4,)), dma((4,)), dma((4,)), dma((4,)), dma((4,)), dma((4,)),
            dma((4, 4)), dma((4, 4)), dma((4, 4)), dma((8, 2)), dma((2,)),
        ],
        compiler_params=pltpu.CompilerParams(
            collective_id=0, has_side_effects=True, vmem_limit_bytes=56 << 20
        ),
        name="ssm_exchange",
    )(x, b, c, ef, cumt, cumg, ecum, wg, live, skip)


def attend_kernel(limits, q_ref, kv_ref, out_ref):
    first = limits[0]
    length = limits[1]
    tile = 256
    tiles = (jnp.minimum(first + ROWS, length) + tile - 1) // tile
    scale = math.log2(math.e) / math.sqrt(HD)
    query_pos = first + lax.broadcasted_iota(jnp.int32, (ROWS, tile), 0)
    key_off = lax.broadcasted_iota(jnp.int32, (ROWS, tile), 1)
    for k in range(8):
        query = jnp.concatenate(
            [q_ref[:, (4 * k + i) * HD : (4 * k + i + 1) * HD] for i in range(4)], axis=0
        )

        def step(t, carry):
            top, total, acc = carry
            at = pl.ds(pl.multiple_of(t * tile, tile), tile)
            scores = lax.dot_general(
                query, kv_ref[at, k * HD : (k + 1) * HD], (((1,), (1,)), ((), ())),
                preferred_element_type=F32,
            )
            key_pos = key_off + t * tile
            bias = jnp.where((key_pos <= query_pos) & (key_pos < length), 0.0, -1e30)
            scores = scores + jnp.concatenate([bias] * 4, axis=0)
            new_top = jnp.maximum(top, jnp.max(scores, axis=1, keepdims=True))
            weights = jnp.exp2((scores - new_top) * scale)
            fix = jnp.exp2((top - new_top) * scale)
            total = total * fix + jnp.sum(weights, axis=1, keepdims=True)
            acc = acc * fix + jnp.dot(
                weights.astype(BF16), kv_ref[at, 1024 + k * HD : 1024 + (k + 1) * HD],
                preferred_element_type=F32,
            )
            return new_top, total, acc

        top, total, acc = lax.fori_loop(
            0, tiles, step,
            (
                jnp.full((4 * ROWS, 1), -1e30, F32),
                jnp.zeros((4 * ROWS, 1), F32),
                jnp.zeros((4 * ROWS, HD), F32),
            ),
        )
        result = (acc / total).astype(BF16)
        for i in range(4):
            out_ref[:, (4 * k + i) * HD : (4 * k + i + 1) * HD] = result[i * ROWS : (i + 1) * ROWS]


def attend_call(limits, q, kv):
    vmem = pl.BlockSpec(memory_space=pltpu.VMEM)
    return pl.pallas_call(
        attend_kernel,
        out_shape=jax.ShapeDtypeStruct((ROWS, 4096), BF16),
        in_specs=[pl.BlockSpec(memory_space=pltpu.SMEM), vmem, vmem],
        out_specs=vmem,
        compiler_params=pltpu.CompilerParams(vmem_limit_bytes=48 << 20),
        cost_estimate=pl.CostEstimate(
            flops=4 << 30, bytes_accessed=10 << 20, transcendentals=8 << 20
        ),
        name="attend",
    )(limits, q, kv)


def body(
    queries, cache_keys, cache_values, ssm_input, input_map, output_map, log_decay, skip_gain,
    lengths, page_owner,
):
    rep_count = lax.axis_size("rep")
    my_index = lax.axis_index("ctx")
    length = lengths[0]
    key_rows = cache_keys[0]
    value_rows = cache_values[0]
    kv_width = key_rows.shape[1]
    first = my_index * ROWS

    both = jnp.concatenate([key_rows, value_rows], axis=1)
    gathered = lax.all_gather(both, "ctx", axis=0, tiled=True)

    live = (first < length).astype(F32)
    cum = jnp.cumsum(log_decay[0] * live, axis=0)
    cumt = jnp.transpose(cum)
    last = cumt[:, -1:]
    ef = (jnp.exp(last - cumt) * live).reshape(GR, HG, ROWS)
    wg = jnp.broadcast_to(jnp.exp(last), (128, 128)).reshape(GR, HG, 128)
    cumg = jnp.transpose(cum.reshape(ROWS, GR, HG), (1, 0, 2))
    ecum = jnp.transpose(jnp.exp(cum).reshape(ROWS, GR, 8, 4), (1, 2, 0, 3))
    skip = jnp.broadcast_to(jnp.repeat(skip_gain, MP)[None], (8, GR * GW))
    ssm_rows, pool = ssm_call(
        ssm_input[0], input_map[0], output_map[0], ef, cumt.reshape(GR, HG, ROWS), cumg, ecum,
        wg, jnp.broadcast_to(live, (8, 128)), skip,
    )

    page_rows = ROWS // PAGE
    stacked = jnp.stack(
        [
            key_rows.reshape(page_rows, PAGE, kv_width),
            value_rows.reshape(page_rows, PAGE, kv_width),
        ],
        axis=1,
    )
    page_number = my_index * page_rows + jnp.arange(page_rows, dtype=jnp.int32)
    alive_page = page_number * PAGE < length
    owners = page_owner[0, :, 0]
    onehot = (owners[:, None] == jnp.arange(rep_count, dtype=jnp.int32)[None, :]).astype(jnp.int32)
    ranking = jnp.cumsum(onehot, axis=0) - onehot
    slot_index = jnp.sum(ranking * onehot, axis=1)
    selector = jnp.transpose(onehot)[:, None, :] * (
        slot_index[None, None, :] == jnp.arange(CAP, dtype=jnp.int32)[None, :, None]
    ).astype(jnp.int32)
    selector = selector * alive_page.astype(jnp.int32)[None, None, :]
    buffer = jnp.einsum(
        "oqp,px->oqx",
        selector.astype(BF16),
        stacked.reshape(page_rows, 2 * PAGE * kv_width),
        preferred_element_type=F32,
    ).astype(BF16)
    buffer = buffer.reshape(rep_count, CAP, 2, PAGE, kv_width)
    page_ids = jnp.sum(selector * (page_number + 1)[None, None, :], axis=2) - 1
    got_pages = lax.all_to_all(buffer, "rep", split_axis=0, concat_axis=0, tiled=True)
    got_ids = lax.all_to_all(page_ids, "rep", split_axis=0, concat_axis=0, tiled=True)

    limits = jnp.stack([first, length]).astype(jnp.int32)
    attention_rows = attend_call(limits, queries[0], gathered)
    return (
        attention_rows[None],
        ssm_rows[None],
        pool[None],
        got_pages[None, None],
        got_ids[None, None],
    )


def solution(mesh):
    rows = P("rep", "ctx", None)
    return jax.shard_map(
        body,
        mesh=mesh,
        in_specs=(rows, rows, rows, rows, rows, rows, rows, P(), P("rep"), rows),
        out_specs=(
            rows,
            rows,
            P("ctx", None, "rep", None, None),
            P("ctx", "rep", None, None, None, None, None),
            P("ctx", "rep", None, None),
        ),
        check_vma=False,
    )
```

```python
import math

import jax
import jax.numpy as jnp
from jax import lax
from jax.experimental import pallas as pl
from jax.experimental.pallas import tpu as pltpu
from jax.sharding import PartitionSpec as P

HD = 128
GR = 4
PAGE = 16
CAP = 4
MP = 64
NS = 256
ROWS = 128
HG = 32
GW = HG * MP
HALF = GW // 2
MESH = pl.DeviceIdType.MESH
F32 = jnp.float32
BF16 = jnp.bfloat16
ORDER = (1, 3, 2)


def mod4(v):
    return lax.rem(v + 8, 4)


def chunk_rows(piece):
    return pl.ds(pl.multiple_of(piece * 256, 256), 256)


def widen(rows):
    heads = rows.shape[0]
    both = jnp.concatenate([rows, rows], axis=1)
    return jnp.broadcast_to(both[:, None, :], (heads, MP, NS)).reshape(heads * MP, NS)


def pair_kernel(
    meta, q_ref, k_ref, v_ref, x_hbm, b_ref, c_ref, decay_ref, skip_ref,
    attn_ref, out_ref, pool_ref, pages_ref, ids_ref,
    x_ref, ef, cumt, cumg, ecum, wg, ft, ft_in, b_in, w_in, part, wprod, t_out, t_in, w4_in,
    e0_out, e0_in, e_out, e_in, inner, snap, q_in, kv_in, a_out, page_buf, id_buf,
    l_x, l_q, l_a, l_p, l_g, l_i,
    s_k, r_k, s_v, r_v, s_q, r_q, s_kv, r_kv, s_a, r_a, s_g, r_g, s_i, r_i,
    s_ft, r_ft, s_b, r_b, s_w, r_w, s_t, r_t, s_w4, r_w4, s_e0, r_e0, s_e, r_e, s_p, r_p,
):
    ctx = lax.axis_index("ctx")
    rep = lax.axis_index("rep")
    mx = lax.rem(ctx, 4)
    my = ctx // 4
    mz = rep // 2
    first = ctx * ROWS
    length = meta[0]

    def row_peer(j):
        return (my * 4 + j, rep)

    def col_peer(j):
        return (j * 4 + mx, rep)

    def remote(src, dst, send, recv, device):
        return pltpu.make_async_remote_copy(
            src_ref=src, dst_ref=dst, send_sem=send, recv_sem=recv, device_id=device,
            device_id_type=MESH,
        )

    local_x = pltpu.make_async_copy(x_hbm, x_ref, l_x)
    local_x.start()
    barrier = pltpu.get_barrier_semaphore()
    for i in range(1, 4):
        pl.semaphore_signal(barrier, inc=1, device_id=row_peer(mod4(mx + i)), device_id_type=MESH)
        pl.semaphore_signal(barrier, inc=1, device_id=col_peer(mod4(my + i)), device_id_type=MESH)
    for i in range(1, 8):
        pl.semaphore_signal(
            barrier, inc=1, device_id=(ctx, lax.rem(rep + i, 8)), device_id_type=MESH
        )

    lane = lax.broadcasted_iota(jnp.int32, (ROWS, 128), 1)
    line = lax.broadcasted_iota(jnp.int32, (ROWS, 128), 0)
    causal = lane <= line
    low = lane < MP
    live = jnp.where(jnp.full((1, 128), first, jnp.int32) < length, 1.0, 0.0)

    cum = jnp.dot(
        jnp.where(causal, 1.0, 0.0), decay_ref[...] * live,
        precision=lax.Precision.HIGHEST, preferred_element_type=F32,
    )
    turned = jnp.transpose(cum)
    last = turned[:, 127:128]
    ef[...] = (jnp.exp(last - turned) * live).reshape(GR, HG, ROWS)
    cumt[...] = turned.reshape(GR, HG, ROWS)
    wg[...] = jnp.broadcast_to(jnp.exp(last), (128, 128)).reshape(GR, HG, 128)
    grown = jnp.exp(cum)
    for g in range(GR):
        cumg[g] = cum[:, g * HG : (g + 1) * HG]
        for p in range(8):
            ecum[g, p] = grown[:, g * HG + p * 4 : g * HG + p * 4 + 4]

    pl.semaphore_wait(barrier, 13)
    sent = []

    def go(copy):
        copy.start()
        sent.append(copy)

    for i in ORDER:
        j = mod4(my + i)
        lanes = pl.ds(pl.multiple_of(j * 256, 256), 256)
        go(remote(k_ref.at[:, lanes], kv_in.at[my, mx, :, pl.ds(0, 256)], s_k.at[i], r_k.at[my],
                  col_peer(j)))
        go(remote(v_ref.at[:, lanes], kv_in.at[my, mx, :, pl.ds(256, 256)], s_v.at[i], r_v.at[my],
                  col_peer(j)))
    for i in ORDER:
        j = mod4(my + i)
        lanes = pl.ds(pl.multiple_of(j * 1024, 1024), 1024)
        go(remote(q_ref.at[:, lanes], q_in.at[my], s_q.at[i], r_q.at[my], col_peer(j)))
    own = pl.ds(pl.multiple_of(my * 256, 256), 256)
    kv_in[my, mx, :, 0:256] = k_ref[:, own]
    kv_in[my, mx, :, 256:512] = v_ref[:, own]
    local_q = pltpu.make_async_copy(
        q_ref.at[:, pl.ds(pl.multiple_of(my * 1024, 1024), 1024)], q_in.at[my], l_q
    )
    local_q.start()
    local_x.wait()

    def fade(j, u):
        def tile(t, carry):
            d = t // 2
            p = lax.rem(t, 2)
            lanes = pl.ds(pl.multiple_of(j * GW + d * 512 + u * 256 + p * 128, 128), 128)
            values = jnp.transpose(x_ref[:, lanes].astype(F32))
            factor = jnp.broadcast_to(
                ef[j, pl.ds(8 * d + 4 * u + 2 * p, 2), :][:, None, :], (2, MP, ROWS)
            ).reshape(128, ROWS)
            ft[j, u, pl.ds(pl.multiple_of(t * 128, 128), 128), :] = (values * factor).astype(BF16)
            return carry

        lax.fori_loop(0, 8, tile, 0, unroll=4)

    for u in range(2):
        for i in ORDER:
            j = mod4(mx + i)
            if u == 0:
                lanes = pl.ds(pl.multiple_of(j * NS, NS), NS)
                go(remote(b_ref.at[:, lanes], b_in.at[mx], s_b.at[i], r_b.at[mx], row_peer(j)))
                go(remote(wg.at[j], w_in.at[mx], s_w.at[i], r_w.at[mx], row_peer(j)))
            fade(j, u)
            go(remote(ft.at[j, u], ft_in.at[mx, u], s_ft.at[u, i], r_ft.at[u, mx], row_peer(j)))
        fade(mx, u)
        ft_in[mx, u] = ft[mx, u]
    b_in[mx] = b_ref[:, pl.ds(pl.multiple_of(mx * NS, NS), NS)]
    w_in[mx] = wg[mx]

    def fill_pages(o, carry):
        labels = []
        picks = []
        for e in range(CAP):
            label = meta[40 + o * CAP + e]
            labels.append(label)
            start = meta[8 + o * CAP + e] * PAGE
            hit = (lane[:PAGE] - line[:PAGE] == start) & (label >= 0)
            picks.append(jnp.where(hit, 1.0, 0.0))
        pick = jnp.concatenate(picks, axis=0).astype(BF16)
        for z, rows in enumerate((k_ref, v_ref)):
            taken = jnp.dot(pick, rows[...], preferred_element_type=F32).astype(BF16)
            page_buf[o, :, z] = taken.reshape(CAP, PAGE, 1024)
        spot = lax.broadcasted_iota(jnp.int32, (8, 128), 1)
        id_buf[o] = jnp.where(
            spot == 0, labels[0],
            jnp.where(spot == 1, labels[1], jnp.where(spot == 2, labels[2], labels[3])),
        )
        return carry

    lax.fori_loop(0, 8, fill_pages, 0)
    for i in range(1, 8):
        o = lax.rem(rep + i, 8)
        go(remote(page_buf.at[o], pages_ref.at[rep], s_g.at[i], r_g.at[rep], (ctx, o)))
        go(remote(id_buf.at[o], ids_ref.at[rep], s_i.at[i], r_i.at[rep], (ctx, o)))
    local_pages = pltpu.make_async_copy(page_buf.at[rep], pages_ref.at[rep], l_g)
    local_pages.start()
    local_ids = pltpu.make_async_copy(id_buf.at[rep], ids_ref.at[rep], l_i)
    local_ids.start()

    def inner_group(g, carry):
        lanes = pl.ds(pl.multiple_of(g * NS, NS), NS)
        products = lax.dot_general(
            c_ref[:, lanes], b_ref[:, lanes], (((1,), (1,)), ((), ())),
            preferred_element_type=F32,
        )
        products = jnp.where(causal, products * live, 0.0)
        for p in range(HG // 2):
            at = pl.ds(pl.multiple_of(g * GW + p * 128, 128), 128)
            values = x_ref[:, at]
            halves = []
            for k in range(2):
                h = 2 * p + k
                column = cumg[g, :, h : h + 1]
                row = cumt[g, h : h + 1, :]
                mix = (products * jnp.exp(jnp.minimum(column - row, 0.0))).astype(BF16)
                halves.append(jnp.dot(mix, values, preferred_element_type=F32))
            inner[:, at] = jnp.where(low, halves[0], halves[1]) + skip_ref[0:1, at] * (
                values.astype(F32) * live
            )
        return carry

    lax.fori_loop(0, GR, inner_group, 0)

    for i in ORDER:
        j = mod4(mx + i)
        remote(b_in.at[j], b_in.at[j], s_b.at[i], r_b.at[j], row_peer(j)).wait_recv()
        remote(w_in.at[j], w_in.at[j], s_w.at[i], r_w.at[j], row_peer(j)).wait_recv()

    running = w_in[0]
    for k in range(1, 4):
        wprod[k - 1] = running
        running = running * w_in[k]
    wprod[3] = running

    def scan_piece(u, piece):
        at = chunk_rows(piece)
        heads = pl.ds(piece * 8 + u * 4, 4)
        state = jnp.dot(ft_in[0, u, at, :], b_in[0], preferred_element_type=F32)
        for k in range(1, 4):
            part[k - 1, u, at, :] = state
            state = state * widen(w_in[k, heads, :]) + jnp.dot(
                ft_in[k, u, at, :], b_in[k], preferred_element_type=F32
            )
        t_out[u, at, :] = state.astype(BF16)

    for u in range(2):
        for i in ORDER:
            j = mod4(mx + i)
            remote(
                ft_in.at[j, u], ft_in.at[j, u], s_ft.at[u, i], r_ft.at[u, j], row_peer(j)
            ).wait_recv()
        for i in ORDER:
            j = mod4(my + i)
            scan_piece(u, j)
            if u == 0:
                heads = pl.ds(pl.multiple_of(j * 8, 8), 8)
                go(remote(wprod.at[3, heads, :], w4_in.at[my], s_w4.at[i], r_w4.at[my],
                          col_peer(j)))
            go(remote(t_out.at[u, chunk_rows(j), :], t_in.at[u, my], s_t.at[u, i], r_t.at[u, my],
                      col_peer(j)))
        scan_piece(u, my)
        t_in[u, my] = t_out[u, chunk_rows(my), :]
        if u == 0:
            w4_in[my] = wprod[3, pl.ds(pl.multiple_of(my * 8, 8), 8), :]
            for i in ORDER:
                j = mod4(my + i)
                for z, (send, recv) in enumerate(((s_k, r_k), (s_v, r_v))):
                    there = kv_in.at[j, mx, :, pl.ds(256 * z, 256)]
                    remote(there, there, send.at[i], recv.at[j], col_peer(j)).wait_recv()
            for i in ORDER:
                j = mod4(mx + i)
                go(remote(kv_in.at[:, mx], kv_in.at[:, mx], s_kv.at[i], r_kv.at[mx], row_peer(j)))

    for u in range(2):
        for i in ORDER:
            j = mod4(my + i)
            remote(t_in.at[u, j], t_in.at[u, j], s_t.at[u, i], r_t.at[u, j], col_peer(j)).wait_recv()
            if u == 0:
                remote(w4_in.at[j], w4_in.at[j], s_w4.at[i], r_w4.at[j], col_peer(j)).wait_recv()
        state = jnp.zeros((256, NS), F32)
        for k in range(4):
            e0_out[u, k] = state.astype(BF16)
            if k < 3:
                state = state * widen(w4_in[k, 4 * u : 4 * u + 4, :]) + t_in[u, k].astype(F32)
        for i in ORDER:
            j = mod4(my + i)
            go(remote(e0_out.at[u, j], e0_in.at[u, my], s_e0.at[u, i], r_e0.at[u, my], col_peer(j)))
        e0_in[u, my] = e0_out[u, my]

    for u in range(2):
        for d in (0, 1, 3, 2):
            piece = mod4(my + d)
            if d != 0:
                remote(
                    e0_in.at[u, piece], e0_in.at[u, piece], s_e0.at[u, d], r_e0.at[u, piece],
                    col_peer(piece),
                ).wait_recv()
            at = chunk_rows(piece)
            heads = pl.ds(piece * 8 + u * 4, 4)
            e_out[u, 0, at, :] = e0_in[u, piece]
            for k in range(1, 4):
                e_out[u, k, at, :] = (
                    e0_in[u, piece].astype(F32) * widen(wprod[k - 1, heads, :])
                    + part[k - 1, u, at, :]
                ).astype(BF16)
            for i in ORDER:
                j = mod4(mx + i)
                go(remote(e_out.at[u, j, at, :], e_in.at[u, mx, at, :], s_e.at[u, d, i],
                          r_e.at[u, mx, d], row_peer(j)))
            e_in[u, mx, at, :] = e_out[u, mx, at, :]

    for i in ORDER:
        j = mod4(mx + i)
        remote(kv_in.at[:, j], kv_in.at[:, j], s_kv.at[i], r_kv.at[j], row_peer(j)).wait_recv()
    local_q.wait()
    for i in ORDER:
        j = mod4(my + i)
        remote(q_in.at[j], q_in.at[j], s_q.at[i], r_q.at[j], col_peer(j)).wait_recv()

    scale = math.log2(math.e) / math.sqrt(HD)
    key_off = lax.broadcasted_iota(jnp.int32, (1, 512), 1)
    spread = lax.broadcasted_iota(jnp.int32, (ROWS, 512), 1) - lax.broadcasted_iota(
        jnp.int32, (ROWS, 512), 0
    )

    def attend(i, h):
        def two_heads(a, carry):
            wide = [
                pl.ds(pl.multiple_of((4 * h + 2 * a + r) * HD, HD), HD) for r in range(2)
            ]
            query = jnp.concatenate([q_in[i, :, wide[0]], q_in[i, :, wide[1]]], axis=0)
            scores = []
            for t in range(i + 1):
                keys = kv_in[t, :, :, h * HD : (h + 1) * HD].reshape(512, HD)
                raw = lax.dot_general(
                    query, keys, (((1,), (1,)), ((), ())), preferred_element_type=F32
                )
                if t > 0:
                    raw = raw + jnp.where(key_off + t * 512 < length, 0.0, -1e30)
                if t == i:
                    bias = jnp.where(spread <= mx * ROWS, 0.0, -1e30)
                    raw = raw + jnp.concatenate([bias, bias], axis=0)
                scores.append(raw)
            top = scores[0]
            for raw in scores[1:]:
                top = jnp.maximum(top, raw)
            top = jnp.max(top, axis=1, keepdims=True)
            total = None
            acc = None
            for t in range(i + 1):
                weights = jnp.exp2((scores[t] - top) * scale)
                values = kv_in[t, :, :, 256 + h * HD : 256 + (h + 1) * HD].reshape(512, HD)
                more = jnp.sum(weights, axis=1, keepdims=True)
                term = jnp.dot(weights.astype(BF16), values, preferred_element_type=F32)
                total = more if total is None else total + more
                acc = term if acc is None else acc + term
            result = (acc / total).astype(BF16)
            for r in range(2):
                a_out[i, :, wide[r]] = result[r * ROWS : (r + 1) * ROWS]
            return carry

        lax.fori_loop(0, 2, two_heads, 0)

    def a_copies(i):
        target = attn_ref.at[:, pl.ds(pl.multiple_of(my * 1024, 1024), 1024)]
        return (
            remote(a_out.at[i], target, s_a.at[i], r_a.at[my], col_peer(i)),
            pltpu.make_async_copy(a_out.at[i], target, l_a),
        )

    def snap_copies(u, d, s):
        piece = mod4(my + d)
        j = mod4(mx + mz + s)
        owner = 2 * j + piece // 2
        half = lax.rem(piece, 2)
        source = snap.at[j, pl.ds(piece * 8 + 4 * u, 4)]
        target = pool_ref.at[rep, pl.ds(half * 8 + 4 * u, 4)]
        return (
            owner,
            remote(source, target, s_p.at[u, d, s], r_p.at[rep, half, u], (ctx, owner)),
            pltpu.make_async_copy(source, target, l_p.at[half, u]),
        )

    units = [(3, 0), (3, 1), (2, 0), (2, 1), (1, 0), (1, 1), (0, 0), (0, 1)]
    for u in range(2):
        for d in (0, 1, 3, 2):
            piece = mod4(my + d)
            at = chunk_rows(piece)

            def finish(s, carry):
                j = mod4(mx + mz + s)

                @pl.when(j != mx)
                def _():
                    remote(
                        e_in.at[u, j, at, :], e_in.at[u, j, at, :], s_e.at[u, d, 1],
                        r_e.at[u, j, d], row_peer(j),
                    ).wait_recv()

                lanes = pl.ds(pl.multiple_of(j * NS, NS), NS)
                entering = e_in[u, j, at, :]
                mine = jnp.dot(ft[j, u, at, :], b_ref[:, lanes], preferred_element_type=F32)
                factor = widen(wg[j, pl.ds(piece * 8 + u * 4, 4), :])
                leaving = (mine + factor * entering.astype(F32)).astype(BF16)
                snap[j, pl.ds(piece * 8 + u * 4, 4)] = leaving.reshape(4, MP, NS)
                owner, away, here = snap_copies(u, d, s)

                @pl.when(owner != rep)
                def _():
                    away.start()

                @pl.when(owner == rep)
                def _():
                    here.start()

                carried = lax.dot_general(
                    c_ref[:, lanes], entering, (((1,), (1,)), ((), ())),
                    preferred_element_type=F32,
                )
                for p in range(2):
                    scales = [
                        jnp.broadcast_to(
                            ecum[j, piece * 2 + u, :, 2 * p + k : 2 * p + k + 1], (ROWS, 128)
                        )
                        for k in range(2)
                    ]
                    wide = pl.ds(
                        pl.multiple_of(j * GW + piece * 512 + u * 256 + p * 128, 128), 128
                    )
                    out_ref[:, wide] = (
                        inner[:, wide]
                        + jnp.where(low, scales[0], scales[1]) * carried[:, p * 128 : p * 128 + 128]
                    ).astype(BF16)
                return carry

            lax.fori_loop(0, 4, finish, 0)
            i, h = units.pop(0)
            attend(i, h)
            if h == 1:
                away, here = a_copies(i)
                pl.when(i != my)(away.start)
                pl.when(i == my)(here.start)

    for c in sent:
        c.wait_send()
    for i in range(4):
        away, here = a_copies(i)
        pl.when(i != my)(away.wait_send)
        pl.when(i == my)(here.wait)
    for u in range(2):
        for d in range(4):

            def drain(s, carry):
                owner, away, here = snap_copies(u, d, s)
                pl.when(owner != rep)(away.wait_send)
                pl.when(owner == rep)(here.wait)
                return carry

            lax.fori_loop(0, 4, drain, 0)
    local_pages.wait()
    local_ids.wait()
    for i in ORDER:
        j = mod4(my + i)
        there = attn_ref.at[:, pl.ds(pl.multiple_of(j * 1024, 1024), 1024)]
        remote(there, there, s_a.at[i], r_a.at[j], col_peer(j)).wait_recv()
    for i in range(1, 8):
        o = lax.rem(rep + i, 8)
        remote(pages_ref.at[o], pages_ref.at[o], s_g.at[i], r_g.at[o], (ctx, o)).wait_recv()
        remote(ids_ref.at[o], ids_ref.at[o], s_i.at[i], r_i.at[o], (ctx, o)).wait_recv()
        for half in range(2):
            for u in range(2):
                there = pool_ref.at[o, pl.ds(half * 8 + 4 * u, 4)]
                remote(there, there, s_p.at[0, 0, 0], r_p.at[o, half, u], (ctx, o)).wait_recv()


def pair_call(meta, q, k, v, x, b, c, decay, skip):
    def dma(*shape):
        return pltpu.SemaphoreType.DMA(shape)

    vmem = pl.BlockSpec(memory_space=pltpu.VMEM)
    far = pl.BlockSpec(memory_space=pl.ANY)
    return pl.pallas_call(
        pair_kernel,
        out_shape=(
            jax.ShapeDtypeStruct((ROWS, 4096), BF16),
            jax.ShapeDtypeStruct((ROWS, GR * GW), BF16),
            jax.ShapeDtypeStruct((8, 16, MP, NS), BF16),
            jax.ShapeDtypeStruct((8, CAP, 2, PAGE, 1024), BF16),
            jax.ShapeDtypeStruct((8, 8, 128), jnp.int32),
        ),
        in_specs=[
            pl.BlockSpec(memory_space=pltpu.SMEM), far, vmem, vmem, far, vmem, vmem, vmem, vmem
        ],
        out_specs=(far, vmem, far, far, far),
        scratch_shapes=[
            pltpu.VMEM((ROWS, GR * GW), BF16),
            pltpu.VMEM((GR, HG, ROWS), F32),
            pltpu.VMEM((GR, HG, ROWS), F32),
            pltpu.VMEM((GR, ROWS, HG), F32),
            pltpu.VMEM((GR, 8, ROWS, 4), F32),
            pltpu.VMEM((GR, HG, 128), F32),
            pltpu.VMEM((4, 2, HALF, ROWS), BF16),
            pltpu.VMEM((4, 2, HALF, ROWS), BF16),
            pltpu.VMEM((4, ROWS, NS), BF16),
            pltpu.VMEM((4, HG, 128), F32),
            pltpu.VMEM((3, 2, HALF, NS), F32),
            pltpu.VMEM((4, HG, 128), F32),
            pltpu.VMEM((2, HALF, NS), BF16),
            pltpu.VMEM((2, 4, 256, NS), BF16),
            pltpu.VMEM((4, 8, 128), F32),
            pltpu.VMEM((2, 4, 256, NS), BF16),
            pltpu.VMEM((2, 4, 256, NS), BF16),
            pltpu.VMEM((2, 4, HALF, NS), BF16),
            pltpu.VMEM((2, 4, HALF, NS), BF16),
            pltpu.VMEM((ROWS, GR * GW), F32),
            pltpu.VMEM((4, HG, MP, NS), BF16),
            pltpu.VMEM((4, ROWS, 1024), BF16),
            pltpu.VMEM((4, 4, ROWS, 512), BF16),
            pltpu.VMEM((4, ROWS, 1024), BF16),
            pltpu.VMEM((8, CAP, 2, PAGE, 1024), BF16),
            pltpu.VMEM((8, 8, 128), jnp.int32),
            pltpu.SemaphoreType.DMA, pltpu.SemaphoreType.DMA, pltpu.SemaphoreType.DMA,
            dma(2, 2), pltpu.SemaphoreType.DMA, pltpu.SemaphoreType.DMA,
            dma(4), dma(4), dma(4), dma(4), dma(4), dma(4), dma(4), dma(4), dma(4), dma(4),
            dma(8), dma(8), dma(8), dma(8),
            dma(2, 4), dma(2, 4), dma(4), dma(4), dma(4), dma(4),
            dma(2, 4), dma(2, 4), dma(4), dma(4), dma(2, 4), dma(2, 4),
            dma(2, 4, 4), dma(2, 4, 4), dma(2, 4, 4), dma(8, 2, 2),
        ],
        compiler_params=pltpu.CompilerParams(
            collective_id=0, has_side_effects=True, vmem_limit_bytes=60 << 20
        ),
        name="layer_pair",
    )(meta, q, k, v, x, b, c, decay, skip)


def body(
    queries, cache_keys, cache_values, ssm_input, input_map, output_map, log_decay, skip_gain,
    lengths, page_owner,
):
    page_rows = ROWS // PAGE
    page_number = lax.axis_index("ctx") * page_rows + jnp.arange(page_rows, dtype=jnp.int32)
    alive_page = page_number * PAGE < lengths[0]
    owners = page_owner[0, :, 0]
    same = (owners[:, None] == owners[None, :]) & (
        jnp.arange(page_rows)[None, :] < jnp.arange(page_rows)[:, None]
    )
    slot = jnp.sum(same.astype(jnp.int32), axis=1)
    place = owners * CAP + slot
    chosen = (
        (jnp.arange(8 * CAP, dtype=jnp.int32)[:, None] == place[None, :]) & alive_page[None, :]
    ).astype(jnp.int32)
    index = jnp.sum(chosen * jnp.arange(page_rows, dtype=jnp.int32)[None, :], axis=1)
    label = jnp.sum(chosen * (page_number + 1)[None, :], axis=1) - 1
    meta = jnp.concatenate([jnp.broadcast_to(lengths, (8,)), index, label]).astype(jnp.int32)
    skip = jnp.repeat(skip_gain, MP)[None]
    attention, rows, pool, pages, ids = pair_call(
        meta, queries[0], cache_keys[0], cache_values[0], ssm_input[0], input_map[0],
        output_map[0], log_decay[0], skip,
    )
    return (
        attention[None], rows[None], pool[None], pages[None, None], ids[None, None, :, 0, :CAP]
    )


def solution(mesh):
    rows = P("rep", "ctx", None)
    return jax.shard_map(
        body,
        mesh=mesh,
        in_specs=(rows, rows, rows, rows, rows, rows, rows, P(), P("rep"), rows),
        out_specs=(
            rows,
            rows,
            P("ctx", None, "rep", None, None),
            P("ctx", "rep", None, None, None, None, None),
            P("ctx", "rep", None, None),
        ),
        check_vma=False,
    )
```

```python
import math

import jax
import jax.numpy as jnp
from jax import lax
from jax.experimental import pallas as pl
from jax.experimental.pallas import tpu as pltpu
from jax.sharding import PartitionSpec as P

HD = 128
GR = 4
PAGE = 16
CAP = 4
MP = 64
NS = 256
ROWS = 128
HG = 32
GW = HG * MP
HALF = GW // 2
MESH = pl.DeviceIdType.MESH
F32 = jnp.float32
BF16 = jnp.bfloat16
ORDER = (1, 3, 2)


def mod4(v):
    return lax.rem(v + 8, 4)


def chunk_rows(piece):
    return pl.ds(pl.multiple_of(piece * 256, 256), 256)


def widen(rows):
    heads = rows.shape[0]
    both = jnp.concatenate([rows, rows], axis=1)
    return jnp.broadcast_to(both[:, None, :], (heads, MP, NS)).reshape(heads * MP, NS)


def pair_kernel(
    lengths, owners, gains, q_ref, k_hbm, v_hbm, x_hbm, b_hbm, c_hbm, decay_hbm,
    attn_ref, out_ref, pool_ref, pages_ref, ids_ref,
    k_ref, v_ref, x_ref, b_ref, c_ref, decay_ref, ef, cumt, cumg, ecum, wg, ft, ft_in, b_in, w_in, part, wprod, t_out, t_in, w4_in,
    e0_out, e0_in, e_out, e_in, inner, snap, q_in, kv_in, a_out, page_buf, id_buf,
    l_in, l_q, l_a, l_p, l_g, l_i,
    s_k, r_k, s_v, r_v, s_q, r_q, s_kv, r_kv, s_kw, r_kw, s_a, r_a, s_g, r_g, s_i, r_i,
    s_ft, r_ft, s_b, r_b, s_w, r_w, s_t, r_t, s_w4, r_w4, s_e0, r_e0, s_e, r_e, s_p, r_p,
):
    ctx = lax.axis_index("ctx")
    rep = lax.axis_index("rep")
    mx = lax.rem(ctx, 4)
    my = ctx // 4
    mz = rep // 2
    first = ctx * ROWS
    length = lengths[0]

    def row_peer(j):
        return (my * 4 + j, rep)

    def col_peer(j):
        return (j * 4 + mx, rep)

    def remote(src, dst, send, recv, device):
        return pltpu.make_async_remote_copy(
            src_ref=src, dst_ref=dst, send_sem=send, recv_sem=recv, device_id=device,
            device_id_type=MESH,
        )

    barrier = pltpu.get_barrier_semaphore()
    for i in range(1, 4):
        pl.semaphore_signal(barrier, inc=1, device_id=row_peer(mod4(mx + i)), device_id_type=MESH)
        pl.semaphore_signal(barrier, inc=1, device_id=col_peer(mod4(my + i)), device_id_type=MESH)
    for i in range(1, 8):
        pl.semaphore_signal(
            barrier, inc=1, device_id=(ctx, lax.rem(rep + i, 8)), device_id_type=MESH
        )
    loads = [
        pltpu.make_async_copy(src, dst, l_in.at[n])
        for n, (src, dst) in enumerate((
            (decay_hbm, decay_ref), (x_hbm, x_ref), (b_hbm, b_ref), (k_hbm, k_ref),
            (v_hbm, v_ref), (c_hbm, c_ref),
        ))
    ]
    for load in loads:
        load.start()

    lane = lax.broadcasted_iota(jnp.int32, (ROWS, 128), 1)
    line = lax.broadcasted_iota(jnp.int32, (ROWS, 128), 0)
    causal = lane <= line
    low = lane < MP
    live = jnp.where(jnp.full((1, 128), first, jnp.int32) < length, 1.0, 0.0)

    loads[0].wait()
    cum = jnp.dot(
        jnp.where(causal, 1.0, 0.0), decay_ref[...] * live,
        precision=lax.Precision.HIGHEST, preferred_element_type=F32,
    )
    turned = jnp.transpose(cum)
    last = turned[:, 127:128]
    ef[...] = (jnp.exp(last - turned) * live).reshape(GR, HG, ROWS)
    cumt[...] = turned.reshape(GR, HG, ROWS)
    wg[...] = jnp.broadcast_to(jnp.exp(last), (128, 128)).reshape(GR, HG, 128)
    grown = jnp.exp(cum)
    for g in range(GR):
        cumg[g] = cum[:, g * HG : (g + 1) * HG]
        for p in range(8):
            ecum[g, p] = grown[:, g * HG + p * 4 : g * HG + p * 4 + 4]

    pl.semaphore_wait(barrier, 13)
    sent = []

    def go(copy):
        copy.start()
        sent.append(copy)

    def fade(j, u):
        def tile(t, carry):
            d = t // 2
            p = lax.rem(t, 2)
            lanes = pl.ds(pl.multiple_of(j * GW + d * 512 + u * 256 + p * 128, 128), 128)
            values = jnp.transpose(x_ref[:, lanes].astype(F32))
            factor = jnp.broadcast_to(
                ef[j, pl.ds(8 * d + 4 * u + 2 * p, 2), :][:, None, :], (2, MP, ROWS)
            ).reshape(128, ROWS)
            ft[j, u, pl.ds(pl.multiple_of(t * 128, 128), 128), :] = (values * factor).astype(BF16)
            return carry

        lax.fori_loop(0, 8, tile, 0, unroll=4)

    loads[1].wait()
    loads[2].wait()
    for u in range(2):
        for i in ORDER:
            j = mod4(mx + i)
            if u == 0:
                lanes = pl.ds(pl.multiple_of(j * NS, NS), NS)
                go(remote(b_ref.at[:, lanes], b_in.at[mx], s_b.at[i], r_b.at[mx], row_peer(j)))
                go(remote(wg.at[j], w_in.at[mx], s_w.at[i], r_w.at[mx], row_peer(j)))
            fade(j, u)
            go(remote(ft.at[j, u], ft_in.at[mx, u], s_ft.at[u, i], r_ft.at[u, mx], row_peer(j)))
        if u == 0:
            loads[3].wait()
            loads[4].wait()
            for i in ORDER:
                j = mod4(my + i)
                lanes = pl.ds(pl.multiple_of(j * 256, 256), 256)
                go(remote(k_ref.at[:, lanes], kv_in.at[my, mx, :, pl.ds(0, 256)], s_k.at[i], r_k.at[my],
                          col_peer(j)))
                go(remote(v_ref.at[:, lanes], kv_in.at[my, mx, :, pl.ds(256, 256)], s_v.at[i], r_v.at[my],
                          col_peer(j)))
            for i in ORDER:
                j = mod4(my + i)
                lanes = pl.ds(pl.multiple_of(j * 1024, 1024), 1024)
                go(remote(q_ref.at[:, lanes], q_in.at[my], s_q.at[i], r_q.at[my], col_peer(j)))
            own = pl.ds(pl.multiple_of(my * 256, 256), 256)
            kv_in[my, mx, :, 0:256] = k_ref[:, own]
            kv_in[my, mx, :, 256:512] = v_ref[:, own]
            local_q = pltpu.make_async_copy(
                q_ref.at[:, pl.ds(pl.multiple_of(my * 1024, 1024), 1024)], q_in.at[my], l_q
            )
            local_q.start()
        fade(mx, u)
        ft_in[mx, u] = ft[mx, u]
    b_in[mx] = b_ref[:, pl.ds(pl.multiple_of(mx * NS, NS), NS)]
    w_in[mx] = wg[mx]

    places = []
    for p in range(8):
        slot = jnp.int32(0)
        for r in range(p):
            slot = slot + jnp.where(owners[r] == owners[p], 1, 0)
        places.append(jnp.where(first < length, owners[p] * CAP + slot, -1))

    def fill_pages(o, carry):
        labels = []
        picks = []
        for e in range(CAP):
            page = jnp.int32(-1000)
            for p in range(8):
                page = jnp.where(places[p] == o * CAP + e, p, page)
            labels.append(jnp.where(page >= 0, page + ctx * 8, -1))
            picks.append(jnp.where(lane[:PAGE] - line[:PAGE] == page * PAGE, 1.0, 0.0))
        pick = jnp.concatenate(picks, axis=0).astype(BF16)
        for z, rows in enumerate((k_ref, v_ref)):
            taken = jnp.dot(pick, rows[...], preferred_element_type=F32).astype(BF16)
            page_buf[o, :, z] = taken.reshape(CAP, PAGE, 1024)
        spot = lax.broadcasted_iota(jnp.int32, (8, 128), 1)
        id_buf[o] = jnp.where(
            spot == 0, labels[0],
            jnp.where(spot == 1, labels[1], jnp.where(spot == 2, labels[2], labels[3])),
        )
        return carry

    lax.fori_loop(0, 8, fill_pages, 0)
    for i in range(1, 8):
        o = lax.rem(rep + i, 8)
        go(remote(page_buf.at[o], pages_ref.at[rep], s_g.at[i], r_g.at[rep], (ctx, o)))
        go(remote(id_buf.at[o], ids_ref.at[rep], s_i.at[i], r_i.at[rep], (ctx, o)))
    local_pages = pltpu.make_async_copy(page_buf.at[rep], pages_ref.at[rep], l_g)
    local_pages.start()
    local_ids = pltpu.make_async_copy(id_buf.at[rep], ids_ref.at[rep], l_i)
    local_ids.start()

    loads[5].wait()

    def inner_group(g, carry):
        lanes = pl.ds(pl.multiple_of(g * NS, NS), NS)
        products = lax.dot_general(
            c_ref[:, lanes], b_ref[:, lanes], (((1,), (1,)), ((), ())),
            preferred_element_type=F32,
        )
        products = jnp.where(causal, products * live, 0.0)
        for p in range(HG // 2):
            at = pl.ds(pl.multiple_of(g * GW + p * 128, 128), 128)
            values = x_ref[:, at]
            halves = []
            for k in range(2):
                h = 2 * p + k
                column = cumg[g, :, h : h + 1]
                row = cumt[g, h : h + 1, :]
                mix = (products * jnp.exp(jnp.minimum(column - row, 0.0))).astype(BF16)
                halves.append(jnp.dot(mix, values, preferred_element_type=F32))
            gain = jnp.where(low[0:1], gains[g * HG + 2 * p], gains[g * HG + 2 * p + 1]) * live
            inner[:, at] = jnp.where(low, halves[0], halves[1]) + gain * values.astype(F32)
        return carry

    lax.fori_loop(0, GR, inner_group, 0)

    for i in ORDER:
        j = mod4(mx + i)
        remote(b_in.at[j], b_in.at[j], s_b.at[i], r_b.at[j], row_peer(j)).wait_recv()
        remote(w_in.at[j], w_in.at[j], s_w.at[i], r_w.at[j], row_peer(j)).wait_recv()

    running = w_in[0]
    for k in range(1, 4):
        wprod[k - 1] = running
        running = running * w_in[k]
    wprod[3] = running

    def scan_piece(u, piece):
        at = chunk_rows(piece)
        heads = pl.ds(piece * 8 + u * 4, 4)
        state = jnp.dot(ft_in[0, u, at, :], b_in[0], preferred_element_type=F32)
        for k in range(1, 4):
            part[k - 1, u, at, :] = state
            state = state * widen(w_in[k, heads, :]) + jnp.dot(
                ft_in[k, u, at, :], b_in[k], preferred_element_type=F32
            )
        t_out[u, at, :] = state.astype(BF16)

    for u in range(2):
        for i in ORDER:
            j = mod4(mx + i)
            remote(
                ft_in.at[j, u], ft_in.at[j, u], s_ft.at[u, i], r_ft.at[u, j], row_peer(j)
            ).wait_recv()
        for i in ORDER:
            j = mod4(my + i)
            scan_piece(u, j)
            if u == 0:
                heads = pl.ds(pl.multiple_of(j * 8, 8), 8)
                go(remote(wprod.at[3, heads, :], w4_in.at[my], s_w4.at[i], r_w4.at[my],
                          col_peer(j)))
            go(remote(t_out.at[u, chunk_rows(j), :], t_in.at[u, my], s_t.at[u, i], r_t.at[u, my],
                      col_peer(j)))
        scan_piece(u, my)
        t_in[u, my] = t_out[u, chunk_rows(my), :]
        if u == 0:
            w4_in[my] = wprod[3, pl.ds(pl.multiple_of(my * 8, 8), 8), :]
            for i in ORDER:
                j = mod4(my + i)
                for z, (send, recv) in enumerate(((s_k, r_k), (s_v, r_v))):
                    there = kv_in.at[j, mx, :, pl.ds(256 * z, 256)]
                    remote(there, there, send.at[i], recv.at[j], col_peer(j)).wait_recv()
            for i in (1, 3):
                j = mod4(mx + i)
                go(remote(kv_in.at[:, mx], kv_in.at[:, mx], s_kv.at[i], r_kv.at[mx], row_peer(j)))

    for u in range(2):
        for i in ORDER:
            j = mod4(my + i)
            remote(t_in.at[u, j], t_in.at[u, j], s_t.at[u, i], r_t.at[u, j], col_peer(j)).wait_recv()
            if u == 0:
                remote(w4_in.at[j], w4_in.at[j], s_w4.at[i], r_w4.at[j], col_peer(j)).wait_recv()
        state = jnp.zeros((256, NS), F32)
        for k in range(4):
            e0_out[u, k] = state.astype(BF16)
            if k < 3:
                state = state * widen(w4_in[k, 4 * u : 4 * u + 4, :]) + t_in[u, k].astype(F32)
        for i in ORDER:
            j = mod4(my + i)
            go(remote(e0_out.at[u, j], e0_in.at[u, my], s_e0.at[u, i], r_e0.at[u, my], col_peer(j)))
        e0_in[u, my] = e0_out[u, my]

    for n, i in enumerate((1, 3)):
        j = mod4(mx - i)
        remote(kv_in.at[:, j], kv_in.at[:, j], s_kv.at[i], r_kv.at[j], row_peer(j)).wait_recv()
        there = kv_in.at[pl.ds(2 * n, 2), j]
        go(remote(there, there, s_kw.at[n], r_kw.at[n], row_peer(mod4(mx + i))))

    for u in range(2):
        for d in (0, 1, 3, 2):
            piece = mod4(my + d)
            if d != 0:
                remote(
                    e0_in.at[u, piece], e0_in.at[u, piece], s_e0.at[u, d], r_e0.at[u, piece],
                    col_peer(piece),
                ).wait_recv()
            at = chunk_rows(piece)
            heads = pl.ds(piece * 8 + u * 4, 4)
            e_out[u, 0, at, :] = e0_in[u, piece]
            for k in range(1, 4):
                e_out[u, k, at, :] = (
                    e0_in[u, piece].astype(F32) * widen(wprod[k - 1, heads, :])
                    + part[k - 1, u, at, :]
                ).astype(BF16)
            for i in ORDER:
                j = mod4(mx + i)
                go(remote(e_out.at[u, j, at, :], e_in.at[u, mx, at, :], s_e.at[u, d, i],
                          r_e.at[u, mx, d], row_peer(j)))
            e_in[u, mx, at, :] = e_out[u, mx, at, :]

    for n in range(2):
        there = kv_in.at[pl.ds(2 * n, 2), mod4(mx + 2)]
        remote(there, there, s_kw.at[n], r_kw.at[n], row_peer(mod4(mx + 1))).wait_recv()
    local_q.wait()
    for i in ORDER:
        j = mod4(my + i)
        remote(q_in.at[j], q_in.at[j], s_q.at[i], r_q.at[j], col_peer(j)).wait_recv()

    scale = math.log2(math.e) / math.sqrt(HD)
    key_off = lax.broadcasted_iota(jnp.int32, (1, 512), 1)
    spread = lax.broadcasted_iota(jnp.int32, (ROWS, 512), 1) - lax.broadcasted_iota(
        jnp.int32, (ROWS, 512), 0
    )

    def attend(i, h):
        def two_heads(a, carry):
            wide = [
                pl.ds(pl.multiple_of((4 * h + 2 * a + r) * HD, HD), HD) for r in range(2)
            ]
            query = jnp.concatenate([q_in[i, :, wide[0]], q_in[i, :, wide[1]]], axis=0)
            scores = []
            for t in range(i + 1):
                keys = kv_in[t, :, :, h * HD : (h + 1) * HD].reshape(512, HD)
                raw = lax.dot_general(
                    query, keys, (((1,), (1,)), ((), ())), preferred_element_type=F32
                )
                if t > 0:
                    raw = raw + jnp.where(key_off + t * 512 < length, 0.0, -1e30)
                if t == i:
                    bias = jnp.where(spread <= mx * ROWS, 0.0, -1e30)
                    raw = raw + jnp.concatenate([bias, bias], axis=0)
                scores.append(raw)
            top = scores[0]
            for raw in scores[1:]:
                top = jnp.maximum(top, raw)
            top = jnp.max(top, axis=1, keepdims=True)
            total = None
            acc = None
            for t in range(i + 1):
                weights = jnp.exp2((scores[t] - top) * scale)
                values = kv_in[t, :, :, 256 + h * HD : 256 + (h + 1) * HD].reshape(512, HD)
                more = jnp.sum(weights, axis=1, keepdims=True)
                term = jnp.dot(weights.astype(BF16), values, preferred_element_type=F32)
                total = more if total is None else total + more
                acc = term if acc is None else acc + term
            result = (acc / total).astype(BF16)
            for r in range(2):
                a_out[i, :, wide[r]] = result[r * ROWS : (r + 1) * ROWS]
            return carry

        lax.fori_loop(0, 2, two_heads, 0)

    def a_copies(i):
        target = attn_ref.at[:, pl.ds(pl.multiple_of(my * 1024, 1024), 1024)]
        return (
            remote(a_out.at[i], target, s_a.at[i], r_a.at[my], col_peer(i)),
            pltpu.make_async_copy(a_out.at[i], target, l_a),
        )

    def snap_copies(u, d, s):
        piece = mod4(my + d)
        j = mod4(mx + mz + s)
        owner = 2 * j + piece // 2
        half = lax.rem(piece, 2)
        source = snap.at[j, pl.ds(piece * 8 + 4 * u, 4)]
        target = pool_ref.at[rep, pl.ds(half * 8 + 4 * u, 4)]
        return (
            owner,
            remote(source, target, s_p.at[u, d, s], r_p.at[rep, half, u], (ctx, owner)),
            pltpu.make_async_copy(source, target, l_p.at[half, u]),
        )

    units = [(3, 0), (3, 1), (2, 0), (2, 1), (1, 0), (1, 1), (0, 0), (0, 1)]
    for u in range(2):
        for d in (0, 1, 3, 2):
            piece = mod4(my + d)
            at = chunk_rows(piece)

            def finish(s, carry):
                j = mod4(mx + mz + s)

                @pl.when(j != mx)
                def _():
                    remote(
                        e_in.at[u, j, at, :], e_in.at[u, j, at, :], s_e.at[u, d, 1],
                        r_e.at[u, j, d], row_peer(j),
                    ).wait_recv()

                lanes = pl.ds(pl.multiple_of(j * NS, NS), NS)
                entering = e_in[u, j, at, :]
                mine = jnp.dot(ft[j, u, at, :], b_ref[:, lanes], preferred_element_type=F32)
                factor = widen(wg[j, pl.ds(piece * 8 + u * 4, 4), :])
                leaving = (mine + factor * entering.astype(F32)).astype(BF16)
                snap[j, pl.ds(piece * 8 + u * 4, 4)] = leaving.reshape(4, MP, NS)
                owner, away, here = snap_copies(u, d, s)

                @pl.when(owner != rep)
                def _():
                    away.start()

                @pl.when(owner == rep)
                def _():
                    here.start()

                carried = lax.dot_general(
                    c_ref[:, lanes], entering, (((1,), (1,)), ((), ())),
                    preferred_element_type=F32,
                )
                for p in range(2):
                    scales = [
                        jnp.broadcast_to(
                            ecum[j, piece * 2 + u, :, 2 * p + k : 2 * p + k + 1], (ROWS, 128)
                        )
                        for k in range(2)
                    ]
                    wide = pl.ds(
                        pl.multiple_of(j * GW + piece * 512 + u * 256 + p * 128, 128), 128
                    )
                    out_ref[:, wide] = (
                        inner[:, wide]
                        + jnp.where(low, scales[0], scales[1]) * carried[:, p * 128 : p * 128 + 128]
                    ).astype(BF16)
                return carry

            lax.fori_loop(0, 4, finish, 0)
            i, h = units.pop(0)
            attend(i, h)
            if h == 1:
                away, here = a_copies(i)
                pl.when(i != my)(away.start)
                pl.when(i == my)(here.start)

    for c in sent:
        c.wait_send()
    for i in range(4):
        away, here = a_copies(i)
        pl.when(i != my)(away.wait_send)
        pl.when(i == my)(here.wait)
    for u in range(2):
        for d in range(4):

            def drain(s, carry):
                owner, away, here = snap_copies(u, d, s)
                pl.when(owner != rep)(away.wait_send)
                pl.when(owner == rep)(here.wait)
                return carry

            lax.fori_loop(0, 4, drain, 0)
    local_pages.wait()
    local_ids.wait()
    for i in ORDER:
        j = mod4(my + i)
        there = attn_ref.at[:, pl.ds(pl.multiple_of(j * 1024, 1024), 1024)]
        remote(there, there, s_a.at[i], r_a.at[j], col_peer(j)).wait_recv()
    for i in range(1, 8):
        o = lax.rem(rep + i, 8)
        remote(pages_ref.at[o], pages_ref.at[o], s_g.at[i], r_g.at[o], (ctx, o)).wait_recv()
        remote(ids_ref.at[o], ids_ref.at[o], s_i.at[i], r_i.at[o], (ctx, o)).wait_recv()
        for half in range(2):
            for u in range(2):
                there = pool_ref.at[o, pl.ds(half * 8 + 4 * u, 4)]
                remote(there, there, s_p.at[0, 0, 0], r_p.at[o, half, u], (ctx, o)).wait_recv()


def pair_call(lengths, owners, gains, q, k, v, x, b, c, decay):
    def dma(*shape):
        return pltpu.SemaphoreType.DMA(shape)

    vmem = pl.BlockSpec(memory_space=pltpu.VMEM)
    far = pl.BlockSpec(memory_space=pl.ANY)
    return pl.pallas_call(
        pair_kernel,
        out_shape=(
            jax.ShapeDtypeStruct((ROWS, 4096), BF16),
            jax.ShapeDtypeStruct((ROWS, GR * GW), BF16),
            jax.ShapeDtypeStruct((8, 16, MP, NS), BF16),
            jax.ShapeDtypeStruct((8, CAP, 2, PAGE, 1024), BF16),
            jax.ShapeDtypeStruct((8, 8, 128), jnp.int32),
        ),
        in_specs=[pl.BlockSpec(memory_space=pltpu.SMEM)] * 3 + [far] * 7,
        out_specs=(far, vmem, far, far, far),
        scratch_shapes=[
            pltpu.VMEM((ROWS, 1024), BF16),
            pltpu.VMEM((ROWS, 1024), BF16),
            pltpu.VMEM((ROWS, GR * GW), BF16),
            pltpu.VMEM((ROWS, 1024), BF16),
            pltpu.VMEM((ROWS, 1024), BF16),
            pltpu.VMEM((ROWS, 128), F32),
            pltpu.VMEM((GR, HG, ROWS), F32),
            pltpu.VMEM((GR, HG, ROWS), F32),
            pltpu.VMEM((GR, ROWS, HG), F32),
            pltpu.VMEM((GR, 8, ROWS, 4), F32),
            pltpu.VMEM((GR, HG, 128), F32),
            pltpu.VMEM((4, 2, HALF, ROWS), BF16),
            pltpu.VMEM((4, 2, HALF, ROWS), BF16),
            pltpu.VMEM((4, ROWS, NS), BF16),
            pltpu.VMEM((4, HG, 128), F32),
            pltpu.VMEM((3, 2, HALF, NS), F32),
            pltpu.VMEM((4, HG, 128), F32),
            pltpu.VMEM((2, HALF, NS), BF16),
            pltpu.VMEM((2, 4, 256, NS), BF16),
            pltpu.VMEM((4, 8, 128), F32),
            pltpu.VMEM((2, 4, 256, NS), BF16),
            pltpu.VMEM((2, 4, 256, NS), BF16),
            pltpu.VMEM((2, 4, HALF, NS), BF16),
            pltpu.VMEM((2, 4, HALF, NS), BF16),
            pltpu.VMEM((ROWS, GR * GW), F32),
            pltpu.VMEM((4, HG, MP, NS), BF16),
            pltpu.VMEM((4, ROWS, 1024), BF16),
            pltpu.VMEM((4, 4, ROWS, 512), BF16),
            pltpu.VMEM((4, ROWS, 1024), BF16),
            pltpu.VMEM((8, CAP, 2, PAGE, 1024), BF16),
            pltpu.VMEM((8, 8, 128), jnp.int32),
            dma(6), pltpu.SemaphoreType.DMA, pltpu.SemaphoreType.DMA,
            dma(2, 2), pltpu.SemaphoreType.DMA, pltpu.SemaphoreType.DMA,
            dma(4), dma(4), dma(4), dma(4), dma(4), dma(4), dma(4), dma(4), dma(2), dma(2),
            dma(4), dma(4),
            dma(8), dma(8), dma(8), dma(8),
            dma(2, 4), dma(2, 4), dma(4), dma(4), dma(4), dma(4),
            dma(2, 4), dma(2, 4), dma(4), dma(4), dma(2, 4), dma(2, 4),
            dma(2, 4, 4), dma(2, 4, 4), dma(2, 4, 4), dma(8, 2, 2),
        ],
        compiler_params=pltpu.CompilerParams(
            collective_id=0, has_side_effects=True, vmem_limit_bytes=60 << 20
        ),
        name="layer_pair",
    )(lengths, owners, gains, q, k, v, x, b, c, decay)


def place_kernel(a, b, c, d, ids, a_out, b_out, c_out, d_out, ids_out, sems):
    copies = []
    for src, dst, parts in ((c, c_out, 8), (b, b_out, 4), (d, d_out, 4), (a, a_out, 2)):
        size = src.shape[0] // parts
        for n in range(parts):
            at = pl.ds(n * size, size)
            copies.append(pltpu.make_async_copy(src.at[at], dst.at[at], sems.at[len(copies)]))
    for copy in copies:
        copy.start()
    turned = jnp.transpose(ids[:, 0, :].astype(F32))
    ids_out[...] = turned[:CAP].astype(jnp.int32)
    for copy in copies:
        copy.wait()


def place_call(*arrays):
    far = pl.BlockSpec(memory_space=pl.ANY)
    vmem = pl.BlockSpec(memory_space=pltpu.VMEM)
    shapes = [jax.ShapeDtypeStruct(x.shape, x.dtype) for x in arrays[:4]]
    return pl.pallas_call(
        place_kernel,
        out_shape=(*shapes, jax.ShapeDtypeStruct((CAP, 8), jnp.int32)),
        in_specs=[far] * 4 + [vmem],
        out_specs=(far, far, far, far, vmem),
        scratch_shapes=[pltpu.SemaphoreType.DMA((18,))],
        compiler_params=pltpu.CompilerParams(vmem_limit_bytes=60 << 20),
        name="place_outputs",
    )(*arrays)


def body(
    queries, cache_keys, cache_values, ssm_input, input_map, output_map, log_decay, skip_gain,
    lengths, page_owner,
):
    results = pair_call(
        lengths, page_owner.reshape(8), skip_gain, queries[0], cache_keys[0], cache_values[0],
        ssm_input[0], input_map[0], output_map[0], log_decay[0],
    )
    attention, rows, pool, pages, ids = place_call(*results)
    return (
        attention[None], rows[None], pool[None], pages[None, None], jnp.transpose(ids)[None, None]
    )


def solution(mesh):
    rows = P("rep", "ctx", None)
    return jax.shard_map(
        body,
        mesh=mesh,
        in_specs=(rows, rows, rows, rows, rows, rows, rows, P(), P("rep"), rows),
        out_specs=(
            rows,
            rows,
            P("ctx", None, "rep", None, None),
            P("ctx", "rep", None, None, None, None, None),
            P("ctx", "rep", None, None),
        ),
        check_vma=False,
    )
```

```python
import math

import jax
import jax.numpy as jnp
from jax import lax
from jax.experimental import pallas as pl
from jax.experimental.pallas import tpu as pltpu
from jax.sharding import PartitionSpec as P

HD = 128
GR = 4
PAGE = 16
CAP = 4
MP = 64
NS = 256
ROWS = 128
HG = 32
GW = HG * MP
HALF = GW // 2
MESH = pl.DeviceIdType.MESH
F32 = jnp.float32
BF16 = jnp.bfloat16
ORDER = (1, 3, 2)


def mod4(v):
    return lax.rem(v + 8, 4)


def chunk_rows(piece):
    return pl.ds(pl.multiple_of(piece * 256, 256), 256)


def widen(rows):
    heads = rows.shape[0]
    both = jnp.concatenate([rows, rows], axis=1)
    return jnp.broadcast_to(both[:, None, :], (heads, MP, NS)).reshape(heads * MP, NS)


def pair_kernel(
    lengths, owners, gains, q_ref, k_hbm, v_hbm, x_hbm, b_hbm, c_hbm, decay_hbm,
    attn_ref, out_ref, pool_ref, pages_ref, ids_ref,
    k_ref, v_ref, x_ref, b_ref, c_ref, decay_ref, ef, cumt, cumg, ecum, wg, ft, ft_in, b_in, w_in, part, wprod, t_out, t_in, w4_in,
    e0_out, e0_in, e_out, e_in, inner, snap, q_in, kv_in, a_out, page_buf, id_buf,
    l_in, l_q, l_a, l_p, l_g, l_i,
    s_k, r_k, s_v, r_v, s_q, r_q, s_kv, r_kv, s_kw, r_kw, s_a, r_a, s_g, r_g, s_i, r_i,
    s_ft, r_ft, s_b, r_b, s_w, r_w, s_t, r_t, s_w4, r_w4, s_e0, r_e0, s_e, r_e, s_p, r_p,
):
    ctx = lax.axis_index("ctx")
    rep = lax.axis_index("rep")
    mx = lax.rem(ctx, 4)
    my = ctx // 4
    mz = rep // 2
    first = ctx * ROWS
    length = lengths[0]

    def row_peer(j):
        return (my * 4 + j, rep)

    def col_peer(j):
        return (j * 4 + mx, rep)

    def remote(src, dst, send, recv, device):
        return pltpu.make_async_remote_copy(
            src_ref=src, dst_ref=dst, send_sem=send, recv_sem=recv, device_id=device,
            device_id_type=MESH,
        )

    barrier = pltpu.get_barrier_semaphore()
    for i in range(1, 4):
        pl.semaphore_signal(barrier, inc=1, device_id=row_peer(mod4(mx + i)), device_id_type=MESH)
        pl.semaphore_signal(barrier, inc=1, device_id=col_peer(mod4(my + i)), device_id_type=MESH)
    for i in range(1, 8):
        pl.semaphore_signal(
            barrier, inc=1, device_id=(ctx, lax.rem(rep + i, 8)), device_id_type=MESH
        )
    loads = [
        pltpu.make_async_copy(src, dst, l_in.at[n])
        for n, (src, dst) in enumerate((
            (decay_hbm, decay_ref), (x_hbm, x_ref), (b_hbm, b_ref), (k_hbm, k_ref),
            (v_hbm, v_ref), (c_hbm, c_ref),
        ))
    ]
    for load in loads:
        load.start()

    lane = lax.broadcasted_iota(jnp.int32, (ROWS, 128), 1)
    line = lax.broadcasted_iota(jnp.int32, (ROWS, 128), 0)
    causal = lane <= line
    low = lane < MP
    live = jnp.where(jnp.full((1, 128), first, jnp.int32) < length, 1.0, 0.0)

    loads[0].wait()
    cum = jnp.dot(
        jnp.where(causal, 1.0, 0.0), decay_ref[...] * live,
        precision=lax.Precision.HIGHEST, preferred_element_type=F32,
    )
    turned = jnp.transpose(cum)
    last = turned[:, 127:128]
    ef[...] = (jnp.exp(last - turned) * live).reshape(GR, HG, ROWS)
    cumt[...] = turned.reshape(GR, HG, ROWS)
    wg[...] = jnp.broadcast_to(jnp.exp(last), (128, 128)).reshape(GR, HG, 128)
    grown = jnp.exp(cum)
    for g in range(GR):
        cumg[g] = cum[:, g * HG : (g + 1) * HG]
        for p in range(8):
            ecum[g, p] = grown[:, g * HG + p * 4 : g * HG + p * 4 + 4]

    pl.semaphore_wait(barrier, 13)
    sent = []

    def go(copy):
        copy.start()
        sent.append(copy)

    def fade(j, u):
        def tile(t, carry):
            d = t // 2
            p = lax.rem(t, 2)
            lanes = pl.ds(pl.multiple_of(j * GW + d * 512 + u * 256 + p * 128, 128), 128)
            values = jnp.transpose(x_ref[:, lanes].astype(F32))
            factor = jnp.broadcast_to(
                ef[j, pl.ds(8 * d + 4 * u + 2 * p, 2), :][:, None, :], (2, MP, ROWS)
            ).reshape(128, ROWS)
            ft[j, u, pl.ds(pl.multiple_of(t * 128, 128), 128), :] = (values * factor).astype(BF16)
            return carry

        lax.fori_loop(0, 8, tile, 0, unroll=4)

    loads[1].wait()
    loads[2].wait()
    for u in range(2):
        for i in ORDER:
            j = mod4(mx + i)
            if u == 0:
                lanes = pl.ds(pl.multiple_of(j * NS, NS), NS)
                go(remote(b_ref.at[:, lanes], b_in.at[mx], s_b.at[i], r_b.at[mx], row_peer(j)))
                go(remote(wg.at[j], w_in.at[mx], s_w.at[i], r_w.at[mx], row_peer(j)))
            fade(j, u)
            go(remote(ft.at[j, u], ft_in.at[mx, u], s_ft.at[u, i], r_ft.at[u, mx], row_peer(j)))
        if u == 0:
            loads[3].wait()
            loads[4].wait()
            for i in ORDER:
                j = mod4(my + i)
                lanes = pl.ds(pl.multiple_of(j * 256, 256), 256)
                go(remote(k_ref.at[:, lanes], kv_in.at[my, mx, :, pl.ds(0, 256)], s_k.at[i], r_k.at[my],
                          col_peer(j)))
                go(remote(v_ref.at[:, lanes], kv_in.at[my, mx, :, pl.ds(256, 256)], s_v.at[i], r_v.at[my],
                          col_peer(j)))
            own = pl.ds(pl.multiple_of(my * 256, 256), 256)
            kv_in[my, mx, :, 0:256] = k_ref[:, own]
            kv_in[my, mx, :, 256:512] = v_ref[:, own]
            local_q = pltpu.make_async_copy(
                q_ref.at[:, pl.ds(pl.multiple_of(my * 1024, 1024), 1024)], q_in.at[my], l_q
            )
            local_q.start()
        fade(mx, u)
        ft_in[mx, u] = ft[mx, u]
    b_in[mx] = b_ref[:, pl.ds(pl.multiple_of(mx * NS, NS), NS)]
    w_in[mx] = wg[mx]

    places = []
    for p in range(8):
        slot = jnp.int32(0)
        for r in range(p):
            slot = slot + jnp.where(owners[r] == owners[p], 1, 0)
        places.append(jnp.where(first < length, owners[p] * CAP + slot, -1))

    def fill_pages(o, carry):
        labels = []
        picks = []
        for e in range(CAP):
            page = jnp.int32(-1000)
            for p in range(8):
                page = jnp.where(places[p] == o * CAP + e, p, page)
            labels.append(jnp.where(page >= 0, page + ctx * 8, -1))
            picks.append(jnp.where(lane[:PAGE] - line[:PAGE] == page * PAGE, 1.0, 0.0))
        pick = jnp.concatenate(picks, axis=0).astype(BF16)
        for z, rows in enumerate((k_ref, v_ref)):
            taken = jnp.dot(pick, rows[...], preferred_element_type=F32).astype(BF16)
            page_buf[o, :, z] = taken.reshape(CAP, PAGE, 1024)
        spot = lax.broadcasted_iota(jnp.int32, (8, 128), 1)
        id_buf[o] = jnp.where(
            spot == 0, labels[0],
            jnp.where(spot == 1, labels[1], jnp.where(spot == 2, labels[2], labels[3])),
        )
        return carry

    lax.fori_loop(0, 8, fill_pages, 0)
    for i in range(1, 8):
        o = lax.rem(rep + i, 8)
        go(remote(page_buf.at[o], pages_ref.at[rep], s_g.at[i], r_g.at[rep], (ctx, o)))
        go(remote(id_buf.at[o], ids_ref.at[rep], s_i.at[i], r_i.at[rep], (ctx, o)))
    local_pages = pltpu.make_async_copy(page_buf.at[rep], pages_ref.at[rep], l_g)
    local_pages.start()
    local_ids = pltpu.make_async_copy(id_buf.at[rep], ids_ref.at[rep], l_i)
    local_ids.start()

    loads[5].wait()

    def inner_group(g, carry):
        lanes = pl.ds(pl.multiple_of(g * NS, NS), NS)
        products = lax.dot_general(
            c_ref[:, lanes], b_ref[:, lanes], (((1,), (1,)), ((), ())),
            preferred_element_type=F32,
        )
        products = jnp.where(causal, products * live, 0.0)
        for p in range(HG // 2):
            at = pl.ds(pl.multiple_of(g * GW + p * 128, 128), 128)
            values = x_ref[:, at]
            halves = []
            for k in range(2):
                h = 2 * p + k
                column = cumg[g, :, h : h + 1]
                row = cumt[g, h : h + 1, :]
                mix = (products * jnp.exp(jnp.minimum(column - row, 0.0))).astype(BF16)
                halves.append(jnp.dot(mix, values, preferred_element_type=F32))
            gain = jnp.where(low[0:1], gains[g * HG + 2 * p], gains[g * HG + 2 * p + 1]) * live
            inner[:, at] = jnp.where(low, halves[0], halves[1]) + gain * values.astype(F32)
        return carry

    lax.fori_loop(0, GR, inner_group, 0)

    for i in ORDER:
        j = mod4(mx + i)
        remote(b_in.at[j], b_in.at[j], s_b.at[i], r_b.at[j], row_peer(j)).wait_recv()
        remote(w_in.at[j], w_in.at[j], s_w.at[i], r_w.at[j], row_peer(j)).wait_recv()

    running = w_in[0]
    for k in range(1, 4):
        wprod[k - 1] = running
        running = running * w_in[k]
    wprod[3] = running

    def scan_piece(u, piece):
        at = chunk_rows(piece)
        heads = pl.ds(piece * 8 + u * 4, 4)
        state = jnp.dot(ft_in[0, u, at, :], b_in[0], preferred_element_type=F32)
        for k in range(1, 4):
            part[k - 1, u, at, :] = state
            state = state * widen(w_in[k, heads, :]) + jnp.dot(
                ft_in[k, u, at, :], b_in[k], preferred_element_type=F32
            )
        t_out[u, at, :] = state.astype(BF16)

    def take_inputs(u):
        for i in ORDER:
            j = mod4(mx + i)
            remote(
                ft_in.at[j, u], ft_in.at[j, u], s_ft.at[u, i], r_ft.at[u, j], row_peer(j)
            ).wait_recv()
        for i in ORDER:
            j = mod4(my + i)
            scan_piece(u, j)
            if u == 0:
                heads = pl.ds(pl.multiple_of(j * 8, 8), 8)
                go(remote(wprod.at[3, heads, :], w4_in.at[my], s_w4.at[i], r_w4.at[my],
                          col_peer(j)))
            go(remote(t_out.at[u, chunk_rows(j), :], t_in.at[u, my], s_t.at[u, i], r_t.at[u, my],
                      col_peer(j)))
        scan_piece(u, my)
        t_in[u, my] = t_out[u, chunk_rows(my), :]
        if u == 0:
            w4_in[my] = wprod[3, pl.ds(pl.multiple_of(my * 8, 8), 8), :]

    def start_kv():
        for i in ORDER:
            j = mod4(my + i)
            for z, (send, recv) in enumerate(((s_k, r_k), (s_v, r_v))):
                there = kv_in.at[j, mx, :, pl.ds(256 * z, 256)]
                remote(there, there, send.at[i], recv.at[j], col_peer(j)).wait_recv()
        for i in (1, 3):
            j = mod4(mx + i)
            go(remote(kv_in.at[:, mx], kv_in.at[:, mx], s_kv.at[i], r_kv.at[mx], row_peer(j)))

    def relay_kv():
        for n, i in enumerate((1, 3)):
            j = mod4(mx - i)
            remote(kv_in.at[:, j], kv_in.at[:, j], s_kv.at[i], r_kv.at[j], row_peer(j)).wait_recv()
            there = kv_in.at[pl.ds(2 * n, 2), j]
            go(remote(there, there, s_kw.at[n], r_kw.at[n], row_peer(mod4(mx + i))))

    def send_queries():
        for i in ORDER:
            j = mod4(my + i)
            lanes = pl.ds(pl.multiple_of(j * 1024, 1024), 1024)
            go(remote(q_ref.at[:, lanes], q_in.at[my], s_q.at[i], r_q.at[my], col_peer(j)))

    def chain_rows(u):
        for i in ORDER:
            j = mod4(my + i)
            remote(t_in.at[u, j], t_in.at[u, j], s_t.at[u, i], r_t.at[u, j], col_peer(j)).wait_recv()
            if u == 0:
                remote(w4_in.at[j], w4_in.at[j], s_w4.at[i], r_w4.at[j], col_peer(j)).wait_recv()
        state = jnp.zeros((256, NS), F32)
        for k in range(4):
            e0_out[u, k] = state.astype(BF16)
            if k < 3:
                state = state * widen(w4_in[k, 4 * u : 4 * u + 4, :]) + t_in[u, k].astype(F32)
        for i in ORDER:
            j = mod4(my + i)
            go(remote(e0_out.at[u, j], e0_in.at[u, my], s_e0.at[u, i], r_e0.at[u, my], col_peer(j)))
        e0_in[u, my] = e0_out[u, my]

    def enter(u, d):
        piece = mod4(my + d)
        if d != 0:
            remote(
                e0_in.at[u, piece], e0_in.at[u, piece], s_e0.at[u, d], r_e0.at[u, piece],
                col_peer(piece),
            ).wait_recv()
        at = chunk_rows(piece)
        heads = pl.ds(piece * 8 + u * 4, 4)
        e_out[u, 0, at, :] = e0_in[u, piece]
        for k in range(1, 4):
            e_out[u, k, at, :] = (
                e0_in[u, piece].astype(F32) * widen(wprod[k - 1, heads, :])
                + part[k - 1, u, at, :]
            ).astype(BF16)
        for i in ORDER:
            j = mod4(mx + i)
            go(remote(e_out.at[u, j, at, :], e_in.at[u, mx, at, :], s_e.at[u, d, i],
                      r_e.at[u, mx, d], row_peer(j)))
        e_in[u, mx, at, :] = e_out[u, mx, at, :]

    def snap_copies(u, d, j):
        piece = mod4(my + d)
        owner = 2 * j + piece // 2
        half = lax.rem(piece, 2)
        source = snap.at[j, pl.ds(piece * 8 + 4 * u, 4)]
        target = pool_ref.at[rep, pl.ds(half * 8 + 4 * u, 4)]
        return (
            owner,
            remote(source, target, s_p.at[u, d, j], r_p.at[rep, half, u], (ctx, owner)),
            pltpu.make_async_copy(source, target, l_p.at[half, u]),
        )

    def finish(u, d, j):
        piece = mod4(my + d)
        at = chunk_rows(piece)
        lanes = pl.ds(pl.multiple_of(j * NS, NS), NS)
        entering = e_in[u, j, at, :]
        mine = jnp.dot(ft[j, u, at, :], b_ref[:, lanes], preferred_element_type=F32)
        factor = widen(wg[j, pl.ds(piece * 8 + u * 4, 4), :])
        leaving = (mine + factor * entering.astype(F32)).astype(BF16)
        snap[j, pl.ds(piece * 8 + u * 4, 4)] = leaving.reshape(4, MP, NS)
        owner, away, here = snap_copies(u, d, j)
        pl.when(owner != rep)(away.start)
        pl.when(owner == rep)(here.start)
        carried = lax.dot_general(
            c_ref[:, lanes], entering, (((1,), (1,)), ((), ())), preferred_element_type=F32
        )
        for p in range(2):
            scales = [
                jnp.broadcast_to(
                    ecum[j, piece * 2 + u, :, 2 * p + k : 2 * p + k + 1], (ROWS, 128)
                )
                for k in range(2)
            ]
            wide = pl.ds(pl.multiple_of(j * GW + piece * 512 + u * 256 + p * 128, 128), 128)
            out_ref[:, wide] = (
                inner[:, wide]
                + jnp.where(low, scales[0], scales[1]) * carried[:, p * 128 : p * 128 + 128]
            ).astype(BF16)

    send_queries()
    take_inputs(0)
    start_kv()
    chain_rows(0)
    take_inputs(1)
    steps = [(u, d) for u in range(2) for d in (0, 1, 3, 2)]
    for step in steps[:3]:
        enter(*step)
        finish(*step, mx)
    chain_rows(1)
    relay_kv()


    def wait_attention():
        for n in range(2):
            there = kv_in.at[pl.ds(2 * n, 2), mod4(mx + 2)]
            remote(there, there, s_kw.at[n], r_kw.at[n], row_peer(mod4(mx + 1))).wait_recv()
        local_q.wait()
        for i in ORDER:
            j = mod4(my + i)
            remote(q_in.at[j], q_in.at[j], s_q.at[i], r_q.at[j], col_peer(j)).wait_recv()

    scale = math.log2(math.e) / math.sqrt(HD)
    key_off = lax.broadcasted_iota(jnp.int32, (1, 512), 1)
    spread = lax.broadcasted_iota(jnp.int32, (ROWS, 512), 1) - lax.broadcasted_iota(
        jnp.int32, (ROWS, 512), 0
    )

    def attend(i, h):
        def two_heads(a, carry):
            wide = [
                pl.ds(pl.multiple_of((4 * h + 2 * a + r) * HD, HD), HD) for r in range(2)
            ]
            query = jnp.concatenate([q_in[i, :, wide[0]], q_in[i, :, wide[1]]], axis=0)
            scores = []
            for t in range(i + 1):
                keys = kv_in[t, :, :, h * HD : (h + 1) * HD].reshape(512, HD)
                raw = lax.dot_general(
                    query, keys, (((1,), (1,)), ((), ())), preferred_element_type=F32
                )
                if t > 0:
                    raw = raw + jnp.where(key_off + t * 512 < length, 0.0, -1e30)
                if t == i:
                    bias = jnp.where(spread <= mx * ROWS, 0.0, -1e30)
                    raw = raw + jnp.concatenate([bias, bias], axis=0)
                scores.append(raw)
            top = scores[0]
            for raw in scores[1:]:
                top = jnp.maximum(top, raw)
            top = jnp.max(top, axis=1, keepdims=True)
            total = None
            acc = None
            for t in range(i + 1):
                weights = jnp.exp2((scores[t] - top) * scale)
                values = kv_in[t, :, :, 256 + h * HD : 256 + (h + 1) * HD].reshape(512, HD)
                more = jnp.sum(weights, axis=1, keepdims=True)
                term = jnp.dot(weights.astype(BF16), values, preferred_element_type=F32)
                total = more if total is None else total + more
                acc = term if acc is None else acc + term
            result = (acc / total).astype(BF16)
            for r in range(2):
                a_out[i, :, wide[r]] = result[r * ROWS : (r + 1) * ROWS]
            return carry

        lax.fori_loop(0, 2, two_heads, 0)

    def a_copies(i):
        target = attn_ref.at[:, pl.ds(pl.multiple_of(my * 1024, 1024), 1024)]
        return (
            remote(a_out.at[i], target, s_a.at[i], r_a.at[my], col_peer(i)),
            pltpu.make_async_copy(a_out.at[i], target, l_a),
        )

    units = [(3, 0), (3, 1), (2, 0), (2, 1), (1, 0), (1, 1), (0, 0), (0, 1)]
    for k, (u, d) in enumerate(steps):
        at = chunk_rows(mod4(my + d))
        for i in ORDER:
            j = mod4(mx + i)
            remote(
                e_in.at[u, j, at, :], e_in.at[u, j, at, :], s_e.at[u, d, i], r_e.at[u, j, d],
                row_peer(j),
            ).wait_recv()
        if k + 3 < 8:
            enter(*steps[k + 3])

        def finish_other(n, carry):
            j = mod4(mx + mz + n)
            pl.when(j != mx)(lambda: finish(u, d, j))
            return carry

        lax.fori_loop(0, 4, finish_other, 0)
        if k + 3 < 8:
            finish(*steps[k + 3], mx)
        if k == 1:
            wait_attention()
        if k in (1, 2, 3, 4):
            for i, h in (units.pop(0), units.pop(0)):
                attend(i, h)
                if h == 1:
                    away, here = a_copies(i)
                    pl.when(i != my)(away.start)
                    pl.when(i == my)(here.start)

    for c in sent:
        c.wait_send()
    for i in range(4):
        away, here = a_copies(i)
        pl.when(i != my)(away.wait_send)
        pl.when(i == my)(here.wait)
    for u in range(2):
        for d in range(4):

            def drain(j, carry):
                owner, away, here = snap_copies(u, d, j)
                pl.when(owner != rep)(away.wait_send)
                pl.when(owner == rep)(here.wait)
                return carry

            lax.fori_loop(0, 4, drain, 0)
    local_pages.wait()
    local_ids.wait()
    for i in ORDER:
        j = mod4(my + i)
        there = attn_ref.at[:, pl.ds(pl.multiple_of(j * 1024, 1024), 1024)]
        remote(there, there, s_a.at[i], r_a.at[j], col_peer(j)).wait_recv()
    for i in range(1, 8):
        o = lax.rem(rep + i, 8)
        remote(pages_ref.at[o], pages_ref.at[o], s_g.at[i], r_g.at[o], (ctx, o)).wait_recv()
        remote(ids_ref.at[o], ids_ref.at[o], s_i.at[i], r_i.at[o], (ctx, o)).wait_recv()
        for half in range(2):
            for u in range(2):
                there = pool_ref.at[o, pl.ds(half * 8 + 4 * u, 4)]
                remote(there, there, s_p.at[0, 0, 0], r_p.at[o, half, u], (ctx, o)).wait_recv()


def pair_call(lengths, owners, gains, q, k, v, x, b, c, decay):
    def dma(*shape):
        return pltpu.SemaphoreType.DMA(shape)

    vmem = pl.BlockSpec(memory_space=pltpu.VMEM)
    far = pl.BlockSpec(memory_space=pl.ANY)
    return pl.pallas_call(
        pair_kernel,
        out_shape=(
            jax.ShapeDtypeStruct((ROWS, 4096), BF16),
            jax.ShapeDtypeStruct((ROWS, GR * GW), BF16),
            jax.ShapeDtypeStruct((8, 16, MP, NS), BF16),
            jax.ShapeDtypeStruct((8, CAP, 2, PAGE, 1024), BF16),
            jax.ShapeDtypeStruct((8, 8, 128), jnp.int32),
        ),
        in_specs=[pl.BlockSpec(memory_space=pltpu.SMEM)] * 3 + [far] * 7,
        out_specs=(far, vmem, far, far, far),
        scratch_shapes=[
            pltpu.VMEM((ROWS, 1024), BF16),
            pltpu.VMEM((ROWS, 1024), BF16),
            pltpu.VMEM((ROWS, GR * GW), BF16),
            pltpu.VMEM((ROWS, 1024), BF16),
            pltpu.VMEM((ROWS, 1024), BF16),
            pltpu.VMEM((ROWS, 128), F32),
            pltpu.VMEM((GR, HG, ROWS), F32),
            pltpu.VMEM((GR, HG, ROWS), F32),
            pltpu.VMEM((GR, ROWS, HG), F32),
            pltpu.VMEM((GR, 8, ROWS, 4), F32),
            pltpu.VMEM((GR, HG, 128), F32),
            pltpu.VMEM((4, 2, HALF, ROWS), BF16),
            pltpu.VMEM((4, 2, HALF, ROWS), BF16),
            pltpu.VMEM((4, ROWS, NS), BF16),
            pltpu.VMEM((4, HG, 128), F32),
            pltpu.VMEM((3, 2, HALF, NS), F32),
            pltpu.VMEM((4, HG, 128), F32),
            pltpu.VMEM((2, HALF, NS), BF16),
            pltpu.VMEM((2, 4, 256, NS), BF16),
            pltpu.VMEM((4, 8, 128), F32),
            pltpu.VMEM((2, 4, 256, NS), BF16),
            pltpu.VMEM((2, 4, 256, NS), BF16),
            pltpu.VMEM((2, 4, HALF, NS), BF16),
            pltpu.VMEM((2, 4, HALF, NS), BF16),
            pltpu.VMEM((ROWS, GR * GW), F32),
            pltpu.VMEM((4, HG, MP, NS), BF16),
            pltpu.VMEM((4, ROWS, 1024), BF16),
            pltpu.VMEM((4, 4, ROWS, 512), BF16),
            pltpu.VMEM((4, ROWS, 1024), BF16),
            pltpu.VMEM((8, CAP, 2, PAGE, 1024), BF16),
            pltpu.VMEM((8, 8, 128), jnp.int32),
            dma(6), pltpu.SemaphoreType.DMA, pltpu.SemaphoreType.DMA,
            dma(2, 2), pltpu.SemaphoreType.DMA, pltpu.SemaphoreType.DMA,
            dma(4), dma(4), dma(4), dma(4), dma(4), dma(4), dma(4), dma(4), dma(2), dma(2),
            dma(4), dma(4),
            dma(8), dma(8), dma(8), dma(8),
            dma(2, 4), dma(2, 4), dma(4), dma(4), dma(4), dma(4),
            dma(2, 4), dma(2, 4), dma(4), dma(4), dma(2, 4), dma(2, 4),
            dma(2, 4, 4), dma(2, 4, 4), dma(2, 4, 4), dma(8, 2, 2),
        ],
        compiler_params=pltpu.CompilerParams(
            collective_id=0, has_side_effects=True, vmem_limit_bytes=60 << 20
        ),
        name="layer_pair",
    )(lengths, owners, gains, q, k, v, x, b, c, decay)


PARTS = (4, 4, 8, 8)


def place_kernel(a, b, c, d, ids, a_out, b_out, c_out, d_out, ids_out, ta, tb, tc, td, s_in, s_out):
    loads = []
    stores = []
    for src, mid, dst, parts in zip(
        (a, b, c, d), (ta, tb, tc, td), (a_out, b_out, c_out, d_out), PARTS
    ):
        size = src.shape[0] // parts
        for n in range(parts):
            at = pl.ds(n * size, size)
            k = len(loads)
            loads.append(pltpu.make_async_copy(src.at[at], mid.at[at], s_in.at[k]))
            stores.append(pltpu.make_async_copy(mid.at[at], dst.at[at], s_out.at[k]))
    for load in loads:
        load.start()
    turned = jnp.transpose(ids[:, 0, :].astype(F32))
    ids_out[...] = turned[:CAP].astype(jnp.int32)
    for load, store in zip(loads, stores):
        load.wait()
        store.start()
    for store in stores:
        store.wait()


def place_call(*arrays):
    far = pl.BlockSpec(memory_space=pl.ANY)
    vmem = pl.BlockSpec(memory_space=pltpu.VMEM)
    shapes = [jax.ShapeDtypeStruct(x.shape, x.dtype) for x in arrays[:4]]
    return pl.pallas_call(
        place_kernel,
        out_shape=(*shapes, jax.ShapeDtypeStruct((CAP, 8), jnp.int32)),
        in_specs=[far] * 4 + [vmem],
        out_specs=(far, far, far, far, vmem),
        scratch_shapes=[pltpu.VMEM(x.shape, x.dtype) for x in arrays[:4]]
        + [pltpu.SemaphoreType.DMA((sum(PARTS),)), pltpu.SemaphoreType.DMA((sum(PARTS),))],
        compiler_params=pltpu.CompilerParams(vmem_limit_bytes=60 << 20),
        name="place_outputs",
    )(*arrays)


def body(
    queries, cache_keys, cache_values, ssm_input, input_map, output_map, log_decay, skip_gain,
    lengths, page_owner,
):
    results = pair_call(
        lengths, page_owner.reshape(8), skip_gain, queries[0], cache_keys[0], cache_values[0],
        ssm_input[0], input_map[0], output_map[0], log_decay[0],
    )
    attention, rows, pool, pages, ids = place_call(*results)
    return (
        attention[None], rows[None], pool[None], pages[None, None], jnp.transpose(ids)[None, None]
    )


def solution(mesh):
    rows = P("rep", "ctx", None)
    return jax.shard_map(
        body,
        mesh=mesh,
        in_specs=(rows, rows, rows, rows, rows, rows, rows, P(), P("rep"), rows),
        out_specs=(
            rows,
            rows,
            P("ctx", None, "rep", None, None),
            P("ctx", "rep", None, None, None, None, None),
            P("ctx", "rep", None, None),
        ),
        check_vma=False,
    )
```

```python
import math

import jax
import jax.numpy as jnp
from jax import lax
from jax.experimental import pallas as pl
from jax.experimental.pallas import tpu as pltpu
from jax.sharding import PartitionSpec as P

HD = 128
GR = 4
PAGE = 16
CAP = 4
MP = 64
NS = 256
ROWS = 128
HG = 32
GW = HG * MP
HALF = GW // 2
MESH = pl.DeviceIdType.MESH
F32 = jnp.float32
BF16 = jnp.bfloat16
ORDER = (1, 3, 2)
UNITS = (0, 2, 2, 2, 2, 0, 0, 0)


def mod4(v):
    return lax.rem(v + 8, 4)


def chunk_rows(piece):
    return pl.ds(pl.multiple_of(piece * 256, 256), 256)


def widen(rows):
    heads = rows.shape[0]
    both = jnp.concatenate([rows, rows], axis=1)
    return jnp.broadcast_to(both[:, None, :], (heads, MP, NS)).reshape(heads * MP, NS)


def pair_kernel(
    lengths, owners, gains, q_ref, k_hbm, v_hbm, x_hbm, b_hbm, c_hbm, decay_hbm,
    attn_ref, out_ref, pool_ref, pages_ref, ids_ref,
    k_ref, v_ref, x_ref, b_ref, c_ref, decay_ref, ef, cumt, cumg, ecum, wg, ft, ft_in, b_in, w_in, part, wprod, t_out, t_in, w4_in,
    e0_out, e0_in, e_out, e_in, inner, snap, q_in, kv_in, a_out, page_buf, id_buf,
    l_in, l_q, l_a, l_p, l_g, l_i,
    s_k, r_k, s_v, r_v, s_q, r_q, s_kv, r_kv, s_kw, r_kw, s_a, r_a, s_g, r_g, s_i, r_i,
    s_ft, r_ft, s_b, r_b, s_w, r_w, s_t, r_t, s_w4, r_w4, s_e0, r_e0, s_e, r_e, s_p, r_p,
):
    ctx = lax.axis_index("ctx")
    rep = lax.axis_index("rep")
    mx = lax.rem(ctx, 4)
    my = ctx // 4
    mz = rep // 2
    first = ctx * ROWS
    length = lengths[0]

    def row_peer(j):
        return (my * 4 + j, rep)

    def col_peer(j):
        return (j * 4 + mx, rep)

    def remote(src, dst, send, recv, device):
        return pltpu.make_async_remote_copy(
            src_ref=src, dst_ref=dst, send_sem=send, recv_sem=recv, device_id=device,
            device_id_type=MESH,
        )

    barrier = pltpu.get_barrier_semaphore()
    for i in range(1, 4):
        pl.semaphore_signal(barrier, inc=1, device_id=row_peer(mod4(mx + i)), device_id_type=MESH)
        pl.semaphore_signal(barrier, inc=1, device_id=col_peer(mod4(my + i)), device_id_type=MESH)
    for i in range(1, 8):
        pl.semaphore_signal(
            barrier, inc=1, device_id=(ctx, lax.rem(rep + i, 8)), device_id_type=MESH
        )
    loads = [
        pltpu.make_async_copy(src, dst, l_in.at[n])
        for n, (src, dst) in enumerate((
            (decay_hbm, decay_ref), (x_hbm, x_ref), (b_hbm, b_ref), (k_hbm, k_ref),
            (v_hbm, v_ref), (c_hbm, c_ref),
        ))
    ]
    for load in loads:
        load.start()

    lane = lax.broadcasted_iota(jnp.int32, (ROWS, 128), 1)
    line = lax.broadcasted_iota(jnp.int32, (ROWS, 128), 0)
    causal = lane <= line
    low = lane < MP
    live = jnp.where(jnp.full((1, 128), first, jnp.int32) < length, 1.0, 0.0)

    loads[0].wait()
    cum = jnp.dot(
        jnp.where(causal, 1.0, 0.0), decay_ref[...] * live,
        precision=lax.Precision.HIGHEST, preferred_element_type=F32,
    )
    turned = jnp.transpose(cum)
    last = turned[:, 127:128]
    ef[...] = (jnp.exp(last - turned) * live).reshape(GR, HG, ROWS)
    cumt[...] = turned.reshape(GR, HG, ROWS)
    wg[...] = jnp.broadcast_to(jnp.exp(last), (128, 128)).reshape(GR, HG, 128)
    grown = jnp.exp(cum)
    for g in range(GR):
        cumg[g] = cum[:, g * HG : (g + 1) * HG]
        for p in range(8):
            ecum[g, p] = grown[:, g * HG + p * 4 : g * HG + p * 4 + 4]

    pl.semaphore_wait(barrier, 13)
    sent = []

    def go(copy):
        copy.start()
        sent.append(copy)

    def fade(j, u):
        def tile(t, carry):
            d = t // 2
            p = lax.rem(t, 2)
            lanes = pl.ds(pl.multiple_of(j * GW + d * 512 + u * 256 + p * 128, 128), 128)
            values = jnp.transpose(x_ref[:, lanes].astype(F32))
            factor = jnp.broadcast_to(
                ef[j, pl.ds(8 * d + 4 * u + 2 * p, 2), :][:, None, :], (2, MP, ROWS)
            ).reshape(128, ROWS)
            ft[j, u, pl.ds(pl.multiple_of(t * 128, 128), 128), :] = (values * factor).astype(BF16)
            return carry

        lax.fori_loop(0, 8, tile, 0, unroll=4)

    loads[1].wait()
    loads[2].wait()
    for u in range(2):
        for i in ORDER:
            j = mod4(mx + i)
            if u == 0:
                lanes = pl.ds(pl.multiple_of(j * NS, NS), NS)
                go(remote(b_ref.at[:, lanes], b_in.at[mx], s_b.at[i], r_b.at[mx], row_peer(j)))
                go(remote(wg.at[j], w_in.at[mx], s_w.at[i], r_w.at[mx], row_peer(j)))
            fade(j, u)
            go(remote(ft.at[j, u], ft_in.at[mx, u], s_ft.at[u, i], r_ft.at[u, mx], row_peer(j)))
        if u == 0:
            loads[3].wait()
            loads[4].wait()
            for i in ORDER:
                j = mod4(my + i)
                lanes = pl.ds(pl.multiple_of(j * 256, 256), 256)
                go(remote(k_ref.at[:, lanes], kv_in.at[my, mx, :, pl.ds(0, 256)], s_k.at[i], r_k.at[my],
                          col_peer(j)))
                go(remote(v_ref.at[:, lanes], kv_in.at[my, mx, :, pl.ds(256, 256)], s_v.at[i], r_v.at[my],
                          col_peer(j)))
            own = pl.ds(pl.multiple_of(my * 256, 256), 256)
            kv_in[my, mx, :, 0:256] = k_ref[:, own]
            kv_in[my, mx, :, 256:512] = v_ref[:, own]
            local_q = pltpu.make_async_copy(
                q_ref.at[:, pl.ds(pl.multiple_of(my * 1024, 1024), 1024)], q_in.at[my], l_q
            )
            local_q.start()
        fade(mx, u)
        ft_in[mx, u] = ft[mx, u]
    b_in[mx] = b_ref[:, pl.ds(pl.multiple_of(mx * NS, NS), NS)]
    w_in[mx] = wg[mx]

    places = []
    for p in range(8):
        slot = jnp.int32(0)
        for r in range(p):
            slot = slot + jnp.where(owners[r] == owners[p], 1, 0)
        places.append(jnp.where(first < length, owners[p] * CAP + slot, -1))

    def fill_pages(o, carry):
        labels = []
        picks = []
        for e in range(CAP):
            page = jnp.int32(-1000)
            for p in range(8):
                page = jnp.where(places[p] == o * CAP + e, p, page)
            labels.append(jnp.where(page >= 0, page + ctx * 8, -1))
            picks.append(jnp.where(lane[:PAGE] - line[:PAGE] == page * PAGE, 1.0, 0.0))
        pick = jnp.concatenate(picks, axis=0).astype(BF16)
        for z, rows in enumerate((k_ref, v_ref)):
            taken = jnp.dot(pick, rows[...], preferred_element_type=F32).astype(BF16)
            page_buf[o, :, z] = taken.reshape(CAP, PAGE, 1024)
        spot = lax.broadcasted_iota(jnp.int32, (8, 128), 1)
        id_buf[o] = jnp.where(
            spot == 0, labels[0],
            jnp.where(spot == 1, labels[1], jnp.where(spot == 2, labels[2], labels[3])),
        )
        return carry

    lax.fori_loop(0, 8, fill_pages, 0)
    for i in range(1, 8):
        o = lax.rem(rep + i, 8)
        go(remote(page_buf.at[o], pages_ref.at[rep], s_g.at[i], r_g.at[rep], (ctx, o)))
        go(remote(id_buf.at[o], ids_ref.at[rep], s_i.at[i], r_i.at[rep], (ctx, o)))
    local_pages = pltpu.make_async_copy(page_buf.at[rep], pages_ref.at[rep], l_g)
    local_pages.start()
    local_ids = pltpu.make_async_copy(id_buf.at[rep], ids_ref.at[rep], l_i)
    local_ids.start()

    loads[5].wait()

    def inner_group(g, carry):
        lanes = pl.ds(pl.multiple_of(g * NS, NS), NS)
        products = lax.dot_general(
            c_ref[:, lanes], b_ref[:, lanes], (((1,), (1,)), ((), ())),
            preferred_element_type=F32,
        )
        products = jnp.where(causal, products * live, 0.0)
        for p in range(HG // 2):
            at = pl.ds(pl.multiple_of(g * GW + p * 128, 128), 128)
            values = x_ref[:, at]
            halves = []
            for k in range(2):
                h = 2 * p + k
                column = cumg[g, :, h : h + 1]
                row = cumt[g, h : h + 1, :]
                mix = (products * jnp.exp(jnp.minimum(column - row, 0.0))).astype(BF16)
                halves.append(jnp.dot(mix, values, preferred_element_type=F32))
            gain = jnp.where(low[0:1], gains[g * HG + 2 * p], gains[g * HG + 2 * p + 1]) * live
            inner[:, at] = jnp.where(low, halves[0], halves[1]) + gain * values.astype(F32)
        return carry

    lax.fori_loop(0, GR, inner_group, 0)

    for i in ORDER:
        j = mod4(mx + i)
        remote(b_in.at[j], b_in.at[j], s_b.at[i], r_b.at[j], row_peer(j)).wait_recv()
        remote(w_in.at[j], w_in.at[j], s_w.at[i], r_w.at[j], row_peer(j)).wait_recv()

    running = w_in[0]
    for k in range(1, 4):
        wprod[k - 1] = running
        running = running * w_in[k]
    wprod[3] = running

    def scan_piece(u, piece):
        at = chunk_rows(piece)
        heads = pl.ds(piece * 8 + u * 4, 4)
        state = jnp.dot(ft_in[0, u, at, :], b_in[0], preferred_element_type=F32)
        for k in range(1, 4):
            part[k - 1, u, at, :] = state
            state = state * widen(w_in[k, heads, :]) + jnp.dot(
                ft_in[k, u, at, :], b_in[k], preferred_element_type=F32
            )
        t_out[u, at, :] = state.astype(BF16)

    def take_inputs(u):
        for i in ORDER:
            j = mod4(mx + i)
            remote(
                ft_in.at[j, u], ft_in.at[j, u], s_ft.at[u, i], r_ft.at[u, j], row_peer(j)
            ).wait_recv()
        for i in ORDER:
            j = mod4(my + i)
            scan_piece(u, j)
            if u == 0:
                heads = pl.ds(pl.multiple_of(j * 8, 8), 8)
                go(remote(wprod.at[3, heads, :], w4_in.at[my], s_w4.at[i], r_w4.at[my],
                          col_peer(j)))
            go(remote(t_out.at[u, chunk_rows(j), :], t_in.at[u, my], s_t.at[u, i], r_t.at[u, my],
                      col_peer(j)))
        scan_piece(u, my)
        t_in[u, my] = t_out[u, chunk_rows(my), :]
        if u == 0:
            w4_in[my] = wprod[3, pl.ds(pl.multiple_of(my * 8, 8), 8), :]

    def start_kv():
        for i in ORDER:
            j = mod4(my + i)
            for z, (send, recv) in enumerate(((s_k, r_k), (s_v, r_v))):
                there = kv_in.at[j, mx, :, pl.ds(256 * z, 256)]
                remote(there, there, send.at[i], recv.at[j], col_peer(j)).wait_recv()
        for i in (1, 3):
            j = mod4(mx + i)
            go(remote(kv_in.at[:, mx], kv_in.at[:, mx], s_kv.at[i], r_kv.at[mx], row_peer(j)))

    def relay_kv():
        for n, i in enumerate((1, 3)):
            j = mod4(mx - i)
            remote(kv_in.at[:, j], kv_in.at[:, j], s_kv.at[i], r_kv.at[j], row_peer(j)).wait_recv()
            there = kv_in.at[pl.ds(2 * n, 2), j]
            go(remote(there, there, s_kw.at[n], r_kw.at[n], row_peer(mod4(mx + i))))

    def send_queries():
        for i in ORDER:
            j = mod4(my + i)
            lanes = pl.ds(pl.multiple_of(j * 1024, 1024), 1024)
            go(remote(q_ref.at[:, lanes], q_in.at[my], s_q.at[i], r_q.at[my], col_peer(j)))

    def chain_rows(u):
        for i in ORDER:
            j = mod4(my + i)
            remote(t_in.at[u, j], t_in.at[u, j], s_t.at[u, i], r_t.at[u, j], col_peer(j)).wait_recv()
            if u == 0:
                remote(w4_in.at[j], w4_in.at[j], s_w4.at[i], r_w4.at[j], col_peer(j)).wait_recv()
        state = jnp.zeros((256, NS), F32)
        for k in range(4):
            e0_out[u, k] = state.astype(BF16)
            if k < 3:
                state = state * widen(w4_in[k, 4 * u : 4 * u + 4, :]) + t_in[u, k].astype(F32)
        for i in ORDER:
            j = mod4(my + i)
            go(remote(e0_out.at[u, j], e0_in.at[u, my], s_e0.at[u, i], r_e0.at[u, my], col_peer(j)))
        e0_in[u, my] = e0_out[u, my]

    def enter(u, d):
        piece = mod4(my + d)
        if d != 0:
            remote(
                e0_in.at[u, piece], e0_in.at[u, piece], s_e0.at[u, d], r_e0.at[u, piece],
                col_peer(piece),
            ).wait_recv()
        at = chunk_rows(piece)
        heads = pl.ds(piece * 8 + u * 4, 4)
        e_out[u, 0, at, :] = e0_in[u, piece]
        for k in range(1, 4):
            e_out[u, k, at, :] = (
                e0_in[u, piece].astype(F32) * widen(wprod[k - 1, heads, :])
                + part[k - 1, u, at, :]
            ).astype(BF16)
        for i in ORDER:
            j = mod4(mx + i)
            go(remote(e_out.at[u, j, at, :], e_in.at[u, mx, at, :], s_e.at[u, d, i],
                      r_e.at[u, mx, d], row_peer(j)))
        e_in[u, mx, at, :] = e_out[u, mx, at, :]

    def snap_copies(u, d, j):
        piece = mod4(my + d)
        owner = 2 * j + piece // 2
        half = lax.rem(piece, 2)
        source = snap.at[j, pl.ds(piece * 8 + 4 * u, 4)]
        target = pool_ref.at[rep, pl.ds(half * 8 + 4 * u, 4)]
        return (
            owner,
            remote(source, target, s_p.at[u, d, j], r_p.at[rep, half, u], (ctx, owner)),
            pltpu.make_async_copy(source, target, l_p.at[half, u]),
        )

    def finish(u, d, j):
        piece = mod4(my + d)
        at = chunk_rows(piece)
        lanes = pl.ds(pl.multiple_of(j * NS, NS), NS)
        entering = e_in[u, j, at, :]
        mine = jnp.dot(ft[j, u, at, :], b_ref[:, lanes], preferred_element_type=F32)
        factor = widen(wg[j, pl.ds(piece * 8 + u * 4, 4), :])
        leaving = (mine + factor * entering.astype(F32)).astype(BF16)
        snap[j, pl.ds(piece * 8 + u * 4, 4)] = leaving.reshape(4, MP, NS)
        owner, away, here = snap_copies(u, d, j)
        pl.when(owner != rep)(away.start)
        pl.when(owner == rep)(here.start)
        carried = lax.dot_general(
            c_ref[:, lanes], entering, (((1,), (1,)), ((), ())), preferred_element_type=F32
        )
        for p in range(2):
            scales = [
                jnp.broadcast_to(
                    ecum[j, piece * 2 + u, :, 2 * p + k : 2 * p + k + 1], (ROWS, 128)
                )
                for k in range(2)
            ]
            wide = pl.ds(pl.multiple_of(j * GW + piece * 512 + u * 256 + p * 128, 128), 128)
            out_ref[:, wide] = (
                inner[:, wide]
                + jnp.where(low, scales[0], scales[1]) * carried[:, p * 128 : p * 128 + 128]
            ).astype(BF16)

    send_queries()
    take_inputs(0)
    start_kv()
    chain_rows(0)
    take_inputs(1)
    steps = [(u, d) for u in range(2) for d in (0, 1, 3, 2)]
    for step in steps[:3]:
        enter(*step)
        finish(*step, mx)
    chain_rows(1)
    relay_kv()


    def wait_attention():
        for n in range(2):
            there = kv_in.at[pl.ds(2 * n, 2), mod4(mx + 2)]
            remote(there, there, s_kw.at[n], r_kw.at[n], row_peer(mod4(mx + 1))).wait_recv()
        local_q.wait()
        for i in ORDER:
            j = mod4(my + i)
            remote(q_in.at[j], q_in.at[j], s_q.at[i], r_q.at[j], col_peer(j)).wait_recv()

    scale = math.log2(math.e) / math.sqrt(HD)
    key_off = lax.broadcasted_iota(jnp.int32, (1, 512), 1)
    spread = lax.broadcasted_iota(jnp.int32, (ROWS, 512), 1) - lax.broadcasted_iota(
        jnp.int32, (ROWS, 512), 0
    )

    def attend(i, h):
        def two_heads(a, carry):
            wide = [
                pl.ds(pl.multiple_of((4 * h + 2 * a + r) * HD, HD), HD) for r in range(2)
            ]
            query = jnp.concatenate([q_in[i, :, wide[0]], q_in[i, :, wide[1]]], axis=0)
            scores = []
            for t in range(i + 1):
                keys = kv_in[t, :, :, h * HD : (h + 1) * HD].reshape(512, HD)
                raw = lax.dot_general(
                    query, keys, (((1,), (1,)), ((), ())), preferred_element_type=F32
                )
                if t > 0:
                    raw = raw + jnp.where(key_off + t * 512 < length, 0.0, -1e30)
                if t == i:
                    bias = jnp.where(spread <= mx * ROWS, 0.0, -1e30)
                    raw = raw + jnp.concatenate([bias, bias], axis=0)
                scores.append(raw)
            top = scores[0]
            for raw in scores[1:]:
                top = jnp.maximum(top, raw)
            top = jnp.max(top, axis=1, keepdims=True)
            total = None
            acc = None
            for t in range(i + 1):
                weights = jnp.exp2((scores[t] - top) * scale)
                values = kv_in[t, :, :, 256 + h * HD : 256 + (h + 1) * HD].reshape(512, HD)
                more = jnp.sum(weights, axis=1, keepdims=True)
                term = jnp.dot(weights.astype(BF16), values, preferred_element_type=F32)
                total = more if total is None else total + more
                acc = term if acc is None else acc + term
            result = (acc / total).astype(BF16)
            for r in range(2):
                a_out[i, :, wide[r]] = result[r * ROWS : (r + 1) * ROWS]
            return carry

        lax.fori_loop(0, 2, two_heads, 0)

    def a_copies(i):
        target = attn_ref.at[:, pl.ds(pl.multiple_of(my * 1024, 1024), 1024)]
        return (
            remote(a_out.at[i], target, s_a.at[i], r_a.at[my], col_peer(i)),
            pltpu.make_async_copy(a_out.at[i], target, l_a),
        )

    units = [(3, 0), (3, 1), (2, 0), (2, 1), (1, 0), (1, 1), (0, 0), (0, 1)]
    for k, (u, d) in enumerate(steps):
        at = chunk_rows(mod4(my + d))
        for i in ORDER:
            j = mod4(mx + i)
            remote(
                e_in.at[u, j, at, :], e_in.at[u, j, at, :], s_e.at[u, d, i], r_e.at[u, j, d],
                row_peer(j),
            ).wait_recv()
        if k + 3 < 8:
            enter(*steps[k + 3])

        def finish_other(n, carry):
            j = mod4(mx + mz + n)
            pl.when(j != mx)(lambda: finish(u, d, j))
            return carry

        lax.fori_loop(0, 4, finish_other, 0)
        if k + 3 < 8:
            finish(*steps[k + 3], mx)
        if k == 1:
            wait_attention()
        for _ in range(UNITS[k]):
            i, h = units.pop(0)
            attend(i, h)
            if h == 1:
                away, here = a_copies(i)
                pl.when(i != my)(away.start)
                pl.when(i == my)(here.start)

    for c in sent:
        c.wait_send()
    for i in range(4):
        away, here = a_copies(i)
        pl.when(i != my)(away.wait_send)
        pl.when(i == my)(here.wait)
    for u in range(2):
        for d in range(4):

            def drain(j, carry):
                owner, away, here = snap_copies(u, d, j)
                pl.when(owner != rep)(away.wait_send)
                pl.when(owner == rep)(here.wait)
                return carry

            lax.fori_loop(0, 4, drain, 0)
    local_pages.wait()
    local_ids.wait()
    for i in ORDER:
        j = mod4(my + i)
        there = attn_ref.at[:, pl.ds(pl.multiple_of(j * 1024, 1024), 1024)]
        remote(there, there, s_a.at[i], r_a.at[j], col_peer(j)).wait_recv()
    for i in range(1, 8):
        o = lax.rem(rep + i, 8)
        remote(pages_ref.at[o], pages_ref.at[o], s_g.at[i], r_g.at[o], (ctx, o)).wait_recv()
        remote(ids_ref.at[o], ids_ref.at[o], s_i.at[i], r_i.at[o], (ctx, o)).wait_recv()
        for half in range(2):
            for u in range(2):
                there = pool_ref.at[o, pl.ds(half * 8 + 4 * u, 4)]
                remote(there, there, s_p.at[0, 0, 0], r_p.at[o, half, u], (ctx, o)).wait_recv()


def pair_call(lengths, owners, gains, q, k, v, x, b, c, decay):
    def dma(*shape):
        return pltpu.SemaphoreType.DMA(shape)

    far = pl.BlockSpec(memory_space=pl.ANY)
    vmem = pl.BlockSpec(memory_space=pltpu.VMEM)
    return pl.pallas_call(
        pair_kernel,
        out_shape=(
            pltpu.VMEM((ROWS, 4096), BF16),
            pltpu.VMEM((ROWS, GR * GW), BF16),
            pltpu.VMEM((8, 16, MP, NS), BF16),
            pltpu.VMEM((8, CAP, 2, PAGE, 1024), BF16),
            pltpu.VMEM((8, 8, 128), jnp.int32),
        ),
        in_specs=[pl.BlockSpec(memory_space=pltpu.SMEM)] * 3 + [far] * 7,
        out_specs=(vmem, vmem, vmem, vmem, vmem),
        scratch_shapes=[
            pltpu.VMEM((ROWS, 1024), BF16),
            pltpu.VMEM((ROWS, 1024), BF16),
            pltpu.VMEM((ROWS, GR * GW), BF16),
            pltpu.VMEM((ROWS, 1024), BF16),
            pltpu.VMEM((ROWS, 1024), BF16),
            pltpu.VMEM((ROWS, 128), F32),
            pltpu.VMEM((GR, HG, ROWS), F32),
            pltpu.VMEM((GR, HG, ROWS), F32),
            pltpu.VMEM((GR, ROWS, HG), F32),
            pltpu.VMEM((GR, 8, ROWS, 4), F32),
            pltpu.VMEM((GR, HG, 128), F32),
            pltpu.VMEM((4, 2, HALF, ROWS), BF16),
            pltpu.VMEM((4, 2, HALF, ROWS), BF16),
            pltpu.VMEM((4, ROWS, NS), BF16),
            pltpu.VMEM((4, HG, 128), F32),
            pltpu.VMEM((3, 2, HALF, NS), F32),
            pltpu.VMEM((4, HG, 128), F32),
            pltpu.VMEM((2, HALF, NS), BF16),
            pltpu.VMEM((2, 4, 256, NS), BF16),
            pltpu.VMEM((4, 8, 128), F32),
            pltpu.VMEM((2, 4, 256, NS), BF16),
            pltpu.VMEM((2, 4, 256, NS), BF16),
            pltpu.VMEM((2, 4, HALF, NS), BF16),
            pltpu.VMEM((2, 4, HALF, NS), BF16),
            pltpu.VMEM((ROWS, GR * GW), F32),
            pltpu.VMEM((4, HG, MP, NS), BF16),
            pltpu.VMEM((4, ROWS, 1024), BF16),
            pltpu.VMEM((4, 4, ROWS, 512), BF16),
            pltpu.VMEM((4, ROWS, 1024), BF16),
            pltpu.VMEM((8, CAP, 2, PAGE, 1024), BF16),
            pltpu.VMEM((8, 8, 128), jnp.int32),
            dma(6), pltpu.SemaphoreType.DMA, pltpu.SemaphoreType.DMA,
            dma(2, 2), pltpu.SemaphoreType.DMA, pltpu.SemaphoreType.DMA,
            dma(4), dma(4), dma(4), dma(4), dma(4), dma(4), dma(4), dma(4), dma(2), dma(2),
            dma(4), dma(4),
            dma(8), dma(8), dma(8), dma(8),
            dma(2, 4), dma(2, 4), dma(4), dma(4), dma(4), dma(4),
            dma(2, 4), dma(2, 4), dma(4), dma(4), dma(2, 4), dma(2, 4),
            dma(2, 4, 4), dma(2, 4, 4), dma(2, 4, 4), dma(8, 2, 2),
        ],
        compiler_params=pltpu.CompilerParams(
            collective_id=0, has_side_effects=True, vmem_limit_bytes=50 << 20
        ),
        name="layer_pair",
    )(lengths, owners, gains, q, k, v, x, b, c, decay)


PARTS = (2, 4, 8, 4)


def place_kernel(a, b, c, d, ids, a_out, b_out, c_out, d_out, ids_out, sems):
    stores = []
    for src, dst, parts in zip((c, b, d, a), (c_out, b_out, d_out, a_out), PARTS[::-1]):
        size = src.shape[0] // parts
        for n in range(parts):
            at = pl.ds(n * size, size)
            stores.append(pltpu.make_async_copy(src.at[at], dst.at[at], sems.at[len(stores)]))
    for store in stores:
        store.start()
    turned = jnp.transpose(ids[:, 0, :].astype(F32))
    ids_out[...] = turned[:CAP].astype(jnp.int32)
    for store in stores:
        store.wait()


def place_call(*arrays):
    far = pl.BlockSpec(memory_space=pl.ANY)
    vmem = pl.BlockSpec(memory_space=pltpu.VMEM)
    shapes = [jax.ShapeDtypeStruct(x.shape, x.dtype) for x in arrays[:4]]
    return pl.pallas_call(
        place_kernel,
        out_shape=(*shapes, jax.ShapeDtypeStruct((CAP, 8), jnp.int32)),
        in_specs=[vmem] * 5,
        out_specs=(far, far, far, far, vmem),
        scratch_shapes=[pltpu.SemaphoreType.DMA((sum(PARTS),))],
        compiler_params=pltpu.CompilerParams(vmem_limit_bytes=40 << 20),
        name="place_outputs",
    )(*arrays)


def body(
    queries, cache_keys, cache_values, ssm_input, input_map, output_map, log_decay, skip_gain,
    lengths, page_owner,
):
    results = pair_call(
        lengths, page_owner.reshape(8), skip_gain, queries[0], cache_keys[0], cache_values[0],
        ssm_input[0], input_map[0], output_map[0], log_decay[0],
    )
    attention, rows, pool, pages, ids = place_call(*results)
    return (
        attention[None], rows[None], pool[None], pages[None, None], jnp.transpose(ids)[None, None]
    )


def solution(mesh):
    rows = P("rep", "ctx", None)
    return jax.shard_map(
        body,
        mesh=mesh,
        in_specs=(rows, rows, rows, rows, rows, rows, rows, P(), P("rep"), rows),
        out_specs=(
            rows,
            rows,
            P("ctx", None, "rep", None, None),
            P("ctx", "rep", None, None, None, None, None),
            P("ctx", "rep", None, None),
        ),
        check_vma=False,
    )
```

```python
import math

import jax
import jax.numpy as jnp
from jax import lax
from jax.experimental import pallas as pl
from jax.experimental.pallas import tpu as pltpu
from jax.sharding import PartitionSpec as P

HD = 128
GR = 4
PAGE = 16
CAP = 4
MP = 64
NS = 256
ROWS = 128
HG = 32
GW = HG * MP
HALF = GW // 2
MESH = pl.DeviceIdType.MESH
F32 = jnp.float32
BF16 = jnp.bfloat16
ORDER = (1, 3, 2)
UNITS = (0, 2, 2, 2, 2, 0, 0, 0)


def mod4(v):
    return lax.rem(v + 8, 4)


def chunk_rows(piece):
    return pl.ds(pl.multiple_of(piece * 256, 256), 256)


def widen(rows):
    heads = rows.shape[0]
    both = jnp.concatenate([rows, rows], axis=1)
    return jnp.broadcast_to(both[:, None, :], (heads, MP, NS)).reshape(heads * MP, NS)


def pair_kernel(
    lengths, owners, gains, q_ref, k_hbm, v_hbm, x_hbm, b_hbm, c_hbm, decay_hbm,
    attn_ref, out_ref, pool_ref, pages_ref, ids_ref,
    k_ref, v_ref, x_ref, b_ref, c_ref, decay_ref, ef, cumt, cumg, ecum, wg, ft, ft_in, b_in, w_in, part, wprod, t_out, t_in, w4_in,
    e0_out, e0_in, e_out, e_in, inner, snap, q_in, kv_in, a_out, page_buf, id_buf,
    l_in, l_q, l_a, l_p, l_g, l_i,
    s_k, r_k, s_v, r_v, s_q, r_q, s_kv, r_kv, s_kw, r_kw, s_a, r_a, s_g, r_g, s_i, r_i,
    s_ft, r_ft, s_b, r_b, s_w, r_w, s_t, r_t, s_w4, r_w4, s_e0, r_e0, s_e, r_e, s_p, r_p,
):
    ctx = lax.axis_index("ctx")
    rep = lax.axis_index("rep")
    mx = lax.rem(ctx, 4)
    my = ctx // 4
    mz = rep // 2
    first = ctx * ROWS
    length = lengths[0]

    def row_peer(j):
        return (my * 4 + j, rep)

    def col_peer(j):
        return (j * 4 + mx, rep)

    def remote(src, dst, send, recv, device):
        return pltpu.make_async_remote_copy(
            src_ref=src, dst_ref=dst, send_sem=send, recv_sem=recv, device_id=device,
            device_id_type=MESH,
        )

    barrier = pltpu.get_barrier_semaphore()
    for i in range(1, 4):
        pl.semaphore_signal(barrier, inc=1, device_id=row_peer(mod4(mx + i)), device_id_type=MESH)
        pl.semaphore_signal(barrier, inc=1, device_id=col_peer(mod4(my + i)), device_id_type=MESH)
    for i in range(1, 8):
        pl.semaphore_signal(
            barrier, inc=1, device_id=(ctx, lax.rem(rep + i, 8)), device_id_type=MESH
        )
    loads = [
        pltpu.make_async_copy(src, dst, l_in.at[n])
        for n, (src, dst) in enumerate((
            (decay_hbm, decay_ref), (x_hbm, x_ref), (b_hbm, b_ref), (k_hbm, k_ref),
            (v_hbm, v_ref), (c_hbm, c_ref),
        ))
    ]
    for load in loads:
        load.start()

    lane = lax.broadcasted_iota(jnp.int32, (ROWS, 128), 1)
    line = lax.broadcasted_iota(jnp.int32, (ROWS, 128), 0)
    causal = lane <= line
    low = lane < MP
    live = jnp.where(jnp.full((1, 128), first, jnp.int32) < length, 1.0, 0.0)

    loads[0].wait()
    cum = jnp.dot(
        jnp.where(causal, 1.0, 0.0), decay_ref[...] * live,
        precision=lax.Precision.HIGHEST, preferred_element_type=F32,
    )
    turned = jnp.transpose(cum)
    last = turned[:, 127:128]
    ef[...] = (jnp.exp(last - turned) * live).reshape(GR, HG, ROWS)
    cumt[...] = turned.reshape(GR, HG, ROWS)
    wg[...] = jnp.broadcast_to(jnp.exp(last), (128, 128)).reshape(GR, HG, 128)
    grown = jnp.exp(cum)
    for g in range(GR):
        cumg[g] = cum[:, g * HG : (g + 1) * HG]
        for p in range(8):
            ecum[g, p] = grown[:, g * HG + p * 4 : g * HG + p * 4 + 4]

    sent = []

    def go(copy):
        copy.start()
        sent.append(copy)

    def fade(j, u):
        def tile(t, carry):
            d = t // 2
            p = lax.rem(t, 2)
            lanes = pl.ds(pl.multiple_of(j * GW + d * 512 + u * 256 + p * 128, 128), 128)
            values = jnp.transpose(x_ref[:, lanes].astype(F32))
            factor = jnp.broadcast_to(
                ef[j, pl.ds(8 * d + 4 * u + 2 * p, 2), :][:, None, :], (2, MP, ROWS)
            ).reshape(128, ROWS)
            ft[j, u, pl.ds(pl.multiple_of(t * 128, 128), 128), :] = (values * factor).astype(BF16)
            return carry

        lax.fori_loop(0, 8, tile, 0, unroll=4)

    loads[1].wait()
    loads[2].wait()
    for i in ORDER:
        fade(mod4(mx + i), 0)
    pl.semaphore_wait(barrier, 13)
    for u in range(2):
        for i in ORDER:
            j = mod4(mx + i)
            if u == 0:
                lanes = pl.ds(pl.multiple_of(j * NS, NS), NS)
                go(remote(b_ref.at[:, lanes], b_in.at[mx], s_b.at[i], r_b.at[mx], row_peer(j)))
                go(remote(wg.at[j], w_in.at[mx], s_w.at[i], r_w.at[mx], row_peer(j)))
            if u == 1:
                fade(j, u)
            go(remote(ft.at[j, u], ft_in.at[mx, u], s_ft.at[u, i], r_ft.at[u, mx], row_peer(j)))
        if u == 0:
            loads[3].wait()
            loads[4].wait()
            for i in ORDER:
                j = mod4(my + i)
                lanes = pl.ds(pl.multiple_of(j * 256, 256), 256)
                go(remote(k_ref.at[:, lanes], kv_in.at[my, mx, :, pl.ds(0, 256)], s_k.at[i], r_k.at[my],
                          col_peer(j)))
                go(remote(v_ref.at[:, lanes], kv_in.at[my, mx, :, pl.ds(256, 256)], s_v.at[i], r_v.at[my],
                          col_peer(j)))
            own = pl.ds(pl.multiple_of(my * 256, 256), 256)
            kv_in[my, mx, :, 0:256] = k_ref[:, own]
            kv_in[my, mx, :, 256:512] = v_ref[:, own]
            local_q = pltpu.make_async_copy(
                q_ref.at[:, pl.ds(pl.multiple_of(my * 1024, 1024), 1024)], q_in.at[my], l_q
            )
            local_q.start()
        fade(mx, u)
        ft_in[mx, u] = ft[mx, u]
    b_in[mx] = b_ref[:, pl.ds(pl.multiple_of(mx * NS, NS), NS)]
    w_in[mx] = wg[mx]

    places = []
    for p in range(8):
        slot = jnp.int32(0)
        for r in range(p):
            slot = slot + jnp.where(owners[r] == owners[p], 1, 0)
        places.append(jnp.where(first < length, owners[p] * CAP + slot, -1))

    def fill_pages(o, carry):
        labels = []
        picks = []
        for e in range(CAP):
            page = jnp.int32(-1000)
            for p in range(8):
                page = jnp.where(places[p] == o * CAP + e, p, page)
            labels.append(jnp.where(page >= 0, page + ctx * 8, -1))
            picks.append(jnp.where(lane[:PAGE] - line[:PAGE] == page * PAGE, 1.0, 0.0))
        pick = jnp.concatenate(picks, axis=0).astype(BF16)
        for z, rows in enumerate((k_ref, v_ref)):
            taken = jnp.dot(pick, rows[...], preferred_element_type=F32).astype(BF16)
            page_buf[o, :, z] = taken.reshape(CAP, PAGE, 1024)
        spot = lax.broadcasted_iota(jnp.int32, (8, 128), 1)
        id_buf[o] = jnp.where(
            spot == 0, labels[0],
            jnp.where(spot == 1, labels[1], jnp.where(spot == 2, labels[2], labels[3])),
        )
        return carry

    lax.fori_loop(0, 8, fill_pages, 0)
    for i in range(1, 8):
        o = lax.rem(rep + i, 8)
        go(remote(page_buf.at[o], pages_ref.at[rep], s_g.at[i], r_g.at[rep], (ctx, o)))
        go(remote(id_buf.at[o], ids_ref.at[rep], s_i.at[i], r_i.at[rep], (ctx, o)))
    local_pages = pltpu.make_async_copy(page_buf.at[rep], pages_ref.at[rep], l_g)
    local_pages.start()
    local_ids = pltpu.make_async_copy(id_buf.at[rep], ids_ref.at[rep], l_i)
    local_ids.start()

    loads[5].wait()

    def inner_group(g, carry):
        lanes = pl.ds(pl.multiple_of(g * NS, NS), NS)
        products = lax.dot_general(
            c_ref[:, lanes], b_ref[:, lanes], (((1,), (1,)), ((), ())),
            preferred_element_type=F32,
        )
        products = jnp.where(causal, products * live, 0.0)
        for p in range(HG // 2):
            at = pl.ds(pl.multiple_of(g * GW + p * 128, 128), 128)
            values = x_ref[:, at]
            halves = []
            for k in range(2):
                h = 2 * p + k
                column = cumg[g, :, h : h + 1]
                row = cumt[g, h : h + 1, :]
                mix = (products * jnp.exp(jnp.minimum(column - row, 0.0))).astype(BF16)
                halves.append(jnp.dot(mix, values, preferred_element_type=F32))
            gain = jnp.where(low[0:1], gains[g * HG + 2 * p], gains[g * HG + 2 * p + 1]) * live
            inner[:, at] = jnp.where(low, halves[0], halves[1]) + gain * values.astype(F32)
        return carry

    lax.fori_loop(0, GR, inner_group, 0)

    for i in ORDER:
        j = mod4(mx + i)
        remote(b_in.at[j], b_in.at[j], s_b.at[i], r_b.at[j], row_peer(j)).wait_recv()
        remote(w_in.at[j], w_in.at[j], s_w.at[i], r_w.at[j], row_peer(j)).wait_recv()

    running = w_in[0]
    for k in range(1, 4):
        wprod[k - 1] = running
        running = running * w_in[k]
    wprod[3] = running

    def scan_piece(u, piece):
        at = chunk_rows(piece)
        heads = pl.ds(piece * 8 + u * 4, 4)
        state = jnp.dot(ft_in[0, u, at, :], b_in[0], preferred_element_type=F32)
        for k in range(1, 4):
            part[k - 1, u, at, :] = state
            state = state * widen(w_in[k, heads, :]) + jnp.dot(
                ft_in[k, u, at, :], b_in[k], preferred_element_type=F32
            )
        t_out[u, at, :] = state.astype(BF16)

    def take_inputs(u):
        for i in ORDER:
            j = mod4(mx + i)
            remote(
                ft_in.at[j, u], ft_in.at[j, u], s_ft.at[u, i], r_ft.at[u, j], row_peer(j)
            ).wait_recv()
        for i in ORDER:
            j = mod4(my + i)
            scan_piece(u, j)
            if u == 0:
                heads = pl.ds(pl.multiple_of(j * 8, 8), 8)
                go(remote(wprod.at[3, heads, :], w4_in.at[my], s_w4.at[i], r_w4.at[my],
                          col_peer(j)))
            go(remote(t_out.at[u, chunk_rows(j), :], t_in.at[u, my], s_t.at[u, i], r_t.at[u, my],
                      col_peer(j)))
        scan_piece(u, my)
        t_in[u, my] = t_out[u, chunk_rows(my), :]
        if u == 0:
            w4_in[my] = wprod[3, pl.ds(pl.multiple_of(my * 8, 8), 8), :]

    def start_kv():
        for i in ORDER:
            j = mod4(my + i)
            for z, (send, recv) in enumerate(((s_k, r_k), (s_v, r_v))):
                there = kv_in.at[j, mx, :, pl.ds(256 * z, 256)]
                remote(there, there, send.at[i], recv.at[j], col_peer(j)).wait_recv()
        for i in (1, 3):
            j = mod4(mx + i)
            go(remote(kv_in.at[:, mx], kv_in.at[:, mx], s_kv.at[i], r_kv.at[mx], row_peer(j)))

    def relay_kv():
        for n, i in enumerate((1, 3)):
            j = mod4(mx - i)
            remote(kv_in.at[:, j], kv_in.at[:, j], s_kv.at[i], r_kv.at[j], row_peer(j)).wait_recv()
            there = kv_in.at[pl.ds(2 * n, 2), j]
            go(remote(there, there, s_kw.at[n], r_kw.at[n], row_peer(mod4(mx + i))))

    def send_queries():
        for i in ORDER:
            j = mod4(my + i)
            lanes = pl.ds(pl.multiple_of(j * 1024, 1024), 1024)
            go(remote(q_ref.at[:, lanes], q_in.at[my], s_q.at[i], r_q.at[my], col_peer(j)))

    def chain_rows(u):
        for i in ORDER:
            j = mod4(my + i)
            remote(t_in.at[u, j], t_in.at[u, j], s_t.at[u, i], r_t.at[u, j], col_peer(j)).wait_recv()
            if u == 0:
                remote(w4_in.at[j], w4_in.at[j], s_w4.at[i], r_w4.at[j], col_peer(j)).wait_recv()
        state = jnp.zeros((256, NS), F32)
        for k in range(4):
            e0_out[u, k] = state.astype(BF16)
            if k < 3:
                state = state * widen(w4_in[k, 4 * u : 4 * u + 4, :]) + t_in[u, k].astype(F32)
        for i in ORDER:
            j = mod4(my + i)
            go(remote(e0_out.at[u, j], e0_in.at[u, my], s_e0.at[u, i], r_e0.at[u, my], col_peer(j)))
        e0_in[u, my] = e0_out[u, my]

    def enter(u, d):
        piece = mod4(my + d)
        if d != 0:
            remote(
                e0_in.at[u, piece], e0_in.at[u, piece], s_e0.at[u, d], r_e0.at[u, piece],
                col_peer(piece),
            ).wait_recv()
        at = chunk_rows(piece)
        heads = pl.ds(piece * 8 + u * 4, 4)
        e_out[u, 0, at, :] = e0_in[u, piece]
        for k in range(1, 4):
            e_out[u, k, at, :] = (
                e0_in[u, piece].astype(F32) * widen(wprod[k - 1, heads, :])
                + part[k - 1, u, at, :]
            ).astype(BF16)
        for i in ORDER:
            j = mod4(mx + i)
            go(remote(e_out.at[u, j, at, :], e_in.at[u, mx, at, :], s_e.at[u, d, i],
                      r_e.at[u, mx, d], row_peer(j)))
        e_in[u, mx, at, :] = e_out[u, mx, at, :]

    def snap_copies(u, d, j):
        piece = mod4(my + d)
        owner = 2 * j + piece // 2
        half = lax.rem(piece, 2)
        source = snap.at[j, pl.ds(piece * 8 + 4 * u, 4)]
        target = pool_ref.at[rep, pl.ds(half * 8 + 4 * u, 4)]
        return (
            owner,
            remote(source, target, s_p.at[u, d, j], r_p.at[rep, half, u], (ctx, owner)),
            pltpu.make_async_copy(source, target, l_p.at[half, u]),
        )

    def finish(u, d, j):
        piece = mod4(my + d)
        at = chunk_rows(piece)
        lanes = pl.ds(pl.multiple_of(j * NS, NS), NS)
        entering = e_in[u, j, at, :]
        mine = jnp.dot(ft[j, u, at, :], b_ref[:, lanes], preferred_element_type=F32)
        factor = widen(wg[j, pl.ds(piece * 8 + u * 4, 4), :])
        leaving = (mine + factor * entering.astype(F32)).astype(BF16)
        snap[j, pl.ds(piece * 8 + u * 4, 4)] = leaving.reshape(4, MP, NS)
        owner, away, here = snap_copies(u, d, j)
        pl.when(owner != rep)(away.start)
        pl.when(owner == rep)(here.start)

    def project(u, d, j):
        piece = mod4(my + d)
        lanes = pl.ds(pl.multiple_of(j * NS, NS), NS)
        carried = lax.dot_general(
            c_ref[:, lanes], e_in[u, j, chunk_rows(piece), :], (((1,), (1,)), ((), ())), preferred_element_type=F32
        )
        for p in range(2):
            scales = [
                jnp.broadcast_to(
                    ecum[j, piece * 2 + u, :, 2 * p + k : 2 * p + k + 1], (ROWS, 128)
                )
                for k in range(2)
            ]
            wide = pl.ds(pl.multiple_of(j * GW + piece * 512 + u * 256 + p * 128, 128), 128)
            out_ref[:, wide] = (
                inner[:, wide]
                + jnp.where(low, scales[0], scales[1]) * carried[:, p * 128 : p * 128 + 128]
            ).astype(BF16)

    take_inputs(0)
    start_kv()
    chain_rows(0)
    send_queries()
    take_inputs(1)
    relay_kv()
    steps = [(u, d) for u in range(2) for d in (0, 1, 3, 2)]
    for step in steps[:3]:
        enter(*step)
        finish(*step, mx)
    chain_rows(1)


    def wait_attention():
        for n in range(2):
            there = kv_in.at[pl.ds(2 * n, 2), mod4(mx + 2)]
            remote(there, there, s_kw.at[n], r_kw.at[n], row_peer(mod4(mx + 1))).wait_recv()
        local_q.wait()
        for i in ORDER:
            j = mod4(my + i)
            remote(q_in.at[j], q_in.at[j], s_q.at[i], r_q.at[j], col_peer(j)).wait_recv()

    scale = math.log2(math.e) / math.sqrt(HD)
    key_off = lax.broadcasted_iota(jnp.int32, (1, 512), 1)
    spread = lax.broadcasted_iota(jnp.int32, (ROWS, 512), 1) - lax.broadcasted_iota(
        jnp.int32, (ROWS, 512), 0
    )

    def attend(i, h):
        def two_heads(a, carry):
            wide = [
                pl.ds(pl.multiple_of((4 * h + 2 * a + r) * HD, HD), HD) for r in range(2)
            ]
            query = jnp.concatenate([q_in[i, :, wide[0]], q_in[i, :, wide[1]]], axis=0)
            scores = []
            for t in range(i + 1):
                keys = kv_in[t, :, :, h * HD : (h + 1) * HD].reshape(512, HD)
                raw = lax.dot_general(
                    query, keys, (((1,), (1,)), ((), ())), preferred_element_type=F32
                )
                if t > 0:
                    raw = raw + jnp.where(key_off + t * 512 < length, 0.0, -1e30)
                if t == i:
                    bias = jnp.where(spread <= mx * ROWS, 0.0, -1e30)
                    raw = raw + jnp.concatenate([bias, bias], axis=0)
                scores.append(raw)
            top = scores[0]
            for raw in scores[1:]:
                top = jnp.maximum(top, raw)
            top = jnp.max(top, axis=1, keepdims=True)
            total = None
            acc = None
            for t in range(i + 1):
                weights = jnp.exp2((scores[t] - top) * scale)
                values = kv_in[t, :, :, 256 + h * HD : 256 + (h + 1) * HD].reshape(512, HD)
                more = jnp.sum(weights, axis=1, keepdims=True)
                term = jnp.dot(weights.astype(BF16), values, preferred_element_type=F32)
                total = more if total is None else total + more
                acc = term if acc is None else acc + term
            result = (acc / total).astype(BF16)
            for r in range(2):
                a_out[i, :, wide[r]] = result[r * ROWS : (r + 1) * ROWS]
            return carry

        lax.fori_loop(0, 2, two_heads, 0)

    def a_copies(i):
        target = attn_ref.at[:, pl.ds(pl.multiple_of(my * 1024, 1024), 1024)]
        return (
            remote(a_out.at[i], target, s_a.at[i], r_a.at[my], col_peer(i)),
            pltpu.make_async_copy(a_out.at[i], target, l_a),
        )

    units = [(3, 0), (3, 1), (2, 0), (2, 1), (1, 0), (1, 1), (0, 0), (0, 1)]
    for k, (u, d) in enumerate(steps):
        at = chunk_rows(mod4(my + d))
        for i in ORDER:
            j = mod4(mx + i)
            remote(
                e_in.at[u, j, at, :], e_in.at[u, j, at, :], s_e.at[u, d, i], r_e.at[u, j, d],
                row_peer(j),
            ).wait_recv()
        if k + 3 < 8:
            enter(*steps[k + 3])

        def finish_other(n, carry):
            j = mod4(mx + mz + n)
            pl.when(j != mx)(lambda: finish(u, d, j))
            return carry

        lax.fori_loop(0, 4, finish_other, 0)

        def project_all(j, carry):
            project(u, d, j)
            return carry

        lax.fori_loop(0, 4, project_all, 0)
        if k + 3 < 8:
            finish(*steps[k + 3], mx)
        if k == 1:
            wait_attention()
        for _ in range(UNITS[k]):
            i, h = units.pop(0)
            attend(i, h)
            if h == 1:
                away, here = a_copies(i)
                pl.when(i != my)(away.start)
                pl.when(i == my)(here.start)

    for c in sent:
        c.wait_send()
    for i in range(4):
        away, here = a_copies(i)
        pl.when(i != my)(away.wait_send)
        pl.when(i == my)(here.wait)
    for u in range(2):
        for d in range(4):

            def drain(j, carry):
                owner, away, here = snap_copies(u, d, j)
                pl.when(owner != rep)(away.wait_send)
                pl.when(owner == rep)(here.wait)
                return carry

            lax.fori_loop(0, 4, drain, 0)
    local_pages.wait()
    local_ids.wait()
    for i in ORDER:
        j = mod4(my + i)
        there = attn_ref.at[:, pl.ds(pl.multiple_of(j * 1024, 1024), 1024)]
        remote(there, there, s_a.at[i], r_a.at[j], col_peer(j)).wait_recv()
    for i in range(1, 8):
        o = lax.rem(rep + i, 8)
        remote(pages_ref.at[o], pages_ref.at[o], s_g.at[i], r_g.at[o], (ctx, o)).wait_recv()
        remote(ids_ref.at[o], ids_ref.at[o], s_i.at[i], r_i.at[o], (ctx, o)).wait_recv()
        for half in range(2):
            for u in range(2):
                there = pool_ref.at[o, pl.ds(half * 8 + 4 * u, 4)]
                remote(there, there, s_p.at[0, 0, 0], r_p.at[o, half, u], (ctx, o)).wait_recv()


def pair_call(lengths, owners, gains, q, k, v, x, b, c, decay):
    def dma(*shape):
        return pltpu.SemaphoreType.DMA(shape)

    far = pl.BlockSpec(memory_space=pl.ANY)
    vmem = pl.BlockSpec(memory_space=pltpu.VMEM)
    return pl.pallas_call(
        pair_kernel,
        out_shape=(
            pltpu.VMEM((ROWS, 4096), BF16),
            pltpu.VMEM((ROWS, GR * GW), BF16),
            pltpu.VMEM((8, 16, MP, NS), BF16),
            pltpu.VMEM((8, CAP, 2, PAGE, 1024), BF16),
            pltpu.VMEM((8, 8, 128), jnp.int32),
        ),
        in_specs=[pl.BlockSpec(memory_space=pltpu.SMEM)] * 3 + [far] * 7,
        out_specs=(vmem, vmem, vmem, vmem, vmem),
        scratch_shapes=[
            pltpu.VMEM((ROWS, 1024), BF16),
            pltpu.VMEM((ROWS, 1024), BF16),
            pltpu.VMEM((ROWS, GR * GW), BF16),
            pltpu.VMEM((ROWS, 1024), BF16),
            pltpu.VMEM((ROWS, 1024), BF16),
            pltpu.VMEM((ROWS, 128), F32),
            pltpu.VMEM((GR, HG, ROWS), F32),
            pltpu.VMEM((GR, HG, ROWS), F32),
            pltpu.VMEM((GR, ROWS, HG), F32),
            pltpu.VMEM((GR, 8, ROWS, 4), F32),
            pltpu.VMEM((GR, HG, 128), F32),
            pltpu.VMEM((4, 2, HALF, ROWS), BF16),
            pltpu.VMEM((4, 2, HALF, ROWS), BF16),
            pltpu.VMEM((4, ROWS, NS), BF16),
            pltpu.VMEM((4, HG, 128), F32),
            pltpu.VMEM((3, 2, HALF, NS), F32),
            pltpu.VMEM((4, HG, 128), F32),
            pltpu.VMEM((2, HALF, NS), BF16),
            pltpu.VMEM((2, 4, 256, NS), BF16),
            pltpu.VMEM((4, 8, 128), F32),
            pltpu.VMEM((2, 4, 256, NS), BF16),
            pltpu.VMEM((2, 4, 256, NS), BF16),
            pltpu.VMEM((2, 4, HALF, NS), BF16),
            pltpu.VMEM((2, 4, HALF, NS), BF16),
            pltpu.VMEM((ROWS, GR * GW), F32),
            pltpu.VMEM((4, HG, MP, NS), BF16),
            pltpu.VMEM((4, ROWS, 1024), BF16),
            pltpu.VMEM((4, 4, ROWS, 512), BF16),
            pltpu.VMEM((4, ROWS, 1024), BF16),
            pltpu.VMEM((8, CAP, 2, PAGE, 1024), BF16),
            pltpu.VMEM((8, 8, 128), jnp.int32),
            dma(6), pltpu.SemaphoreType.DMA, pltpu.SemaphoreType.DMA,
            dma(2, 2), pltpu.SemaphoreType.DMA, pltpu.SemaphoreType.DMA,
            dma(4), dma(4), dma(4), dma(4), dma(4), dma(4), dma(4), dma(4), dma(2), dma(2),
            dma(4), dma(4),
            dma(8), dma(8), dma(8), dma(8),
            dma(2, 4), dma(2, 4), dma(4), dma(4), dma(4), dma(4),
            dma(2, 4), dma(2, 4), dma(4), dma(4), dma(2, 4), dma(2, 4),
            dma(2, 4, 4), dma(2, 4, 4), dma(2, 4, 4), dma(8, 2, 2),
        ],
        compiler_params=pltpu.CompilerParams(
            collective_id=0, has_side_effects=True, vmem_limit_bytes=50 << 20
        ),
        name="layer_pair",
    )(lengths, owners, gains, q, k, v, x, b, c, decay)


PARTS = (2, 4, 8, 4)


def place_kernel(a, b, c, d, ids, a_out, b_out, c_out, d_out, ids_out, sems):
    stores = []
    for src, dst, parts in zip((c, b, d, a), (c_out, b_out, d_out, a_out), PARTS[::-1]):
        size = src.shape[0] // parts
        for n in range(parts):
            at = pl.ds(n * size, size)
            stores.append(pltpu.make_async_copy(src.at[at], dst.at[at], sems.at[len(stores)]))
    for store in stores:
        store.start()
    turned = jnp.transpose(ids[:, 0, :].astype(F32))
    ids_out[...] = turned[:CAP].astype(jnp.int32)
    for store in stores:
        store.wait()


def place_call(*arrays):
    far = pl.BlockSpec(memory_space=pl.ANY)
    vmem = pl.BlockSpec(memory_space=pltpu.VMEM)
    shapes = [jax.ShapeDtypeStruct(x.shape, x.dtype) for x in arrays[:4]]
    return pl.pallas_call(
        place_kernel,
        out_shape=(*shapes, jax.ShapeDtypeStruct((CAP, 8), jnp.int32)),
        in_specs=[vmem] * 5,
        out_specs=(far, far, far, far, vmem),
        scratch_shapes=[pltpu.SemaphoreType.DMA((sum(PARTS),))],
        compiler_params=pltpu.CompilerParams(vmem_limit_bytes=40 << 20),
        name="place_outputs",
    )(*arrays)


def body(
    queries, cache_keys, cache_values, ssm_input, input_map, output_map, log_decay, skip_gain,
    lengths, page_owner,
):
    results = pair_call(
        lengths, page_owner.reshape(8), skip_gain, queries[0], cache_keys[0], cache_values[0],
        ssm_input[0], input_map[0], output_map[0], log_decay[0],
    )
    attention, rows, pool, pages, ids = place_call(*results)
    return (
        attention[None], rows[None], pool[None], pages[None, None], jnp.transpose(ids)[None, None]
    )


def solution(mesh):
    rows = P("rep", "ctx", None)
    return jax.shard_map(
        body,
        mesh=mesh,
        in_specs=(rows, rows, rows, rows, rows, rows, rows, P(), P("rep"), rows),
        out_specs=(
            rows,
            rows,
            P("ctx", None, "rep", None, None),
            P("ctx", "rep", None, None, None, None, None),
            P("ctx", "rep", None, None),
        ),
        check_vma=False,
    )
```

```python
import math

import jax
import jax.numpy as jnp
from jax import lax
from jax.experimental import pallas as pl
from jax.experimental.pallas import tpu as pltpu
from jax.sharding import PartitionSpec as P

HD = 128
GR = 4
PAGE = 16
CAP = 4
MP = 64
NS = 256
ROWS = 128
HG = 32
GW = HG * MP
HALF = GW // 2
MESH = pl.DeviceIdType.MESH
F32 = jnp.float32
BF16 = jnp.bfloat16
ORDER = (1, 3, 2)
UNITS = (0, 2, 2, 2, 2, 0, 0, 0)


def mod4(v):
    return lax.rem(v + 8, 4)


def chunk_rows(piece):
    return pl.ds(pl.multiple_of(piece * 256, 256), 256)


def widen(rows):
    heads = rows.shape[0]
    both = jnp.concatenate([rows, rows], axis=1)
    return jnp.broadcast_to(both[:, None, :], (heads, MP, NS)).reshape(heads * MP, NS)


def pair_kernel(
    lengths, owners, gains, q_ref, k_hbm, v_hbm, x_hbm, b_hbm, c_hbm, decay_hbm,
    attn_ref, out_ref, pool_ref, pages_ref, ids_ref,
    k_ref, v_ref, x_ref, b_ref, c_ref, decay_ref, ef, cumt, cumg, ecum, wg, ft, ft_in, b_in, w_in, part, wprod, t_out, t_in, w4_in,
    e0_out, e0_in, e_out, e_in, inner, snap, q_in, kv_in, a_out, page_buf, id_buf,
    l_in, l_q, l_a, l_p, l_g, l_i,
    s_k, r_k, s_v, r_v, s_q, r_q, s_kv, r_kv, s_kw, r_kw, s_a, r_a, s_g, r_g, s_i, r_i,
    s_ft, r_ft, s_b, r_b, s_w, r_w, s_t, r_t, s_w4, r_w4, s_e0, r_e0, s_e, r_e, s_p, r_p,
):
    ctx = lax.axis_index("ctx")
    rep = lax.axis_index("rep")
    mx = lax.rem(ctx, 4)
    my = ctx // 4
    mz = rep // 2
    first = ctx * ROWS
    length = lengths[0]

    def row_peer(j):
        return (my * 4 + j, rep)

    def col_peer(j):
        return (j * 4 + mx, rep)

    def remote(src, dst, send, recv, device):
        return pltpu.make_async_remote_copy(
            src_ref=src, dst_ref=dst, send_sem=send, recv_sem=recv, device_id=device,
            device_id_type=MESH,
        )

    barrier = pltpu.get_barrier_semaphore()
    for i in range(1, 4):
        pl.semaphore_signal(barrier, inc=1, device_id=row_peer(mod4(mx + i)), device_id_type=MESH)
        pl.semaphore_signal(barrier, inc=1, device_id=col_peer(mod4(my + i)), device_id_type=MESH)
    for i in range(1, 8):
        pl.semaphore_signal(
            barrier, inc=1, device_id=(ctx, lax.rem(rep + i, 8)), device_id_type=MESH
        )
    loads = [
        pltpu.make_async_copy(src, dst, l_in.at[n])
        for n, (src, dst) in enumerate((
            (decay_hbm, decay_ref), (x_hbm, x_ref), (b_hbm, b_ref), (k_hbm, k_ref),
            (v_hbm, v_ref), (c_hbm, c_ref),
        ))
    ]
    for load in loads:
        load.start()

    lane = lax.broadcasted_iota(jnp.int32, (ROWS, 128), 1)
    line = lax.broadcasted_iota(jnp.int32, (ROWS, 128), 0)
    causal = lane <= line
    low = lane < MP
    live = jnp.where(jnp.full((1, 128), first, jnp.int32) < length, 1.0, 0.0)

    loads[0].wait()
    cum = jnp.dot(
        jnp.where(causal, 1.0, 0.0), decay_ref[...] * live,
        precision=lax.Precision.HIGHEST, preferred_element_type=F32,
    )
    turned = jnp.transpose(cum)
    last = turned[:, 127:128]
    ef[...] = (jnp.exp(last - turned) * live).reshape(GR, HG, ROWS)
    cumt[...] = turned.reshape(GR, HG, ROWS)
    wg[...] = jnp.broadcast_to(jnp.exp(last), (128, 128)).reshape(GR, HG, 128)
    grown = jnp.exp(cum)
    for g in range(GR):
        cumg[g] = cum[:, g * HG : (g + 1) * HG]
        for p in range(8):
            ecum[g, p] = grown[:, g * HG + p * 4 : g * HG + p * 4 + 4]

    sent = []

    def go(copy):
        copy.start()
        sent.append(copy)

    def fade(j, u):
        def tile(t, carry):
            d = t // 2
            p = lax.rem(t, 2)
            lanes = pl.ds(pl.multiple_of(j * GW + d * 512 + u * 256 + p * 128, 128), 128)
            values = jnp.transpose(x_ref[:, lanes].astype(F32))
            factor = jnp.broadcast_to(
                ef[j, pl.ds(8 * d + 4 * u + 2 * p, 2), :][:, None, :], (2, MP, ROWS)
            ).reshape(128, ROWS)
            ft[j, u, pl.ds(pl.multiple_of(t * 128, 128), 128), :] = (values * factor).astype(BF16)
            return carry

        lax.fori_loop(0, 8, tile, 0, unroll=4)

    loads[1].wait()
    loads[2].wait()
    for i in ORDER:
        fade(mod4(mx + i), 0)
    pl.semaphore_wait(barrier, 13)
    for u in range(2):
        for i in ORDER:
            j = mod4(mx + i)
            if u == 0:
                lanes = pl.ds(pl.multiple_of(j * NS, NS), NS)
                go(remote(b_ref.at[:, lanes], b_in.at[mx], s_b.at[i], r_b.at[mx], row_peer(j)))
                go(remote(wg.at[j], w_in.at[mx], s_w.at[i], r_w.at[mx], row_peer(j)))
            if u == 1:
                fade(j, u)
            go(remote(ft.at[j, u], ft_in.at[mx, u], s_ft.at[u, i], r_ft.at[u, mx], row_peer(j)))
        if u == 0:
            loads[3].wait()
            loads[4].wait()
            for i in ORDER:
                j = mod4(my + i)
                lanes = pl.ds(pl.multiple_of(j * 256, 256), 256)
                go(remote(k_ref.at[:, lanes], kv_in.at[my, mx, :, pl.ds(0, 256)], s_k.at[i], r_k.at[my],
                          col_peer(j)))
                go(remote(v_ref.at[:, lanes], kv_in.at[my, mx, :, pl.ds(256, 256)], s_v.at[i], r_v.at[my],
                          col_peer(j)))
            own = pl.ds(pl.multiple_of(my * 256, 256), 256)
            kv_in[my, mx, :, 0:256] = k_ref[:, own]
            kv_in[my, mx, :, 256:512] = v_ref[:, own]
            local_q = pltpu.make_async_copy(
                q_ref.at[:, pl.ds(pl.multiple_of(my * 1024, 1024), 1024)], q_in.at[my], l_q
            )
            local_q.start()
        fade(mx, u)
        ft_in[mx, u] = ft[mx, u]
    b_in[mx] = b_ref[:, pl.ds(pl.multiple_of(mx * NS, NS), NS)]
    w_in[mx] = wg[mx]

    places = []
    for p in range(8):
        slot = jnp.int32(0)
        for r in range(p):
            slot = slot + jnp.where(owners[r] == owners[p], 1, 0)
        places.append(jnp.where(first < length, owners[p] * CAP + slot, -1))

    def fill_pages(o, carry):
        labels = []
        picks = []
        for e in range(CAP):
            page = jnp.int32(-1000)
            for p in range(8):
                page = jnp.where(places[p] == o * CAP + e, p, page)
            labels.append(jnp.where(page >= 0, page + ctx * 8, -1))
            picks.append(jnp.where(lane[:PAGE] - line[:PAGE] == page * PAGE, 1.0, 0.0))
        pick = jnp.concatenate(picks, axis=0).astype(BF16)
        for z, rows in enumerate((k_ref, v_ref)):
            taken = jnp.dot(pick, rows[...], preferred_element_type=F32).astype(BF16)
            page_buf[o, :, z] = taken.reshape(CAP, PAGE, 1024)
        spot = lax.broadcasted_iota(jnp.int32, (8, 128), 1)
        id_buf[o] = jnp.where(
            spot == 0, labels[0],
            jnp.where(spot == 1, labels[1], jnp.where(spot == 2, labels[2], labels[3])),
        )
        return carry

    lax.fori_loop(0, 8, fill_pages, 0)
    for i in range(1, 8):
        o = lax.rem(rep + i, 8)
        go(remote(page_buf.at[o], pages_ref.at[rep], s_g.at[i], r_g.at[rep], (ctx, o)))
        go(remote(id_buf.at[o], ids_ref.at[rep], s_i.at[i], r_i.at[rep], (ctx, o)))
    local_pages = pltpu.make_async_copy(page_buf.at[rep], pages_ref.at[rep], l_g)
    local_pages.start()
    local_ids = pltpu.make_async_copy(id_buf.at[rep], ids_ref.at[rep], l_i)
    local_ids.start()

    loads[5].wait()

    def inner_group(g, carry):
        lanes = pl.ds(pl.multiple_of(g * NS, NS), NS)
        products = lax.dot_general(
            c_ref[:, lanes], b_ref[:, lanes], (((1,), (1,)), ((), ())),
            preferred_element_type=F32,
        )
        products = jnp.where(causal, products * live, 0.0)
        for p in range(HG // 2):
            at = pl.ds(pl.multiple_of(g * GW + p * 128, 128), 128)
            values = x_ref[:, at]
            halves = []
            for k in range(2):
                h = 2 * p + k
                column = cumg[g, :, h : h + 1]
                row = cumt[g, h : h + 1, :]
                mix = (products * jnp.exp(jnp.minimum(column - row, 0.0))).astype(BF16)
                halves.append(jnp.dot(mix, values, preferred_element_type=F32))
            gain = jnp.where(low[0:1], gains[g * HG + 2 * p], gains[g * HG + 2 * p + 1]) * live
            inner[:, at] = jnp.where(low, halves[0], halves[1]) + gain * values.astype(F32)
        return carry

    lax.fori_loop(0, GR, inner_group, 0)

    for i in ORDER:
        j = mod4(mx + i)
        remote(b_in.at[j], b_in.at[j], s_b.at[i], r_b.at[j], row_peer(j)).wait_recv()
        remote(w_in.at[j], w_in.at[j], s_w.at[i], r_w.at[j], row_peer(j)).wait_recv()

    running = w_in[0]
    for k in range(1, 4):
        wprod[k - 1] = running
        running = running * w_in[k]
    wprod[3] = running

    def scan_piece(u, piece):
        at = chunk_rows(piece)
        heads = pl.ds(piece * 8 + u * 4, 4)
        state = jnp.dot(ft_in[0, u, at, :], b_in[0], preferred_element_type=F32)
        for k in range(1, 4):
            part[k - 1, u, at, :] = state
            state = state * widen(w_in[k, heads, :]) + jnp.dot(
                ft_in[k, u, at, :], b_in[k], preferred_element_type=F32
            )
        t_out[u, at, :] = state.astype(BF16)

    def take_inputs(u):
        for i in ORDER:
            j = mod4(mx + i)
            remote(
                ft_in.at[j, u], ft_in.at[j, u], s_ft.at[u, i], r_ft.at[u, j], row_peer(j)
            ).wait_recv()
        for i in ORDER:
            j = mod4(my + i)
            scan_piece(u, j)
            if u == 0:
                heads = pl.ds(pl.multiple_of(j * 8, 8), 8)
                go(remote(wprod.at[3, heads, :], w4_in.at[my], s_w4.at[i], r_w4.at[my],
                          col_peer(j)))
            go(remote(t_out.at[u, chunk_rows(j), :], t_in.at[u, my], s_t.at[u, i], r_t.at[u, my],
                      col_peer(j)))
        scan_piece(u, my)
        t_in[u, my] = t_out[u, chunk_rows(my), :]
        if u == 0:
            w4_in[my] = wprod[3, pl.ds(pl.multiple_of(my * 8, 8), 8), :]

    def start_kv():
        for i in ORDER:
            j = mod4(my + i)
            for z, (send, recv) in enumerate(((s_k, r_k), (s_v, r_v))):
                there = kv_in.at[j, mx, :, pl.ds(256 * z, 256)]
                remote(there, there, send.at[i], recv.at[j], col_peer(j)).wait_recv()
        for i in (1, 3):
            j = mod4(mx + i)
            go(remote(kv_in.at[:, mx], kv_in.at[:, mx], s_kv.at[i], r_kv.at[mx], row_peer(j)))

    def relay_kv():
        for n, i in enumerate((1, 3)):
            j = mod4(mx - i)
            remote(kv_in.at[:, j], kv_in.at[:, j], s_kv.at[i], r_kv.at[j], row_peer(j)).wait_recv()
            there = kv_in.at[pl.ds(2 * n, 2), j]
            go(remote(there, there, s_kw.at[n], r_kw.at[n], row_peer(mod4(mx + i))))

    def send_queries():
        for i in ORDER:
            j = mod4(my + i)
            lanes = pl.ds(pl.multiple_of(j * 1024, 1024), 1024)
            go(remote(q_ref.at[:, lanes], q_in.at[my], s_q.at[i], r_q.at[my], col_peer(j)))

    def chain_rows(u):
        for i in ORDER:
            j = mod4(my + i)
            remote(t_in.at[u, j], t_in.at[u, j], s_t.at[u, i], r_t.at[u, j], col_peer(j)).wait_recv()
            if u == 0:
                remote(w4_in.at[j], w4_in.at[j], s_w4.at[i], r_w4.at[j], col_peer(j)).wait_recv()
        state = jnp.zeros((256, NS), F32)
        for k in range(4):
            e0_out[u, k] = state.astype(BF16)
            if k < 3:
                state = state * widen(w4_in[k, 4 * u : 4 * u + 4, :]) + t_in[u, k].astype(F32)
        for i in ORDER:
            j = mod4(my + i)
            go(remote(e0_out.at[u, j], e0_in.at[u, my], s_e0.at[u, i], r_e0.at[u, my], col_peer(j)))
        e0_in[u, my] = e0_out[u, my]

    def enter(u, d):
        piece = mod4(my + d)
        if d != 0:
            remote(
                e0_in.at[u, piece], e0_in.at[u, piece], s_e0.at[u, d], r_e0.at[u, piece],
                col_peer(piece),
            ).wait_recv()
        at = chunk_rows(piece)
        heads = pl.ds(piece * 8 + u * 4, 4)
        e_out[u, 0, at, :] = e0_in[u, piece]
        for k in range(1, 4):
            e_out[u, k, at, :] = (
                e0_in[u, piece].astype(F32) * widen(wprod[k - 1, heads, :])
                + part[k - 1, u, at, :]
            ).astype(BF16)
        for i in ORDER:
            j = mod4(mx + i)
            go(remote(e_out.at[u, j, at, :], e_in.at[u, mx, at, :], s_e.at[u, d, i],
                      r_e.at[u, mx, d], row_peer(j)))
        e_in[u, mx, at, :] = e_out[u, mx, at, :]

    def snap_copies(u, d, j):
        piece = mod4(my + d)
        owner = 2 * j + piece // 2
        half = lax.rem(piece, 2)
        source = snap.at[j, pl.ds(piece * 8 + 4 * u, 4)]
        target = pool_ref.at[rep, pl.ds(half * 8 + 4 * u, 4)]
        return (
            owner,
            remote(source, target, s_p.at[u, d, j], r_p.at[rep, half, u], (ctx, owner)),
            pltpu.make_async_copy(source, target, l_p.at[half, u]),
        )

    def finish(u, d, j):
        piece = mod4(my + d)
        at = chunk_rows(piece)
        lanes = pl.ds(pl.multiple_of(j * NS, NS), NS)
        entering = e_in[u, j, at, :]
        mine = jnp.dot(ft[j, u, at, :], b_ref[:, lanes], preferred_element_type=F32)
        factor = widen(wg[j, pl.ds(piece * 8 + u * 4, 4), :])
        leaving = (mine + factor * entering.astype(F32)).astype(BF16)
        snap[j, pl.ds(piece * 8 + u * 4, 4)] = leaving.reshape(4, MP, NS)
        owner, away, here = snap_copies(u, d, j)
        pl.when(owner != rep)(away.start)
        pl.when(owner == rep)(here.start)

    def project(u, d, j):
        piece = mod4(my + d)
        lanes = pl.ds(pl.multiple_of(j * NS, NS), NS)
        carried = lax.dot_general(
            c_ref[:, lanes], e_in[u, j, chunk_rows(piece), :], (((1,), (1,)), ((), ())), preferred_element_type=F32
        )
        for p in range(2):
            scales = [
                jnp.broadcast_to(
                    ecum[j, piece * 2 + u, :, 2 * p + k : 2 * p + k + 1], (ROWS, 128)
                )
                for k in range(2)
            ]
            wide = pl.ds(pl.multiple_of(j * GW + piece * 512 + u * 256 + p * 128, 128), 128)
            out_ref[:, wide] = (
                inner[:, wide]
                + jnp.where(low, scales[0], scales[1]) * carried[:, p * 128 : p * 128 + 128]
            ).astype(BF16)

    take_inputs(0)
    start_kv()
    chain_rows(0)
    take_inputs(1)
    send_queries()
    relay_kv()
    steps = [(u, d) for u in range(2) for d in (0, 1, 3, 2)]
    for step in steps[:3]:
        enter(*step)
        finish(*step, mx)
    chain_rows(1)


    def wait_attention():
        for n in range(2):
            there = kv_in.at[pl.ds(2 * n, 2), mod4(mx + 2)]
            remote(there, there, s_kw.at[n], r_kw.at[n], row_peer(mod4(mx + 1))).wait_recv()
        local_q.wait()
        for i in ORDER:
            j = mod4(my + i)
            remote(q_in.at[j], q_in.at[j], s_q.at[i], r_q.at[j], col_peer(j)).wait_recv()

    scale = math.log2(math.e) / math.sqrt(HD)
    key_off = lax.broadcasted_iota(jnp.int32, (1, 512), 1)
    spread = lax.broadcasted_iota(jnp.int32, (ROWS, 512), 1) - lax.broadcasted_iota(
        jnp.int32, (ROWS, 512), 0
    )

    def attend(i, h):
        def two_heads(a, carry):
            wide = [
                pl.ds(pl.multiple_of((4 * h + 2 * a + r) * HD, HD), HD) for r in range(2)
            ]
            query = jnp.concatenate([q_in[i, :, wide[0]], q_in[i, :, wide[1]]], axis=0)
            scores = []
            for t in range(i + 1):
                keys = kv_in[t, :, :, h * HD : (h + 1) * HD].reshape(512, HD)
                raw = lax.dot_general(
                    query, keys, (((1,), (1,)), ((), ())), preferred_element_type=F32
                )
                if t > 0:
                    raw = raw + jnp.where(key_off + t * 512 < length, 0.0, -1e30)
                if t == i:
                    bias = jnp.where(spread <= mx * ROWS, 0.0, -1e30)
                    raw = raw + jnp.concatenate([bias, bias], axis=0)
                scores.append(raw)
            top = scores[0]
            for raw in scores[1:]:
                top = jnp.maximum(top, raw)
            top = jnp.max(top, axis=1, keepdims=True)
            total = None
            acc = None
            for t in range(i + 1):
                weights = jnp.exp2((scores[t] - top) * scale)
                values = kv_in[t, :, :, 256 + h * HD : 256 + (h + 1) * HD].reshape(512, HD)
                more = jnp.sum(weights, axis=1, keepdims=True)
                term = jnp.dot(weights.astype(BF16), values, preferred_element_type=F32)
                total = more if total is None else total + more
                acc = term if acc is None else acc + term
            result = (acc / total).astype(BF16)
            for r in range(2):
                a_out[i, :, wide[r]] = result[r * ROWS : (r + 1) * ROWS]
            return carry

        lax.fori_loop(0, 2, two_heads, 0)

    def a_copies(i):
        target = attn_ref.at[:, pl.ds(pl.multiple_of(my * 1024, 1024), 1024)]
        return (
            remote(a_out.at[i], target, s_a.at[i], r_a.at[my], col_peer(i)),
            pltpu.make_async_copy(a_out.at[i], target, l_a),
        )

    units = [(3, 0), (3, 1), (2, 0), (2, 1), (1, 0), (1, 1), (0, 0), (0, 1)]
    for k, (u, d) in enumerate(steps):
        at = chunk_rows(mod4(my + d))
        for i in ORDER:
            j = mod4(mx + i)
            remote(
                e_in.at[u, j, at, :], e_in.at[u, j, at, :], s_e.at[u, d, i], r_e.at[u, j, d],
                row_peer(j),
            ).wait_recv()
        if k + 3 < 8:
            enter(*steps[k + 3])

        def finish_other(n, carry):
            j = mod4(mx + mz + n)
            pl.when(j != mx)(lambda: finish(u, d, j))
            return carry

        lax.fori_loop(0, 4, finish_other, 0)

        def project_all(j, carry):
            project(u, d, j)
            return carry

        lax.fori_loop(0, 4, project_all, 0)
        if k + 3 < 8:
            finish(*steps[k + 3], mx)
        if k == 1:
            wait_attention()
        for _ in range(UNITS[k]):
            i, h = units.pop(0)
            attend(i, h)
            if h == 1:
                away, here = a_copies(i)
                pl.when(i != my)(away.start)
                pl.when(i == my)(here.start)

    for c in sent:
        c.wait_send()
    for i in range(4):
        away, here = a_copies(i)
        pl.when(i != my)(away.wait_send)
        pl.when(i == my)(here.wait)
    for u in range(2):
        for d in range(4):

            def drain(j, carry):
                owner, away, here = snap_copies(u, d, j)
                pl.when(owner != rep)(away.wait_send)
                pl.when(owner == rep)(here.wait)
                return carry

            lax.fori_loop(0, 4, drain, 0)
    local_pages.wait()
    local_ids.wait()
    for i in ORDER:
        j = mod4(my + i)
        there = attn_ref.at[:, pl.ds(pl.multiple_of(j * 1024, 1024), 1024)]
        remote(there, there, s_a.at[i], r_a.at[j], col_peer(j)).wait_recv()
    for i in range(1, 8):
        o = lax.rem(rep + i, 8)
        remote(pages_ref.at[o], pages_ref.at[o], s_g.at[i], r_g.at[o], (ctx, o)).wait_recv()
        remote(ids_ref.at[o], ids_ref.at[o], s_i.at[i], r_i.at[o], (ctx, o)).wait_recv()
        for half in range(2):
            for u in range(2):
                there = pool_ref.at[o, pl.ds(half * 8 + 4 * u, 4)]
                remote(there, there, s_p.at[0, 0, 0], r_p.at[o, half, u], (ctx, o)).wait_recv()


def pair_call(lengths, owners, gains, q, k, v, x, b, c, decay):
    def dma(*shape):
        return pltpu.SemaphoreType.DMA(shape)

    far = pl.BlockSpec(memory_space=pl.ANY)
    vmem = pl.BlockSpec(memory_space=pltpu.VMEM)
    return pl.pallas_call(
        pair_kernel,
        out_shape=(
            pltpu.VMEM((ROWS, 4096), BF16),
            pltpu.VMEM((ROWS, GR * GW), BF16),
            pltpu.VMEM((8, 16, MP, NS), BF16),
            pltpu.VMEM((8, CAP, 2, PAGE, 1024), BF16),
            pltpu.VMEM((8, 8, 128), jnp.int32),
        ),
        in_specs=[pl.BlockSpec(memory_space=pltpu.SMEM)] * 3 + [far] * 7,
        out_specs=(vmem, vmem, vmem, vmem, vmem),
        scratch_shapes=[
            pltpu.VMEM((ROWS, 1024), BF16),
            pltpu.VMEM((ROWS, 1024), BF16),
            pltpu.VMEM((ROWS, GR * GW), BF16),
            pltpu.VMEM((ROWS, 1024), BF16),
            pltpu.VMEM((ROWS, 1024), BF16),
            pltpu.VMEM((ROWS, 128), F32),
            pltpu.VMEM((GR, HG, ROWS), F32),
            pltpu.VMEM((GR, HG, ROWS), F32),
            pltpu.VMEM((GR, ROWS, HG), F32),
            pltpu.VMEM((GR, 8, ROWS, 4), F32),
            pltpu.VMEM((GR, HG, 128), F32),
            pltpu.VMEM((4, 2, HALF, ROWS), BF16),
            pltpu.VMEM((4, 2, HALF, ROWS), BF16),
            pltpu.VMEM((4, ROWS, NS), BF16),
            pltpu.VMEM((4, HG, 128), F32),
            pltpu.VMEM((3, 2, HALF, NS), F32),
            pltpu.VMEM((4, HG, 128), F32),
            pltpu.VMEM((2, HALF, NS), BF16),
            pltpu.VMEM((2, 4, 256, NS), BF16),
            pltpu.VMEM((4, 8, 128), F32),
            pltpu.VMEM((2, 4, 256, NS), BF16),
            pltpu.VMEM((2, 4, 256, NS), BF16),
            pltpu.VMEM((2, 4, HALF, NS), BF16),
            pltpu.VMEM((2, 4, HALF, NS), BF16),
            pltpu.VMEM((ROWS, GR * GW), F32),
            pltpu.VMEM((4, HG, MP, NS), BF16),
            pltpu.VMEM((4, ROWS, 1024), BF16),
            pltpu.VMEM((4, 4, ROWS, 512), BF16),
            pltpu.VMEM((4, ROWS, 1024), BF16),
            pltpu.VMEM((8, CAP, 2, PAGE, 1024), BF16),
            pltpu.VMEM((8, 8, 128), jnp.int32),
            dma(6), pltpu.SemaphoreType.DMA, pltpu.SemaphoreType.DMA,
            dma(2, 2), pltpu.SemaphoreType.DMA, pltpu.SemaphoreType.DMA,
            dma(4), dma(4), dma(4), dma(4), dma(4), dma(4), dma(4), dma(4), dma(2), dma(2),
            dma(4), dma(4),
            dma(8), dma(8), dma(8), dma(8),
            dma(2, 4), dma(2, 4), dma(4), dma(4), dma(4), dma(4),
            dma(2, 4), dma(2, 4), dma(4), dma(4), dma(2, 4), dma(2, 4),
            dma(2, 4, 4), dma(2, 4, 4), dma(2, 4, 4), dma(8, 2, 2),
        ],
        compiler_params=pltpu.CompilerParams(
            collective_id=0, has_side_effects=True, vmem_limit_bytes=50 << 20
        ),
        name="layer_pair",
    )(lengths, owners, gains, q, k, v, x, b, c, decay)


PARTS = (2, 4, 8, 4)


def place_kernel(a, b, c, d, ids, a_out, b_out, c_out, d_out, ids_out, sems):
    stores = []
    for src, dst, parts in zip((c, b, d, a), (c_out, b_out, d_out, a_out), PARTS[::-1]):
        size = src.shape[0] // parts
        for n in range(parts):
            at = pl.ds(n * size, size)
            stores.append(pltpu.make_async_copy(src.at[at], dst.at[at], sems.at[len(stores)]))
    for store in stores:
        store.start()
    turned = jnp.transpose(ids[:, 0, :].astype(F32))
    ids_out[...] = turned[:CAP].astype(jnp.int32)
    for store in stores:
        store.wait()


def place_call(*arrays):
    far = pl.BlockSpec(memory_space=pl.ANY)
    vmem = pl.BlockSpec(memory_space=pltpu.VMEM)
    shapes = [jax.ShapeDtypeStruct(x.shape, x.dtype) for x in arrays[:4]]
    return pl.pallas_call(
        place_kernel,
        out_shape=(*shapes, jax.ShapeDtypeStruct((CAP, 8), jnp.int32)),
        in_specs=[vmem] * 5,
        out_specs=(far, far, far, far, vmem),
        scratch_shapes=[pltpu.SemaphoreType.DMA((sum(PARTS),))],
        compiler_params=pltpu.CompilerParams(vmem_limit_bytes=40 << 20),
        name="place_outputs",
    )(*arrays)


def body(
    queries, cache_keys, cache_values, ssm_input, input_map, output_map, log_decay, skip_gain,
    lengths, page_owner,
):
    results = pair_call(
        lengths, page_owner.reshape(8), skip_gain, queries[0], cache_keys[0], cache_values[0],
        ssm_input[0], input_map[0], output_map[0], log_decay[0],
    )
    attention, rows, pool, pages, ids = place_call(*results)
    return (
        attention[None], rows[None], pool[None], pages[None, None], jnp.transpose(ids)[None, None]
    )


def solution(mesh):
    rows = P("rep", "ctx", None)
    return jax.shard_map(
        body,
        mesh=mesh,
        in_specs=(rows, rows, rows, rows, rows, rows, rows, P(), P("rep"), rows),
        out_specs=(
            rows,
            rows,
            P("ctx", None, "rep", None, None),
            P("ctx", "rep", None, None, None, None, None),
            P("ctx", "rep", None, None),
        ),
        check_vma=False,
    )
```
